32 devices in a mesh: ctx: 8 (over z, x), tp: 4 (over y, core).
Axes of the slice: x: 2, y: 2, z: 4, core: 2. Of those that a mesh axis runs over, the one named last changes fastest.
Arguments:
- inputs: bfloat16 [4, 8, 2, 64, 1024], P(None, 'ctx', None, 'tp'), may hold values from -6 to 6
- pairing: int32 [4, 8], replicated, may hold values from 0 to 7, each once within a row
- first_gain: bfloat16 [1024], P('ctx'), may hold values from 0.5 to 1.5
- first_shift: bfloat16 [1024], P('ctx'), may hold values from -1 to 1
- query_key_value_weight: bfloat16 [1024, 3, 1024], P('ctx', None, 'tp'), may hold values from -0.1875 to 0.1875
- mix_bias: bfloat16 [2, 4, 256], P(None, 'tp', 'ctx'), may hold values from -1.5 to 1.5
- output_projection_weight: bfloat16 [1024, 1024], P('tp', 'ctx'), may hold values from -0.875 to 0.875
- out_bias: bfloat16 [1024], P('ctx'), may hold values from -1 to 1
- second_gain: bfloat16 [1024], P('ctx'), may hold values from 0.5 to 1.5
- second_shift: bfloat16 [1024], P('ctx'), may hold values from -1 to 1
- up_projection_weight: bfloat16 [1024, 4096], P('ctx', 'tp'), may hold values from -0.1875 to 0.1875
- up_projection_bias: bfloat16 [4, 1024], P('tp', 'ctx'), may hold values from -1.5 to 1.5
- down_projection_weight: bfloat16 [4096, 1024], P('tp', 'ctx'), may hold values from -0.09375 to 0.09375
- down_bias: bfloat16 [1024], P('ctx'), may hold values from -1 to 1
- cotangent: bfloat16 [4, 8, 2, 64, 1024], P(None, 'ctx', None, 'tp'), may hold values from -6 to 6
Outputs:
- result: bfloat16 [4, 8, 2, 64, 1024], P(None, 'ctx', None, 'tp')
- grad_inputs: float32 [4, 8, 2, 64, 1024], P(None, 'ctx', None, 'tp')
- grad_first_gain: float32 [1024], P('ctx')
- grad_first_shift: float32 [1024], P('ctx')
- grad_mix_weight: float32 [1024, 3, 1024], P('ctx', None, 'tp')
- grad_mix_bias: float32 [2, 4, 256], P(None, 'tp', 'ctx')
- grad_out_weight: float32 [1024, 1024], P('tp', 'ctx')
- grad_out_bias: float32 [1024], P('ctx')
- grad_second_gain: float32 [1024], P('ctx')
- grad_second_shift: float32 [1024], P('ctx')
- grad_up_weight: float32 [1024, 4096], P('ctx', 'tp')
- grad_up_bias: float32 [4, 1024], P('tp', 'ctx')
- grad_down_weight: float32 [4096, 1024], P('tp', 'ctx')
- grad_down_bias: float32 [1024], P('ctx')
The draws below stay inside these ranges and needn't reach their ends.
Inputs may be any that keep to these rules, and one draw needn't show every extreme that they name: Each row of pairing is a permutation: every pair of blocks of a sequence is held by exactly one slot.
All inputs are finite; a program needn't handle non-finite values.
Results may differ from the reference program's by a relative error of at most 0.018.
Values may be sent and summed in bfloat16 or wider, within the bound.
No kernel may reach another device: no remote copies, remote signals or barrier semaphores. Data moves between devices by JAX's collectives and lax.ppermute only.
A program may use at most 320 MiB of HBM per device.

```python
from functools import partial
import jax
import jax.numpy as jnp
from jax import lax

D = 1024
H = 16
HD = 64
FEEDFORWARD_SIZE = 4096
SEQS = 4
BLK = 64
LEN = 1024
N_CTX = 8
N_TP = 4


def shard_levels(stream_key, dims, shards, smallest, high):
    factor_of, own = 1.0, jax.random.fold_in(stream_key, 6)
    for dim, shards_of in shards:
        steps = jnp.exp(jax.random.uniform(jax.random.fold_in(own, dim), (shards_of,), jnp.float32, smallest / len(shards), high / len(shards)))
        factor_of = factor_of * jnp.repeat(steps, dims[dim] // shards_of).reshape([-1 if axis == dim else 1 for axis in range(len(dims))])
    return factor_of


def centred(stream_key, dims, width, reach, pieces=(), kind=jnp.bfloat16):
    array = jax.random.normal(stream_key, dims, jnp.float32) * width
    if len(pieces) > 0:
        array = shard_levels(stream_key, dims, pieces, -0.22, 0.18) * array
    return jnp.clip(array, min=-reach, max=reach).astype(kind)


def setup_inputs(seed: int = 0) -> dict:
    key_list = jax.random.split(jax.random.key(seed), 16)
    inputs = centred(key_list[0], (SEQS, N_CTX, 2, BLK, D), 1.0, 6.0, ((1, 8), (3, 4)))
    pairing = jax.vmap(lambda own: jax.random.permutation(own, N_CTX))(jax.random.split(key_list[1], SEQS)).reshape((SEQS, N_CTX)).astype(jnp.int32)
    first_gain = jnp.clip(1.0 + 0.1 * jax.random.normal(key_list[2], (D,), jnp.float32), 0.5, 1.5).astype(jnp.bfloat16)
    first_shift = centred(key_list[3], (D,), 0.2, 1.0, ((0, 8),))
    query_key_value_weight = centred(key_list[4], (D, 3, D), D ** -0.5, 0.1875, ((0, 8), (2, 4)))
    mix_bias = centred(key_list[5], (2, N_TP, D // N_TP), 0.3, 1.5, ((1, 4), (2, 8)))
    output_projection_weight = centred(key_list[6], (D, D), (D / (LEN / 2) ** 0.5) ** -0.5, 0.875, ((0, 4), (1, 8)))
    out_bias = centred(key_list[7], (D,), 0.2, 1.0, ((0, 8),))
    second_gain = jnp.clip(1.0 + 0.1 * jax.random.normal(key_list[8], (D,), jnp.float32), 0.5, 1.5).astype(jnp.bfloat16)
    second_shift = centred(key_list[9], (D,), 0.2, 1.0, ((0, 8),))
    up_projection_weight = centred(key_list[10], (D, FEEDFORWARD_SIZE), D ** -0.5, 0.1875, ((0, 8), (1, 4)))
    up_projection_bias = centred(key_list[11], (N_TP, FEEDFORWARD_SIZE // N_TP), 0.3, 1.5, ((0, 4), (1, 8)))
    down_projection_weight = centred(key_list[12], (FEEDFORWARD_SIZE, D), FEEDFORWARD_SIZE ** -0.5, 0.09375, ((0, 4), (1, 8)))
    down_bias = centred(key_list[13], (D,), 0.2, 1.0, ((0, 8),))
    cotangent = centred(key_list[14], (SEQS, N_CTX, 2, BLK, D), 1.0, 6.0, ((1, 8), (3, 4)))
    return dict(inputs=inputs, pairing=pairing, first_gain=first_gain, first_shift=first_shift, query_key_value_weight=query_key_value_weight, mix_bias=mix_bias, output_projection_weight=output_projection_weight, out_bias=out_bias, second_gain=second_gain, second_shift=second_shift, up_projection_weight=up_projection_weight, up_projection_bias=up_projection_bias, down_projection_weight=down_projection_weight, down_bias=down_bias, cotangent=cotangent)


epsilon = 1e-05
highest_precision = lax.Precision.HIGHEST

@jax.custom_vjp
def low(v):
    return lax.optimization_barrier(v.astype(jnp.bfloat16)).astype(jnp.float32)

@jax.custom_vjp
def lower_backward(v):
    return v

def low_keep(v):
    return (low(v), None)

def low_pass(kept, grad):
    return (grad,)

def back_keep(v):
    return (v, None)

def back_low(kept, grad):
    return (low(grad),)
low.defvjp(low_keep, low_pass)
lower_backward.defvjp(back_keep, back_low)

def normalize(token_rows, scaling, offset):
    row_mean = lax.optimization_barrier(jnp.mean(token_rows, axis=-1, keepdims=True))
    centered = token_rows - row_mean
    variance = lax.optimization_barrier(jnp.mean(centered * centered, axis=-1, keepdims=True))
    return centered * lax.rsqrt(variance + epsilon) * scaling + offset

def attend(queries, key_vectors, value_vectors, key_place):
    scores = jnp.einsum('qhd,khd->hqk', queries, key_vectors, precision=highest_precision) * HD ** (-0.5)
    scores = lower_backward(scores)
    allowed = key_place[None, :, None] >= key_place[None, None, :]
    scores = jnp.where(allowed, scores, -jnp.inf)
    row_max = lax.optimization_barrier(jnp.max(scores, axis=-1, keepdims=True))
    exponent = jnp.exp(scores - row_max)
    probabilities = low(exponent / lax.optimization_barrier(jnp.sum(exponent, axis=-1, keepdims=True)))
    return jnp.einsum('hqk,khd->qhd', probabilities, value_vectors, precision=highest_precision)

def block_layer(pairing, inputs, first_gain, first_shift, query_key_value_weight, mix_bias, output_projection_weight, out_bias, second_gain, second_shift, up_projection_weight, up_projection_bias, down_projection_weight, down_bias):
    token_rows = inputs.reshape(SEQS, LEN, D)
    starts = jnp.stack([pairing, 2 * N_CTX - 1 - pairing], axis=-1) * BLK
    places = (starts[:, :, :, None] + jnp.arange(BLK, dtype=jnp.int32)).reshape(SEQS, LEN).astype(jnp.int32)
    first_norm_output = low(normalize(token_rows, first_gain, first_shift))
    projected_output = jnp.einsum('bzv,vxy->bzxy', first_norm_output, query_key_value_weight, precision=highest_precision)
    bias_rows = mix_bias.reshape(2, D)
    projected_output = projected_output + jnp.stack([bias_rows[0], jnp.zeros((D,), jnp.float32), bias_rows[1]])
    projected_output = lower_backward(low(projected_output))
    split_heads = projected_output.reshape(SEQS, LEN, 3, H, HD)

    def per_sequence(operands):
        sequence_block, key_place = operands
        return attend(sequence_block[:, 0], sequence_block[:, 1], sequence_block[:, 2], key_place)
    attention_result = lax.map(jax.checkpoint(per_sequence), (split_heads, places))
    attention_result = lower_backward(low(attention_result.reshape(SEQS, LEN, D)))
    residual_branch = lower_backward(jnp.einsum('mnp,pa->mna', attention_result, output_projection_weight, precision=highest_precision))
    hidden = token_rows + residual_branch + out_bias
    second_norm_output = low(normalize(hidden, second_gain, second_shift))
    before_activation = jnp.einsum('nvx,xp->nvp', second_norm_output, up_projection_weight, precision=highest_precision) + up_projection_bias.reshape(FEEDFORWARD_SIZE)
    before_activation = lower_backward(before_activation)
    activation_rows = low(jax.nn.gelu(before_activation, approximate=True))
    residual_branch_two = lower_backward(jnp.einsum('hax,xp->hap', activation_rows, down_projection_weight, precision=highest_precision))
    return (hidden + residual_branch_two + down_bias).reshape(SEQS, N_CTX, 2, BLK, D)

def reference(inputs, pairing, first_gain, first_shift, query_key_value_weight, mix_bias, output_projection_weight, out_bias, second_gain, second_shift, up_projection_weight, up_projection_bias, down_projection_weight, down_bias, cotangent):
    params = [arg.astype(jnp.float32) for arg in (inputs, first_gain, first_shift, query_key_value_weight, mix_bias, output_projection_weight, out_bias, second_gain, second_shift, up_projection_weight, up_projection_bias, down_projection_weight, down_bias)]
    forward = partial(block_layer, pairing)
    output, pullback = jax.vjp(forward, *params)
    gradients = pullback(cotangent.astype(jnp.float32))
    return (output.astype(jnp.bfloat16), gradients[0], gradients[1], gradients[2], gradients[3], gradients[4], gradients[5], gradients[6], gradients[7], gradients[8], gradients[9], gradients[10], gradients[11], gradients[12])
```

```python
import jax
import jax.numpy as jnp
from jax import lax
from jax.experimental import pallas as pl
from jax.experimental.pallas import tpu as pltpu
from jax.sharding import PartitionSpec as P

HD = 64


epsilon = 1e-05


def normalize(token_rows, scaling, offset):
    row_mean = jnp.mean(token_rows, axis=-1, keepdims=True)
    centered = token_rows - row_mean
    variance = jnp.mean(centered * centered, axis=-1, keepdims=True)
    return centered * lax.rsqrt(variance + epsilon) * scaling + offset


def gelu_tanh(values_in):
    return jax.nn.gelu(values_in, approximate=True)


def block_places(pairing_rows, block_rows):
    slot_count = pairing_rows.shape[-1]
    starts = jnp.stack([pairing_rows, 2 * slot_count - 1 - pairing_rows], axis=-1) * block_rows
    within = jnp.arange(block_rows, dtype=jnp.int32)
    return (starts[:, :, :, None] + within).reshape(pairing_rows.shape[0], -1)


def by_head(tensor, head_count):
    seq_span, row_span, model_width = tensor.shape
    return jnp.moveaxis(
        tensor.reshape(seq_span, row_span, head_count, model_width // head_count), 2, 0
    )


def from_head(tensor):
    head_count, seq_span, row_span, head_size = tensor.shape
    return jnp.moveaxis(tensor, 0, 2).reshape(seq_span, row_span, head_count * head_size)


def head_scores(queries, key_vectors, allowed, score_scale):
    scores = (
        jnp.einsum("gqd,gkd->gqk", queries, key_vectors, preferred_element_type=jnp.float32)
        * score_scale
    )
    return jnp.where(allowed, scores, -jnp.inf)


def recompute(queries, key_vectors, value_vectors, grad_out, log_total, allowed, score_scale):
    scores = head_scores(queries, key_vectors, allowed, score_scale)
    probabilities = jnp.exp(scores - log_total[:, :, None])
    grad_probs = jnp.einsum(
        "gqd,gkd->gqk", grad_out, value_vectors, preferred_element_type=jnp.float32
    )
    return (probabilities, grad_probs)


def spread_rows(normed):
    return lax.all_gather(normed, "tp", axis=2, tiled=True)


def collect_rows(partial_terms):
    return lax.psum_scatter(
        partial_terms.astype(jnp.bfloat16), "tp", scatter_dimension=2, tiled=True
    ).astype(jnp.float32)


def spread_grads(gradient_part):
    return lax.all_gather(gradient_part, "tp", axis=2, tiled=True)


def collect_grads(partial_terms):
    return lax.psum_scatter(
        partial_terms.astype(jnp.bfloat16), "tp", scatter_dimension=2, tiled=True
    ).astype(jnp.float32)


def fetch_keys(key_part, value_part):
    return (
        lax.all_gather(key_part, "ctx", axis=1, tiled=True),
        lax.all_gather(value_part, "ctx", axis=1, tiled=True),
    )


def general_body(
    inputs,
    pairing,
    first_gain,
    first_shift,
    query_key_value_weight,
    mix_bias,
    output_projection_weight,
    out_bias,
    second_gain,
    second_shift,
    up_projection_weight,
    up_projection_bias,
    down_projection_weight,
    down_bias,
    cotangent,
):
    seq_count = inputs.shape[0]
    part_rows = inputs.shape[3]
    model_width = inputs.shape[4]
    tp_count = lax.axis_size("tp")
    block_rows = part_rows * tp_count
    local_rows = 2 * block_rows
    ctx_index = lax.axis_index("ctx")
    score_scale = HD ** (-0.5)
    batch_seqs = seq_count
    for candidate in range(seq_count, 0, -1):
        if seq_count % candidate == 0 and candidate * local_rows >= 512:
            batch_seqs = candidate
    groups = seq_count // batch_seqs
    vector_stack = jnp.stack(
        [first_gain, first_shift, out_bias, second_gain, second_shift, down_bias]
    )
    fetched = (
        lax.all_gather(vector_stack, "ctx", axis=1, tiled=True),
        lax.all_gather(query_key_value_weight, "ctx", axis=0, tiled=True),
        lax.all_gather(mix_bias, "ctx", axis=2, tiled=True),
        lax.all_gather(output_projection_weight, "ctx", axis=1, tiled=True),
        lax.all_gather(up_projection_weight, "ctx", axis=0, tiled=True),
        lax.all_gather(up_projection_bias, "ctx", axis=1, tiled=True),
        lax.all_gather(down_projection_weight, "ctx", axis=1, tiled=True),
    )
    vectors_full = fetched[0].astype(jnp.float32)
    dim_local = fetched[2].shape[2]
    head_count = dim_local // HD
    token_rows = inputs.reshape(seq_count, 2, part_rows, model_width).astype(jnp.float32)
    first_norm_output = normalize(token_rows, vectors_full[0], vectors_full[1]).astype(jnp.bfloat16)
    first_all = spread_rows(first_norm_output)
    projected_output = jnp.einsum(
        "sabd,dkc->sabkc", first_all, fetched[1], preferred_element_type=jnp.float32
    )
    bias_full = fetched[2].astype(jnp.float32)
    bias_rows = jnp.stack([bias_full[0, 0], jnp.zeros((dim_local,), jnp.float32), bias_full[1, 0]])
    projected_output = (projected_output + bias_rows).astype(jnp.bfloat16)

    def grouped(tensor):
        return tensor.reshape(groups, batch_seqs, local_rows, tensor.shape[-1])

    def ungrouped(tensor):
        return tensor.reshape(seq_count, 2, block_rows, dim_local)

    query_groups = grouped(projected_output[:, :, :, 0])
    key_groups = grouped(projected_output[:, :, :, 1])
    value_groups = grouped(projected_output[:, :, :, 2])
    pairing_groups = pairing.reshape(groups, batch_seqs, pairing.shape[1])

    def forward_group(unused_carry, inputs_group):
        query_part, key_part, value_part, pairing_rows = inputs_group
        key_all, value_all = fetch_keys(key_part, value_part)
        places = block_places(pairing_rows, block_rows)
        own_places = lax.dynamic_slice_in_dim(places, ctx_index * local_rows, local_rows, 1)
        allowed = own_places[:, :, None] >= places[:, None, :]

        def head_forward(operands):
            queries, key_vectors, value_vectors = operands
            scores = head_scores(queries, key_vectors, allowed, score_scale)
            row_max = jnp.max(scores, axis=-1, keepdims=True)
            exponent = jnp.exp(scores - row_max)
            row_total = jnp.sum(exponent, axis=-1, keepdims=True)
            weights_low = (exponent / row_total).astype(jnp.bfloat16)
            attention_result = jnp.einsum(
                "gqk,gkd->gqd", weights_low, value_vectors, preferred_element_type=jnp.float32
            )
            return (attention_result.astype(jnp.bfloat16), (row_max + jnp.log(row_total))[:, :, 0])

        outputs, log_totals = lax.map(
            head_forward,
            (
                by_head(query_part, head_count),
                by_head(key_all, head_count),
                by_head(value_all, head_count),
            ),
        )
        return (unused_carry, (from_head(outputs), log_totals))

    unused_state, (output_groups, log_groups) = lax.scan(
        forward_group, None, (query_groups, key_groups, value_groups, pairing_groups)
    )
    attention_result = ungrouped(output_groups)
    residual_branch = collect_rows(
        jnp.einsum(
            "sabc,cd->sabd", attention_result, fetched[3], preferred_element_type=jnp.float32
        )
    )
    hidden = token_rows + residual_branch + vectors_full[2]
    second_norm_output = normalize(hidden, vectors_full[3], vectors_full[4]).astype(jnp.bfloat16)
    second_all = spread_rows(second_norm_output)
    before_activation = jnp.einsum(
        "sabd,df->sabf", second_all, fetched[4], preferred_element_type=jnp.float32
    ) + fetched[5][0].astype(jnp.float32)
    activation_rows = gelu_tanh(before_activation).astype(jnp.bfloat16)
    residual_branch_two = collect_rows(
        jnp.einsum("sabf,fd->sabd", activation_rows, fetched[6], preferred_element_type=jnp.float32)
    )
    result = (hidden + residual_branch_two + vectors_full[5]).astype(jnp.bfloat16)
    vectors_back = fetched[0].astype(jnp.float32)
    grad_result_low = cotangent.reshape(seq_count, 2, part_rows, model_width)
    grad_result = grad_result_low.astype(jnp.float32)
    grad_down_bias = jnp.sum(grad_result, axis=(0, 1, 2))
    grad_branch_two = spread_grads(grad_result_low)
    grad_down = jnp.einsum(
        "sabf,sabd->fd", activation_rows, grad_branch_two, preferred_element_type=jnp.float32
    )
    grad_activated = jnp.einsum(
        "sabd,fd->sabf", grad_branch_two, fetched[6], preferred_element_type=jnp.float32
    )
    gelu_pull = jax.vjp(gelu_tanh, before_activation)[1]
    grad_pre = gelu_pull(grad_activated)[0].astype(jnp.bfloat16)
    grad_up_bias = jnp.sum(grad_pre, axis=(0, 1, 2), dtype=jnp.float32)
    grad_up = jnp.einsum("sabd,sabf->df", second_all, grad_pre, preferred_element_type=jnp.float32)
    grad_second = collect_grads(
        jnp.einsum("sabf,df->sabd", grad_pre, fetched[4], preferred_element_type=jnp.float32)
    )
    second_pull = jax.vjp(normalize, hidden, vectors_back[3], vectors_back[4])[1]
    grad_hidden_norm, grad_second_gain, grad_second_shift = second_pull(grad_second)
    grad_hidden = grad_result + grad_hidden_norm
    grad_out_bias = jnp.sum(grad_hidden, axis=(0, 1, 2))
    grad_branch = spread_grads(grad_hidden.astype(jnp.bfloat16))
    grad_out_weight = jnp.einsum(
        "sabc,sabd->cd", attention_result, grad_branch, preferred_element_type=jnp.float32
    )
    grad_attended = jnp.einsum(
        "sabd,cd->sabc", grad_branch, fetched[3], preferred_element_type=jnp.float32
    ).astype(jnp.bfloat16)
    grad_groups = grouped(grad_attended)

    def backward_group(unused_carry, inputs_group):
        query_part, key_part, value_part, grad_part, log_part, pairing_rows = inputs_group
        key_all, value_all = fetch_keys(key_part, value_part)
        places = block_places(pairing_rows, block_rows)
        own_places = lax.dynamic_slice_in_dim(places, ctx_index * local_rows, local_rows, 1)
        allowed = own_places[:, :, None] >= places[:, None, :]

        def joint_pass(operands):
            queries, key_vectors, value_vectors, grad_out, log_total = operands
            probabilities, grad_probs = recompute(
                queries, key_vectors, value_vectors, grad_out, log_total, allowed, score_scale
            )
            row_delta = jnp.sum(probabilities * grad_probs, axis=-1, keepdims=True)
            grad_scores = (probabilities * (grad_probs - row_delta)).astype(jnp.bfloat16)
            grad_query = (
                jnp.einsum(
                    "gqk,gkd->gqd", grad_scores, key_vectors, preferred_element_type=jnp.float32
                )
                * score_scale
            )
            grad_key = (
                jnp.einsum("gqk,gqd->gkd", grad_scores, queries, preferred_element_type=jnp.float32)
                * score_scale
            )
            grad_value = jnp.einsum(
                "gqk,gqd->gkd",
                probabilities.astype(jnp.bfloat16),
                grad_out,
                preferred_element_type=jnp.float32,
            )
            return (grad_query, grad_key, grad_value)

        grad_queries, grad_keys, grad_values = lax.map(
            joint_pass,
            (
                by_head(query_part, head_count),
                by_head(key_all, head_count),
                by_head(value_all, head_count),
                by_head(grad_part, head_count),
                log_part,
            ),
        )
        grad_key_rows, grad_value_rows = (
            lax.psum_scatter(from_head(grad_keys), "ctx", scatter_dimension=1, tiled=True),
            lax.psum_scatter(from_head(grad_values), "ctx", scatter_dimension=1, tiled=True),
        )
        return (
            unused_carry,
            (
                from_head(grad_queries).astype(jnp.bfloat16),
                grad_key_rows.astype(jnp.bfloat16),
                grad_value_rows.astype(jnp.bfloat16),
            ),
        )

    unused_back, (query_grads, key_grads, value_grads) = lax.scan(
        backward_group,
        None,
        (query_groups, key_groups, value_groups, grad_groups, log_groups, pairing_groups),
    )
    grad_query_rows = ungrouped(query_grads)
    grad_value_rows = ungrouped(value_grads)
    grad_projected = jnp.stack([grad_query_rows, ungrouped(key_grads), grad_value_rows], axis=3)
    grad_mix_bias = jnp.stack(
        [
            jnp.sum(grad_query_rows, axis=(0, 1, 2), dtype=jnp.float32),
            jnp.sum(grad_value_rows, axis=(0, 1, 2), dtype=jnp.float32),
        ]
    )[:, None, :]
    grad_mix = jnp.einsum(
        "sabd,sabkc->dkc", first_all, grad_projected, preferred_element_type=jnp.float32
    )
    grad_first = collect_grads(
        jnp.einsum(
            "sabkc,dkc->sabd", grad_projected, fetched[1], preferred_element_type=jnp.float32
        )
    )
    first_pull = jax.vjp(normalize, token_rows, vectors_back[0], vectors_back[1])[1]
    grad_token_norm, grad_first_gain, grad_first_shift = first_pull(grad_first)
    grad_inputs = (grad_hidden + grad_token_norm).reshape(inputs.shape)
    vector_grads = jnp.stack(
        [
            grad_first_gain,
            grad_first_shift,
            grad_out_bias,
            grad_second_gain,
            grad_second_shift,
            grad_down_bias,
        ]
    )
    shards = (
        lax.psum_scatter(vector_grads, "ctx", scatter_dimension=1, tiled=True),
        lax.psum_scatter(grad_mix, "ctx", scatter_dimension=0, tiled=True),
        lax.psum_scatter(grad_mix_bias, "ctx", scatter_dimension=2, tiled=True),
        lax.psum_scatter(grad_out_weight, "ctx", scatter_dimension=1, tiled=True),
        lax.psum_scatter(grad_up, "ctx", scatter_dimension=0, tiled=True),
        lax.psum_scatter(grad_up_bias[None, :], "ctx", scatter_dimension=1, tiled=True),
        lax.psum_scatter(grad_down, "ctx", scatter_dimension=1, tiled=True),
    )
    vector_shard = lax.psum(shards[0], "tp")
    return (
        result.reshape(inputs.shape),
        grad_inputs,
        vector_shard[0],
        vector_shard[1],
        shards[1],
        shards[2],
        shards[3],
        vector_shard[2],
        vector_shard[3],
        vector_shard[4],
        shards[4],
        shards[5],
        shards[6],
        vector_shard[5],
    )


LANES = 128
CHUNK = 256
NT = (((1,), (1,)), ((), ()))
NN = (((1,), (0,)), ((), ()))
TN = (((0,), (0,)), ((), ()))


def mm(left, right, dims):
    return lax.dot_general(left, right, dims, preferred_element_type=jnp.float32)


def causal(span, chunk):
    key_place = lax.broadcasted_iota(jnp.int32, (span, chunk), 0)
    query_place = lax.broadcasted_iota(jnp.int32, (span, chunk), 1) + (span - chunk)
    return key_place <= query_place


def to_places(slots_ref, source, target, block_rows):
    for block in range(target.shape[0] // block_rows):
        start = pl.multiple_of(slots_ref[block] * block_rows, block_rows)
        target[pl.ds(block * block_rows, block_rows), :] = source[pl.ds(start, block_rows), :]


def to_slots(slots_ref, values, target, first_block, block_rows):
    for block in range(values.shape[0] // block_rows):
        start = pl.multiple_of(slots_ref[first_block + block] * block_rows, block_rows)
        target[pl.ds(start, block_rows), :] = values[block * block_rows : (block + 1) * block_rows]


def forward_kernel(block_rows, slots_ref, qkv_ref, out_ref, log_ref, rows):
    length, wide = rows.shape
    width = wide // 3
    chunk = min(CHUNK, length)
    to_places(slots_ref, qkv_ref, rows, block_rows)
    log_ref[...] = jnp.zeros(log_ref.shape, jnp.float32)
    for part in range(length // chunk):
        low, high = part * chunk, (part + 1) * chunk
        allowed = causal(high, chunk)
        columns = []
        for head in range(width // HD):
            lane = head * HD
            queries = rows[low:high, lane : lane + HD]
            keys = rows[0:high, width + lane : width + lane + HD]
            values = rows[0:high, 2 * width + lane : 2 * width + lane + HD]
            scores = jnp.where(allowed, mm(keys, queries, NT) * HD ** (-0.5), -1e30)
            top = jnp.max(scores, axis=0, keepdims=True)
            exponent = jnp.exp(scores - top)
            total = jnp.sum(exponent, axis=0, keepdims=True)
            weights = (exponent * (1.0 / total)).astype(jnp.bfloat16)
            columns.append(mm(values, weights, TN))
            log_ref[head : head + 1, low:high] = top + jnp.log(total)
        attended = jnp.concatenate(columns, axis=0).T.astype(jnp.bfloat16)
        to_slots(slots_ref, attended, out_ref, low // block_rows, block_rows)


def backward_kernel(
    block_rows, slots_ref, qkv_ref, grad_ref, log_ref, out_ref, rows, grads, key_sum, value_sum
):
    length, wide = rows.shape
    width = wide // 3
    chunk = min(CHUNK, length)
    scale = HD ** (-0.5)
    to_places(slots_ref, qkv_ref, rows, block_rows)
    to_places(slots_ref, grad_ref, grads, block_rows)
    key_sum[...] = jnp.zeros(key_sum.shape, jnp.float32)
    value_sum[...] = jnp.zeros(value_sum.shape, jnp.float32)
    for part in range(length // chunk):
        low, high = part * chunk, (part + 1) * chunk
        allowed = causal(high, chunk)
        query_columns, key_parts, value_parts = [], [], []
        for head in range(width // HD):
            lane = head * HD
            queries = rows[low:high, lane : lane + HD]
            keys = rows[0:high, width + lane : width + lane + HD]
            values = rows[0:high, 2 * width + lane : 2 * width + lane + HD]
            grad_out = grads[low:high, lane : lane + HD]
            scores = jnp.where(allowed, mm(keys, queries, NT) * scale, -1e30)
            probs = jnp.exp(scores - log_ref[head : head + 1, low:high])
            grad_probs = mm(values, grad_out, NT)
            delta = jnp.sum(probs * grad_probs, axis=0, keepdims=True)
            grad_scores = (probs * (grad_probs - delta)).astype(jnp.bfloat16)
            value_parts.append(mm(probs.astype(jnp.bfloat16), grad_out, NN))
            key_parts.append(mm(grad_scores, queries, NN))
            query_columns.append(mm(keys, grad_scores, TN))
        key_sum[0:high, :] += jnp.concatenate(key_parts, axis=1)
        value_sum[0:high, :] += jnp.concatenate(value_parts, axis=1)
        grad_query = (jnp.concatenate(query_columns, axis=0).T * scale).astype(jnp.bfloat16)
        to_slots(
            slots_ref, grad_query, out_ref.at[:, 0:width], low // block_rows, block_rows
        )
    to_slots(
        slots_ref,
        (key_sum[...] * scale).astype(jnp.bfloat16),
        out_ref.at[:, width : 2 * width],
        0,
        block_rows,
    )
    to_slots(
        slots_ref,
        value_sum[...].astype(jnp.bfloat16),
        out_ref.at[:, 2 * width : 3 * width],
        0,
        block_rows,
    )


SMEM_SPEC = pl.BlockSpec(memory_space=pltpu.SMEM)
VMEM_SPEC = pl.BlockSpec(memory_space=pltpu.VMEM)
KERNEL_PARAMS = pltpu.CompilerParams(vmem_limit_bytes=48 * 1024 * 1024)


def attend_forward(slots, qkv, block_rows):
    length, wide = qkv.shape
    width = wide // 3
    area = length * length * width
    return pl.pallas_call(
        lambda *refs: forward_kernel(block_rows, *refs),
        out_shape=(
            jax.ShapeDtypeStruct((length, width), jnp.bfloat16),
            jax.ShapeDtypeStruct((8, length), jnp.float32),
        ),
        in_specs=[SMEM_SPEC, VMEM_SPEC],
        out_specs=(VMEM_SPEC, VMEM_SPEC),
        scratch_shapes=[pltpu.VMEM((length, wide), jnp.bfloat16)],
        compiler_params=KERNEL_PARAMS,
        cost_estimate=pl.CostEstimate(
            flops=3 * area, bytes_accessed=8 * length * width, transcendentals=area // HD
        ),
        name="attend_forward",
    )(slots, qkv)


def attend_backward(slots, qkv, grad_out, log_total, block_rows):
    length, wide = qkv.shape
    width = wide // 3
    area = length * length * width
    return pl.pallas_call(
        lambda *refs: backward_kernel(block_rows, *refs),
        out_shape=jax.ShapeDtypeStruct((length, wide), jnp.bfloat16),
        in_specs=[SMEM_SPEC, VMEM_SPEC, VMEM_SPEC, VMEM_SPEC],
        out_specs=VMEM_SPEC,
        scratch_shapes=[
            pltpu.VMEM((length, wide), jnp.bfloat16),
            pltpu.VMEM((length, width), jnp.bfloat16),
            pltpu.VMEM((length, width), jnp.float32),
            pltpu.VMEM((length, width), jnp.float32),
        ],
        compiler_params=KERNEL_PARAMS,
        cost_estimate=pl.CostEstimate(
            flops=7 * area, bytes_accessed=14 * length * width, transcendentals=area // HD
        ),
        name="attend_backward",
    )(slots, qkv, grad_out, log_total)


def swap(values, axis, bit):
    count = lax.axis_size(axis)
    return lax.ppermute(values, axis, [(i, i ^ bit) for i in range(count)])


def gather_bits(shard, axis, order):
    held = {0: shard}
    for bit in order:
        keys = sorted(held)
        arrived = swap(jnp.stack([held[key] for key in keys]), axis, bit)
        for place, key in enumerate(keys):
            held[key ^ bit] = arrived[place]
    own = lax.axis_index(axis)
    whole = jnp.zeros((len(held),) + shard.shape, shard.dtype)
    for key in held:
        whole = lax.dynamic_update_index_in_dim(whole, held[key], own ^ key, 0)
    return whole


def gather_ctx(shard):
    count = lax.axis_size("ctx")
    bits = [1 << place for place in range(count.bit_length() - 1)]
    half = shard.shape[0] // 2
    down = bits[::-1]
    first = gather_bits(shard[:half], "ctx", down)
    second = gather_bits(shard[half:], "ctx", bits[:1] + down[:-1])
    return jnp.concatenate([first, second], axis=1)


def gather_rows(part):
    own = lax.axis_index("tp")
    count = lax.axis_size("tp")
    whole = jnp.zeros((part.shape[0], count) + part.shape[1:], part.dtype)
    for key in range(count):
        piece = part if key == 0 else swap(part, "tp", key)
        whole = lax.dynamic_update_index_in_dim(whole, piece, own ^ key, 1)
    return whole.reshape(part.shape[0], -1, part.shape[2])


def add_rows_everywhere(partial):
    own = lax.axis_index("tp")
    core = own & 1
    halves = partial.astype(jnp.bfloat16).reshape(2, -1, partial.shape[-1])
    mine = lax.dynamic_index_in_dim(halves, core, 0, keepdims=False).astype(jnp.float32)
    arrived = swap(lax.dynamic_index_in_dim(halves, 1 - core, 0, keepdims=False), "tp", 1)
    chip_sum = (mine + arrived.astype(jnp.float32)).astype(jnp.bfloat16)
    arrived = swap(chip_sum, "tp", 2)
    whole = (chip_sum.astype(jnp.float32) + arrived.astype(jnp.float32)).astype(jnp.bfloat16)
    other = swap(whole, "tp", 1)
    is_first = core == 0
    return jnp.concatenate(
        [jnp.where(is_first, whole, other), jnp.where(is_first, other, whole)], axis=0
    )


def add_rows_to_owner(partial, part_rows):
    own = lax.axis_index("tp")
    core, row = own & 1, own >> 1
    width = partial.shape[-1]
    parts = partial.astype(jnp.bfloat16).reshape(-1, 2, 2, part_rows, width)
    mine = lax.dynamic_index_in_dim(parts, core, 2, keepdims=False).astype(jnp.float32)
    arrived = swap(lax.dynamic_index_in_dim(parts, 1 - core, 2, keepdims=False), "tp", 1)
    chip_sum = mine + arrived.astype(jnp.float32)
    mine = lax.dynamic_index_in_dim(chip_sum, row, 1, keepdims=False)
    other = lax.dynamic_index_in_dim(chip_sum, 1 - row, 1, keepdims=False)
    return mine + swap(other.astype(jnp.bfloat16), "tp", 2).astype(jnp.float32)


def exchange(pieces):
    return lax.all_to_all(pieces, "ctx", 0, 0, tiled=True)


def norm_parts(rows):
    row_mean = jnp.mean(rows, axis=-1, keepdims=True)
    centered = rows - row_mean
    variance = jnp.mean(centered * centered, axis=-1, keepdims=True)
    return centered, lax.rsqrt(variance + epsilon)


def norm_backward(normal, scale, gradient, gain):
    scaled = gradient * gain
    return scale * (
        scaled
        - jnp.mean(scaled, axis=-1, keepdims=True)
        - normal * jnp.mean(scaled * normal, axis=-1, keepdims=True)
    )


def fast_body(
    inputs,
    pairing,
    first_gain,
    first_shift,
    query_key_value_weight,
    mix_bias,
    output_projection_weight,
    out_bias,
    second_gain,
    second_shift,
    up_projection_weight,
    up_projection_bias,
    down_projection_weight,
    down_bias,
    cotangent,
):
    low = jnp.bfloat16
    wide = jnp.float32
    seq_count, _, _, part_rows, model_width = inputs.shape
    tp_count = lax.axis_size("tp")
    ctx_count = lax.axis_size("ctx")
    block_rows = part_rows * tp_count
    seq_rows = 2 * block_rows
    row_count = seq_count * seq_rows
    shard = model_width // ctx_count
    dim_local = query_key_value_weight.shape[2]
    hidden_local = up_projection_weight.shape[1]
    groups = ctx_count // seq_count
    width = dim_local // groups
    own_tp = lax.axis_index("tp")

    vectors = jnp.concatenate(
        [
            first_gain,
            first_shift,
            out_bias,
            second_gain,
            second_shift,
            down_bias,
            up_projection_bias[0],
            mix_bias[0, 0],
            mix_bias[1, 0],
        ]
    )
    mix_shard = query_key_value_weight.reshape(shard, 3 * dim_local)
    vector_rows = jnp.pad(vectors, (0, 16 * 3 * dim_local - vectors.shape[0])).reshape(16, -1)
    mix_all = gather_ctx(jnp.concatenate([mix_shard, vector_rows], axis=0))
    late_shard = jnp.concatenate(
        [up_projection_weight, down_projection_weight.T, output_projection_weight.T], axis=1
    )
    late_all = lax.all_gather(late_shard, "ctx", axis=0, tiled=True)
    row_all = gather_rows(inputs.reshape(-1, part_rows, model_width)).reshape(row_count, -1)
    mix_full = mix_all[:, :shard].reshape(model_width, 3 * dim_local)
    vectors_all = mix_all[:, shard:].reshape(ctx_count, -1)[:, : vectors.shape[0]].astype(wide)
    piece = 0
    full = []
    for length in [shard] * 6 + [up_projection_bias.shape[1]] + [mix_bias.shape[2]] * 2:
        full.append(vectors_all[:, piece : piece + length].reshape(-1))
        piece += length
    gain_one, shift_one, bias_out, gain_two, shift_two, bias_down, bias_up, bias_q, bias_v = full
    up_full = late_all[:, :hidden_local]
    down_full = late_all[:, hidden_local : 2 * hidden_local]
    out_full = late_all[:, 2 * hidden_local :]

    x_all = row_all.astype(wide)
    centered, scale_one = norm_parts(x_all)
    first_all = (centered * scale_one * gain_one + shift_one).astype(low)
    bias_mix = jnp.concatenate([bias_q, jnp.zeros_like(bias_q), bias_v])
    projected = (mm(first_all, mix_full, NN) + bias_mix).astype(low)
    projected = jnp.transpose(
        projected.reshape(seq_count, seq_rows, 3, groups, width), (0, 3, 1, 2, 4)
    ).reshape(ctx_count, seq_rows, 3 * width)
    sequence = lax.axis_index("ctx") // groups
    pairs = lax.dynamic_index_in_dim(pairing, sequence, 0, keepdims=False)
    blocks = jnp.stack([pairs, 2 * ctx_count - 1 - pairs], axis=-1).reshape(-1)
    places = jnp.arange(2 * ctx_count, dtype=jnp.int32)
    slots = jnp.sum(
        jnp.where(blocks[None, :] == places[:, None], places[None, :], 0), axis=1
    ).astype(jnp.int32)
    qkv = exchange(projected).reshape(ctx_count * seq_rows, 3 * width)
    attended_heads, log_total = attend_forward(slots, qkv, block_rows)
    attended = exchange(attended_heads.reshape(ctx_count, seq_rows, width))
    attended = jnp.transpose(
        attended.reshape(seq_count, groups, seq_rows, width), (0, 2, 1, 3)
    ).reshape(row_count, dim_local)
    branch = add_rows_everywhere(mm(attended, out_full, NT))
    hidden = x_all + branch.astype(wide) + bias_out
    centered_two, scale_two = norm_parts(hidden)
    normal_two = centered_two * scale_two
    second_all = (normal_two * gain_two + shift_two).astype(low)
    pre_act = mm(second_all, up_full, NN) + bias_up
    activated = gelu_tanh(pre_act).astype(low)

    cot_all = gather_rows(cotangent.reshape(-1, part_rows, model_width)).reshape(row_count, -1)
    grad_activated = mm(cot_all, down_full, NN)
    grad_pre = jax.vjp(gelu_tanh, pre_act)[1](grad_activated)[0].astype(low)
    grad_second = add_rows_everywhere(mm(grad_pre, up_full, NT)).astype(wide)
    grad_down = mm(cot_all, activated, TN).astype(low)
    grad_up = mm(second_all, grad_pre, TN).astype(low)
    feed_shards = lax.psum_scatter(
        jnp.concatenate([grad_up, grad_down], axis=1), "ctx", scatter_dimension=0, tiled=True
    )
    grad_hidden = cot_all.astype(wide) + norm_backward(
        normal_two, scale_two, grad_second, gain_two
    )
    grad_branch = grad_hidden.astype(low)
    grad_attended = mm(grad_branch, out_full, NN).astype(low)
    grad_attended = jnp.transpose(
        grad_attended.reshape(seq_count, seq_rows, groups, width), (0, 2, 1, 3)
    ).reshape(ctx_count, seq_rows, width)
    grad_heads = exchange(grad_attended).reshape(ctx_count * seq_rows, width)
    grad_qkv = attend_backward(slots, qkv, grad_heads, log_total, block_rows)
    grad_out = mm(grad_branch, attended, TN).astype(low)
    down_sum = add_rows_to_owner(mm(activated, down_full, NT), part_rows)
    own_hidden = lax.dynamic_index_in_dim(
        hidden.reshape(-1, tp_count, part_rows, model_width), own_tp, 1, keepdims=False
    )
    result = (own_hidden + down_sum + bias_down).astype(low)

    grad_mixed = exchange(grad_qkv.reshape(ctx_count, seq_rows, 3 * width))
    grad_mixed = jnp.transpose(
        grad_mixed.reshape(seq_count, groups, seq_rows, 3, width), (0, 2, 3, 1, 4)
    ).reshape(row_count, 3 * dim_local)
    grad_mix = mm(first_all, grad_mixed, TN).astype(low)
    grad_first = add_rows_to_owner(mm(grad_mixed, mix_full, NT), part_rows)
    own_rows = inputs.reshape(-1, part_rows, model_width).astype(wide)
    own_centered, own_scale = norm_parts(own_rows)
    own_normal = own_centered * own_scale
    own_grad = lax.dynamic_index_in_dim(
        grad_hidden.reshape(-1, tp_count, part_rows, model_width), own_tp, 1, keepdims=False
    )
    grad_inputs = own_grad + norm_backward(own_normal, own_scale, grad_first, gain_one)
    gain_shift = jnp.stack(
        [jnp.sum(grad_first * own_normal, axis=(0, 1)), jnp.sum(grad_first, axis=(0, 1))]
    )
    gain_shift = gain_shift + swap(gain_shift, "tp", 1)
    gain_shift = gain_shift + swap(gain_shift, "tp", 2)

    def by_shard(vector):
        return vector.reshape(ctx_count, -1)

    mixed_sums = jnp.sum(grad_mixed, axis=0, dtype=wide)
    small = jnp.concatenate(
        [
            by_shard(gain_shift[0]),
            by_shard(gain_shift[1]),
            by_shard(jnp.sum(grad_hidden, axis=0)),
            by_shard(jnp.sum(grad_second * normal_two, axis=0)),
            by_shard(jnp.sum(grad_second, axis=0)),
            by_shard(jnp.sum(cot_all, axis=0, dtype=wide)),
            by_shard(jnp.sum(grad_pre, axis=0, dtype=wide)),
            by_shard(mixed_sums[:dim_local]),
            by_shard(mixed_sums[2 * dim_local :]),
        ],
        axis=1,
    )
    small = jnp.sum(exchange(small), axis=0)
    piece = 0
    sums = []
    for length in [shard] * 6 + [hidden_local // ctx_count] + [dim_local // ctx_count] * 2:
        sums.append(small[piece : piece + length])
        piece += length
    weight_terms = jnp.concatenate([grad_mix, grad_out], axis=1).reshape(ctx_count, shard, -1)
    weight_shard = jnp.sum(exchange(weight_terms).astype(wide), axis=0)
    return (
        result.reshape(inputs.shape),
        grad_inputs.reshape(inputs.shape),
        sums[0],
        sums[1],
        weight_shard[:, : 3 * dim_local].reshape(shard, 3, dim_local),
        jnp.stack(sums[7:9])[:, None, :],
        weight_shard[:, 3 * dim_local :].T,
        sums[2],
        sums[3],
        sums[4],
        feed_shards[:, :hidden_local].astype(wide),
        sums[6][None, :],
        feed_shards[:, hidden_local:].astype(wide).T,
        sums[5],
    )


def fits_exchange(inputs, query_key_value_weight):
    ctx_count, tp_count = lax.axis_size("ctx"), lax.axis_size("tp")
    seq_count = inputs.shape[0]
    if tp_count != 4 or ctx_count % seq_count or ctx_count & (ctx_count - 1):
        return False
    dim_local = query_key_value_weight.shape[2]
    groups = ctx_count // seq_count
    length = ctx_count * 2 * tp_count * inputs.shape[3]
    return dim_local % (groups * LANES) == 0 and length <= 2048


def body(inputs, pairing, first_gain, first_shift, query_key_value_weight, *others):
    chosen = fast_body if fits_exchange(inputs, query_key_value_weight) else general_body
    return chosen(inputs, pairing, first_gain, first_shift, query_key_value_weight, *others)


def solution(mesh):
    return jax.shard_map(
        body,
        mesh=mesh,
        in_specs=(
            P(None, "ctx", None, "tp", None),
            P(),
            P("ctx"),
            P("ctx"),
            P("ctx", None, "tp"),
            P(None, "tp", "ctx"),
            P("tp", "ctx"),
            P("ctx"),
            P("ctx"),
            P("ctx"),
            P("ctx", "tp"),
            P("tp", "ctx"),
            P("tp", "ctx"),
            P("ctx"),
            P(None, "ctx", None, "tp", None),
        ),
        out_specs=(
            P(None, "ctx", None, "tp", None),
            P(None, "ctx", None, "tp", None),
            P("ctx"),
            P("ctx"),
            P("ctx", None, "tp"),
            P(None, "tp", "ctx"),
            P("tp", "ctx"),
            P("ctx"),
            P("ctx"),
            P("ctx"),
            P("ctx", "tp"),
            P("tp", "ctx"),
            P("tp", "ctx"),
            P("ctx"),
        ),
        check_vma=False,
    )
```

```python
import jax
import jax.numpy as jnp
from jax import lax
from jax.experimental import pallas as pl
from jax.experimental.pallas import tpu as pltpu
from jax.sharding import PartitionSpec as P

HD = 64


epsilon = 1e-05


def normalize(token_rows, scaling, offset):
    row_mean = jnp.mean(token_rows, axis=-1, keepdims=True)
    centered = token_rows - row_mean
    variance = jnp.mean(centered * centered, axis=-1, keepdims=True)
    return centered * lax.rsqrt(variance + epsilon) * scaling + offset


def gelu_tanh(values_in):
    return jax.nn.gelu(values_in, approximate=True)


def block_places(pairing_rows, block_rows):
    slot_count = pairing_rows.shape[-1]
    starts = jnp.stack([pairing_rows, 2 * slot_count - 1 - pairing_rows], axis=-1) * block_rows
    within = jnp.arange(block_rows, dtype=jnp.int32)
    return (starts[:, :, :, None] + within).reshape(pairing_rows.shape[0], -1)


def by_head(tensor, head_count):
    seq_span, row_span, model_width = tensor.shape
    return jnp.moveaxis(
        tensor.reshape(seq_span, row_span, head_count, model_width // head_count), 2, 0
    )


def from_head(tensor):
    head_count, seq_span, row_span, head_size = tensor.shape
    return jnp.moveaxis(tensor, 0, 2).reshape(seq_span, row_span, head_count * head_size)


def head_scores(queries, key_vectors, allowed, score_scale):
    scores = (
        jnp.einsum("gqd,gkd->gqk", queries, key_vectors, preferred_element_type=jnp.float32)
        * score_scale
    )
    return jnp.where(allowed, scores, -jnp.inf)


def recompute(queries, key_vectors, value_vectors, grad_out, log_total, allowed, score_scale):
    scores = head_scores(queries, key_vectors, allowed, score_scale)
    probabilities = jnp.exp(scores - log_total[:, :, None])
    grad_probs = jnp.einsum(
        "gqd,gkd->gqk", grad_out, value_vectors, preferred_element_type=jnp.float32
    )
    return (probabilities, grad_probs)


def spread_rows(normed):
    return lax.all_gather(normed, "tp", axis=2, tiled=True)


def collect_rows(partial_terms):
    return lax.psum_scatter(
        partial_terms.astype(jnp.bfloat16), "tp", scatter_dimension=2, tiled=True
    ).astype(jnp.float32)


def spread_grads(gradient_part):
    return lax.all_gather(gradient_part, "tp", axis=2, tiled=True)


def collect_grads(partial_terms):
    return lax.psum_scatter(
        partial_terms.astype(jnp.bfloat16), "tp", scatter_dimension=2, tiled=True
    ).astype(jnp.float32)


def fetch_keys(key_part, value_part):
    return (
        lax.all_gather(key_part, "ctx", axis=1, tiled=True),
        lax.all_gather(value_part, "ctx", axis=1, tiled=True),
    )


def general_body(
    inputs,
    pairing,
    first_gain,
    first_shift,
    query_key_value_weight,
    mix_bias,
    output_projection_weight,
    out_bias,
    second_gain,
    second_shift,
    up_projection_weight,
    up_projection_bias,
    down_projection_weight,
    down_bias,
    cotangent,
):
    seq_count = inputs.shape[0]
    part_rows = inputs.shape[3]
    model_width = inputs.shape[4]
    tp_count = lax.axis_size("tp")
    block_rows = part_rows * tp_count
    local_rows = 2 * block_rows
    ctx_index = lax.axis_index("ctx")
    score_scale = HD ** (-0.5)
    batch_seqs = seq_count
    for candidate in range(seq_count, 0, -1):
        if seq_count % candidate == 0 and candidate * local_rows >= 512:
            batch_seqs = candidate
    groups = seq_count // batch_seqs
    vector_stack = jnp.stack(
        [first_gain, first_shift, out_bias, second_gain, second_shift, down_bias]
    )
    fetched = (
        lax.all_gather(vector_stack, "ctx", axis=1, tiled=True),
        lax.all_gather(query_key_value_weight, "ctx", axis=0, tiled=True),
        lax.all_gather(mix_bias, "ctx", axis=2, tiled=True),
        lax.all_gather(output_projection_weight, "ctx", axis=1, tiled=True),
        lax.all_gather(up_projection_weight, "ctx", axis=0, tiled=True),
        lax.all_gather(up_projection_bias, "ctx", axis=1, tiled=True),
        lax.all_gather(down_projection_weight, "ctx", axis=1, tiled=True),
    )
    vectors_full = fetched[0].astype(jnp.float32)
    dim_local = fetched[2].shape[2]
    head_count = dim_local // HD
    token_rows = inputs.reshape(seq_count, 2, part_rows, model_width).astype(jnp.float32)
    first_norm_output = normalize(token_rows, vectors_full[0], vectors_full[1]).astype(jnp.bfloat16)
    first_all = spread_rows(first_norm_output)
    projected_output = jnp.einsum(
        "sabd,dkc->sabkc", first_all, fetched[1], preferred_element_type=jnp.float32
    )
    bias_full = fetched[2].astype(jnp.float32)
    bias_rows = jnp.stack([bias_full[0, 0], jnp.zeros((dim_local,), jnp.float32), bias_full[1, 0]])
    projected_output = (projected_output + bias_rows).astype(jnp.bfloat16)

    def grouped(tensor):
        return tensor.reshape(groups, batch_seqs, local_rows, tensor.shape[-1])

    def ungrouped(tensor):
        return tensor.reshape(seq_count, 2, block_rows, dim_local)

    query_groups = grouped(projected_output[:, :, :, 0])
    key_groups = grouped(projected_output[:, :, :, 1])
    value_groups = grouped(projected_output[:, :, :, 2])
    pairing_groups = pairing.reshape(groups, batch_seqs, pairing.shape[1])

    def forward_group(unused_carry, inputs_group):
        query_part, key_part, value_part, pairing_rows = inputs_group
        key_all, value_all = fetch_keys(key_part, value_part)
        places = block_places(pairing_rows, block_rows)
        own_places = lax.dynamic_slice_in_dim(places, ctx_index * local_rows, local_rows, 1)
        allowed = own_places[:, :, None] >= places[:, None, :]

        def head_forward(operands):
            queries, key_vectors, value_vectors = operands
            scores = head_scores(queries, key_vectors, allowed, score_scale)
            row_max = jnp.max(scores, axis=-1, keepdims=True)
            exponent = jnp.exp(scores - row_max)
            row_total = jnp.sum(exponent, axis=-1, keepdims=True)
            weights_low = (exponent / row_total).astype(jnp.bfloat16)
            attention_result = jnp.einsum(
                "gqk,gkd->gqd", weights_low, value_vectors, preferred_element_type=jnp.float32
            )
            return (attention_result.astype(jnp.bfloat16), (row_max + jnp.log(row_total))[:, :, 0])

        outputs, log_totals = lax.map(
            head_forward,
            (
                by_head(query_part, head_count),
                by_head(key_all, head_count),
                by_head(value_all, head_count),
            ),
        )
        return (unused_carry, (from_head(outputs), log_totals))

    unused_state, (output_groups, log_groups) = lax.scan(
        forward_group, None, (query_groups, key_groups, value_groups, pairing_groups)
    )
    attention_result = ungrouped(output_groups)
    residual_branch = collect_rows(
        jnp.einsum(
            "sabc,cd->sabd", attention_result, fetched[3], preferred_element_type=jnp.float32
        )
    )
    hidden = token_rows + residual_branch + vectors_full[2]
    second_norm_output = normalize(hidden, vectors_full[3], vectors_full[4]).astype(jnp.bfloat16)
    second_all = spread_rows(second_norm_output)
    before_activation = jnp.einsum(
        "sabd,df->sabf", second_all, fetched[4], preferred_element_type=jnp.float32
    ) + fetched[5][0].astype(jnp.float32)
    activation_rows = gelu_tanh(before_activation).astype(jnp.bfloat16)
    residual_branch_two = collect_rows(
        jnp.einsum("sabf,fd->sabd", activation_rows, fetched[6], preferred_element_type=jnp.float32)
    )
    result = (hidden + residual_branch_two + vectors_full[5]).astype(jnp.bfloat16)
    vectors_back = fetched[0].astype(jnp.float32)
    grad_result_low = cotangent.reshape(seq_count, 2, part_rows, model_width)
    grad_result = grad_result_low.astype(jnp.float32)
    grad_down_bias = jnp.sum(grad_result, axis=(0, 1, 2))
    grad_branch_two = spread_grads(grad_result_low)
    grad_down = jnp.einsum(
        "sabf,sabd->fd", activation_rows, grad_branch_two, preferred_element_type=jnp.float32
    )
    grad_activated = jnp.einsum(
        "sabd,fd->sabf", grad_branch_two, fetched[6], preferred_element_type=jnp.float32
    )
    gelu_pull = jax.vjp(gelu_tanh, before_activation)[1]
    grad_pre = gelu_pull(grad_activated)[0].astype(jnp.bfloat16)
    grad_up_bias = jnp.sum(grad_pre, axis=(0, 1, 2), dtype=jnp.float32)
    grad_up = jnp.einsum("sabd,sabf->df", second_all, grad_pre, preferred_element_type=jnp.float32)
    grad_second = collect_grads(
        jnp.einsum("sabf,df->sabd", grad_pre, fetched[4], preferred_element_type=jnp.float32)
    )
    second_pull = jax.vjp(normalize, hidden, vectors_back[3], vectors_back[4])[1]
    grad_hidden_norm, grad_second_gain, grad_second_shift = second_pull(grad_second)
    grad_hidden = grad_result + grad_hidden_norm
    grad_out_bias = jnp.sum(grad_hidden, axis=(0, 1, 2))
    grad_branch = spread_grads(grad_hidden.astype(jnp.bfloat16))
    grad_out_weight = jnp.einsum(
        "sabc,sabd->cd", attention_result, grad_branch, preferred_element_type=jnp.float32
    )
    grad_attended = jnp.einsum(
        "sabd,cd->sabc", grad_branch, fetched[3], preferred_element_type=jnp.float32
    ).astype(jnp.bfloat16)
    grad_groups = grouped(grad_attended)

    def backward_group(unused_carry, inputs_group):
        query_part, key_part, value_part, grad_part, log_part, pairing_rows = inputs_group
        key_all, value_all = fetch_keys(key_part, value_part)
        places = block_places(pairing_rows, block_rows)
        own_places = lax.dynamic_slice_in_dim(places, ctx_index * local_rows, local_rows, 1)
        allowed = own_places[:, :, None] >= places[:, None, :]

        def joint_pass(operands):
            queries, key_vectors, value_vectors, grad_out, log_total = operands
            probabilities, grad_probs = recompute(
                queries, key_vectors, value_vectors, grad_out, log_total, allowed, score_scale
            )
            row_delta = jnp.sum(probabilities * grad_probs, axis=-1, keepdims=True)
            grad_scores = (probabilities * (grad_probs - row_delta)).astype(jnp.bfloat16)
            grad_query = (
                jnp.einsum(
                    "gqk,gkd->gqd", grad_scores, key_vectors, preferred_element_type=jnp.float32
                )
                * score_scale
            )
            grad_key = (
                jnp.einsum("gqk,gqd->gkd", grad_scores, queries, preferred_element_type=jnp.float32)
                * score_scale
            )
            grad_value = jnp.einsum(
                "gqk,gqd->gkd",
                probabilities.astype(jnp.bfloat16),
                grad_out,
                preferred_element_type=jnp.float32,
            )
            return (grad_query, grad_key, grad_value)

        grad_queries, grad_keys, grad_values = lax.map(
            joint_pass,
            (
                by_head(query_part, head_count),
                by_head(key_all, head_count),
                by_head(value_all, head_count),
                by_head(grad_part, head_count),
                log_part,
            ),
        )
        grad_key_rows, grad_value_rows = (
            lax.psum_scatter(from_head(grad_keys), "ctx", scatter_dimension=1, tiled=True),
            lax.psum_scatter(from_head(grad_values), "ctx", scatter_dimension=1, tiled=True),
        )
        return (
            unused_carry,
            (
                from_head(grad_queries).astype(jnp.bfloat16),
                grad_key_rows.astype(jnp.bfloat16),
                grad_value_rows.astype(jnp.bfloat16),
            ),
        )

    unused_back, (query_grads, key_grads, value_grads) = lax.scan(
        backward_group,
        None,
        (query_groups, key_groups, value_groups, grad_groups, log_groups, pairing_groups),
    )
    grad_query_rows = ungrouped(query_grads)
    grad_value_rows = ungrouped(value_grads)
    grad_projected = jnp.stack([grad_query_rows, ungrouped(key_grads), grad_value_rows], axis=3)
    grad_mix_bias = jnp.stack(
        [
            jnp.sum(grad_query_rows, axis=(0, 1, 2), dtype=jnp.float32),
            jnp.sum(grad_value_rows, axis=(0, 1, 2), dtype=jnp.float32),
        ]
    )[:, None, :]
    grad_mix = jnp.einsum(
        "sabd,sabkc->dkc", first_all, grad_projected, preferred_element_type=jnp.float32
    )
    grad_first = collect_grads(
        jnp.einsum(
            "sabkc,dkc->sabd", grad_projected, fetched[1], preferred_element_type=jnp.float32
        )
    )
    first_pull = jax.vjp(normalize, token_rows, vectors_back[0], vectors_back[1])[1]
    grad_token_norm, grad_first_gain, grad_first_shift = first_pull(grad_first)
    grad_inputs = (grad_hidden + grad_token_norm).reshape(inputs.shape)
    vector_grads = jnp.stack(
        [
            grad_first_gain,
            grad_first_shift,
            grad_out_bias,
            grad_second_gain,
            grad_second_shift,
            grad_down_bias,
        ]
    )
    shards = (
        lax.psum_scatter(vector_grads, "ctx", scatter_dimension=1, tiled=True),
        lax.psum_scatter(grad_mix, "ctx", scatter_dimension=0, tiled=True),
        lax.psum_scatter(grad_mix_bias, "ctx", scatter_dimension=2, tiled=True),
        lax.psum_scatter(grad_out_weight, "ctx", scatter_dimension=1, tiled=True),
        lax.psum_scatter(grad_up, "ctx", scatter_dimension=0, tiled=True),
        lax.psum_scatter(grad_up_bias[None, :], "ctx", scatter_dimension=1, tiled=True),
        lax.psum_scatter(grad_down, "ctx", scatter_dimension=1, tiled=True),
    )
    vector_shard = lax.psum(shards[0], "tp")
    return (
        result.reshape(inputs.shape),
        grad_inputs,
        vector_shard[0],
        vector_shard[1],
        shards[1],
        shards[2],
        shards[3],
        vector_shard[2],
        vector_shard[3],
        vector_shard[4],
        shards[4],
        shards[5],
        shards[6],
        vector_shard[5],
    )


LANES = 128
CHUNK = 256
NT = (((1,), (1,)), ((), ()))
NN = (((1,), (0,)), ((), ()))
TN = (((0,), (0,)), ((), ()))


def mm(left, right, dims):
    return lax.dot_general(left, right, dims, preferred_element_type=jnp.float32)


def causal(span, chunk):
    key_place = lax.broadcasted_iota(jnp.int32, (span, chunk), 0)
    query_place = lax.broadcasted_iota(jnp.int32, (span, chunk), 1) + (span - chunk)
    return key_place <= query_place


def to_places(slots_ref, source, target, block_rows):
    for block in range(target.shape[0] // block_rows):
        start = pl.multiple_of(slots_ref[block] * block_rows, block_rows)
        target[pl.ds(block * block_rows, block_rows), :] = source[pl.ds(start, block_rows), :]


def to_slots(slots_ref, values, target, first_block, block_rows):
    for block in range(values.shape[0] // block_rows):
        start = pl.multiple_of(slots_ref[first_block + block] * block_rows, block_rows)
        target[pl.ds(start, block_rows), :] = values[block * block_rows : (block + 1) * block_rows]


def forward_kernel(block_rows, slots_ref, qkv_ref, out_ref, log_ref, rows):
    length, wide = rows.shape
    width = wide // 3
    chunk = min(CHUNK, length)
    to_places(slots_ref, qkv_ref, rows, block_rows)
    log_ref[...] = jnp.zeros(log_ref.shape, jnp.float32)
    for part in range(length // chunk):
        low, high = part * chunk, (part + 1) * chunk
        allowed = causal(high, chunk)
        columns = []
        for head in range(width // HD):
            lane = head * HD
            queries = rows[low:high, lane : lane + HD]
            keys = rows[0:high, width + lane : width + lane + HD]
            values = rows[0:high, 2 * width + lane : 2 * width + lane + HD]
            scores = jnp.where(allowed, mm(keys, queries, NT) * HD ** (-0.5), -1e30)
            top = jnp.max(scores, axis=0, keepdims=True)
            exponent = jnp.exp(scores - top)
            total = jnp.sum(exponent, axis=0, keepdims=True)
            weights = (exponent * (1.0 / total)).astype(jnp.bfloat16)
            columns.append(mm(values, weights, TN))
            log_ref[head : head + 1, low:high] = top + jnp.log(total)
        attended = jnp.concatenate(columns, axis=0).T.astype(jnp.bfloat16)
        to_slots(slots_ref, attended, out_ref, low // block_rows, block_rows)


def backward_kernel(
    block_rows, slots_ref, qkv_ref, grad_ref, log_ref, out_ref, rows, grads, key_sum, value_sum
):
    length, wide = rows.shape
    width = wide // 3
    chunk = min(CHUNK, length)
    scale = HD ** (-0.5)
    to_places(slots_ref, qkv_ref, rows, block_rows)
    to_places(slots_ref, grad_ref, grads, block_rows)
    key_sum[...] = jnp.zeros(key_sum.shape, jnp.float32)
    value_sum[...] = jnp.zeros(value_sum.shape, jnp.float32)
    for part in range(length // chunk):
        low, high = part * chunk, (part + 1) * chunk
        allowed = causal(high, chunk)
        query_columns, key_parts, value_parts = [], [], []
        for head in range(width // HD):
            lane = head * HD
            queries = rows[low:high, lane : lane + HD]
            keys = rows[0:high, width + lane : width + lane + HD]
            values = rows[0:high, 2 * width + lane : 2 * width + lane + HD]
            grad_out = grads[low:high, lane : lane + HD]
            scores = jnp.where(allowed, mm(keys, queries, NT) * scale, -1e30)
            probs = jnp.exp(scores - log_ref[head : head + 1, low:high])
            grad_probs = mm(values, grad_out, NT)
            delta = jnp.sum(probs * grad_probs, axis=0, keepdims=True)
            grad_scores = (probs * (grad_probs - delta)).astype(jnp.bfloat16)
            value_parts.append(mm(probs.astype(jnp.bfloat16), grad_out, NN))
            key_parts.append(mm(grad_scores, queries, NN))
            query_columns.append(mm(keys, grad_scores, TN))
        key_sum[0:high, :] += jnp.concatenate(key_parts, axis=1)
        value_sum[0:high, :] += jnp.concatenate(value_parts, axis=1)
        grad_query = (jnp.concatenate(query_columns, axis=0).T * scale).astype(jnp.bfloat16)
        to_slots(
            slots_ref, grad_query, out_ref.at[:, 0:width], low // block_rows, block_rows
        )
    to_slots(
        slots_ref,
        (key_sum[...] * scale).astype(jnp.bfloat16),
        out_ref.at[:, width : 2 * width],
        0,
        block_rows,
    )
    to_slots(
        slots_ref,
        value_sum[...].astype(jnp.bfloat16),
        out_ref.at[:, 2 * width : 3 * width],
        0,
        block_rows,
    )


def whole_shape(shape):
    return pl.BlockSpec(shape, lambda step: (0,) * len(shape))


def whole_block(array):
    return whole_shape(array.shape)


SMEM_SPEC = pl.BlockSpec(memory_space=pltpu.SMEM)
KERNEL_PARAMS = pltpu.CompilerParams(vmem_limit_bytes=60 * 1024 * 1024)


def attend_forward(slots, qkv, block_rows):
    length, wide = qkv.shape
    width = wide // 3
    area = length * length * width
    return pl.pallas_call(
        lambda *refs: forward_kernel(block_rows, *refs),
        out_shape=(
            jax.ShapeDtypeStruct((length, width), jnp.bfloat16),
            jax.ShapeDtypeStruct((8, length), jnp.float32),
        ),
        grid=(1,),
        in_specs=[SMEM_SPEC, whole_block(qkv)],
        out_specs=(whole_shape((length, width)), whole_shape((8, length))),
        scratch_shapes=[pltpu.VMEM((length, wide), jnp.bfloat16)],
        compiler_params=KERNEL_PARAMS,
        cost_estimate=pl.CostEstimate(
            flops=3 * area, bytes_accessed=8 * length * width, transcendentals=area // HD
        ),
        name="attend_forward",
    )(slots, qkv)


def attend_backward(slots, qkv, grad_out, log_total, block_rows):
    length, wide = qkv.shape
    width = wide // 3
    area = length * length * width
    return pl.pallas_call(
        lambda *refs: backward_kernel(block_rows, *refs),
        out_shape=jax.ShapeDtypeStruct((length, wide), jnp.bfloat16),
        grid=(1,),
        in_specs=[SMEM_SPEC, whole_block(qkv), whole_block(grad_out), whole_block(log_total)],
        out_specs=whole_shape((length, wide)),
        scratch_shapes=[
            pltpu.VMEM((length, wide), jnp.bfloat16),
            pltpu.VMEM((length, width), jnp.bfloat16),
            pltpu.VMEM((length, width), jnp.float32),
            pltpu.VMEM((length, width), jnp.float32),
        ],
        compiler_params=KERNEL_PARAMS,
        cost_estimate=pl.CostEstimate(
            flops=7 * area, bytes_accessed=14 * length * width, transcendentals=area // HD
        ),
        name="attend_backward",
    )(slots, qkv, grad_out, log_total)


def swap(values, axis, bit):
    count = lax.axis_size(axis)
    return lax.ppermute(values, axis, [(i, i ^ bit) for i in range(count)])


def together(*groups):
    return lax.optimization_barrier(groups)


def spread_step(held, axis, bit):
    keys = tuple(key for offsets, _ in held for key in offsets)
    arrays = [array for _, array in held]
    sent = arrays[0] if len(arrays) == 1 else jnp.concatenate(arrays, axis=0)
    return (keys, sent), (tuple(key ^ bit for key in keys), swap(sent, axis, bit))


def pack_kernel(pieces, mix_ref, out_weight_ref, *refs):
    vectors, (head_ref, tail_ref) = refs[:-2], refs[-2:]
    half = tail_ref.shape[1]
    parts, _, part_width = mix_ref.shape
    mix_width = parts * part_width
    shard = 2 * half
    for target, first in ((head_ref, 0), (tail_ref, half)):
        for part in range(parts):
            target[0, 0:half, part * part_width : (part + 1) * part_width] = mix_ref[
                part, first : first + half, :
            ]
        for piece in range(pieces):
            target[0, 0:half, mix_width + piece * shard : mix_width + (piece + 1) * shard] = (
                out_weight_ref[piece * shard + first : piece * shard + first + half, :]
            )
    extra = head_ref.shape[1] - half
    head_ref[0, half:, :] = jnp.zeros((extra, head_ref.shape[2]), jnp.bfloat16)
    for number, vector in enumerate(vectors):
        head_ref[0, half : half + 1, number * shard : number * shard + vector.shape[1]] = vector[...]


def late_kernel(up_ref, down_ref, late_ref):
    hidden_local = up_ref.shape[1]
    late_ref[:, 0:hidden_local] = up_ref[...]
    late_ref[:, hidden_local:] = down_ref[...].T


def pack_late(up_shard, down_shard):
    shard, hidden_local = up_shard.shape
    return pl.pallas_call(
        late_kernel,
        out_shape=jax.ShapeDtypeStruct((shard, 2 * hidden_local), jnp.bfloat16),
        grid=(1,),
        in_specs=[whole_block(up_shard), whole_block(down_shard)],
        out_specs=whole_shape((shard, 2 * hidden_local)),
        compiler_params=KERNEL_PARAMS,
        name="pack_late",
    )(up_shard, down_shard)


def pack(mix_shard, out_shard, vectors):
    parts, shard, part_width = mix_shard.shape
    pieces = out_shard.shape[0] // shard
    total = parts * part_width + out_shard.shape[0]
    return pl.pallas_call(
        lambda *refs: pack_kernel(pieces, *refs),
        out_shape=(
            jax.ShapeDtypeStruct((1, shard // 2 + 16, total), jnp.bfloat16),
            jax.ShapeDtypeStruct((1, shard // 2, total), jnp.bfloat16),
        ),
        grid=(1,),
        in_specs=[whole_block(array) for array in (mix_shard, out_shard, *vectors)],
        out_specs=(
            whole_shape((1, shard // 2 + 16, total)),
            whole_shape((1, shard // 2, total)),
        ),
        compiler_params=KERNEL_PARAMS,
        name="pack",
    )(mix_shard, out_shard, *vectors)


def first_kernel(head_keys, tail_keys, sizes, own_ref, *refs):
    groups, width, vector_count, bias_width = sizes
    tp_count = 4
    parts, refs = refs[:tp_count], refs[tp_count:]
    heads, refs = refs[: len(head_keys)], refs[len(head_keys) :]
    tails, refs = refs[: len(tail_keys)], refs[len(tail_keys) :]
    rows_ref, first_ref, weight_ref, out_weight_ref, table_ref, send_ref, gathered = refs
    own_tp, own_ctx = own_ref[0], own_ref[1]
    mix_width = weight_ref.shape[1]
    half = tails[0].shape[1]
    shard = 2 * half

    def put_out(piece, place, owner, first):
        columns = pl.ds(pl.multiple_of(owner * shard, shard), shard)
        for number in range(out_weight_ref.shape[0] // shard):
            low = mix_width + number * shard
            out_weight_ref[number * shard + first : number * shard + first + half, columns] = piece[
                place, 0:half, low : low + shard
            ]

    for keys, piece in zip(head_keys, heads):
        for place, key in enumerate(keys):
            owner = own_ctx ^ key
            rows = pl.ds(pl.multiple_of(owner * shard, shard), half)
            weight_ref[rows, :] = piece[place, 0:half, 0:mix_width]
            put_out(piece, place, owner, 0)
            extra = piece[place, half:, :].astype(jnp.float32)
            gathered[pl.ds(owner, 1), :] = extra[0:1, :]
    for keys, piece in zip(tail_keys, tails):
        for place, key in enumerate(keys):
            owner = own_ctx ^ key
            rows = pl.ds(pl.multiple_of(owner * shard + half, half), half)
            weight_ref[rows, :] = piece[place, :, 0:mix_width]
            put_out(piece, place, owner, half)
    count = gathered.shape[0]
    vectors = gathered[...]
    table_ref[...] = jnp.zeros(table_ref.shape, jnp.float32)
    for number in range(vector_count):
        lanes = slice(number * shard, (number + 1) * shard)
        for owner in range(count):
            table_ref[number : number + 1, owner * shard : (owner + 1) * shard] = vectors[
                owner : owner + 1, lanes
            ]
    bias_parts = []
    for number in range(2):
        low = vector_count * shard + number * bias_width
        bias_parts.append(
            jnp.concatenate(
                [vectors[owner : owner + 1, low : low + bias_width] for owner in range(count)],
                axis=1,
            )
        )
    bias = jnp.concatenate([bias_parts[0], jnp.zeros_like(bias_parts[0]), bias_parts[1]], axis=1)
    piece_count, part_rows, _ = parts[0].shape
    block_rows = tp_count * part_rows
    for key in range(tp_count):
        for piece in range(piece_count):
            row = pl.multiple_of(piece * block_rows + (own_tp ^ key) * part_rows, part_rows)
            rows_ref[pl.ds(row, part_rows), :] = parts[key][piece]
    seq_rows = send_ref.shape[1]
    dim_local = mix_width // 3
    gain, shift = table_ref[0:1, :], table_ref[1:2, :]
    for seq in range(rows_ref.shape[0] // seq_rows):
        rows = slice(seq * seq_rows, (seq + 1) * seq_rows)
        centered, scale = norm_parts(rows_ref[rows, :].astype(jnp.float32))
        normed = (centered * scale * gain + shift).astype(jnp.bfloat16)
        first_ref[rows, :] = normed
        projected = (mm(normed, weight_ref[...], NN) + bias).astype(jnp.bfloat16)
        for group in range(groups):
            for number in range(3):
                low = number * dim_local + group * width
                send_ref[seq * groups + group, :, number * width : (number + 1) * width] = (
                    projected[:, low : low + width]
                )


def first_part(own, parts, heads, tails, seq_count, groups, vector_count, bias_width):
    piece_count, part_rows, model_width = parts[0].shape
    row_count = piece_count * part_rows * 4
    count = seq_count * groups
    mix_width = 3 * model_width // 4
    head_keys, head_arrays = zip(*heads)
    tail_keys, tail_arrays = zip(*tails)
    seq_rows = row_count // seq_count
    width = mix_width // (3 * groups)
    low = jnp.bfloat16
    shapes = (
        ((row_count, model_width), low),
        ((row_count, model_width), low),
        ((model_width, mix_width), low),
        ((head_arrays[0].shape[2] - mix_width, model_width), low),
        ((8, model_width), jnp.float32),
        ((count, seq_rows, 3 * width), low),
    )
    return pl.pallas_call(
        lambda *refs: first_kernel(
            head_keys, tail_keys, (groups, width, vector_count, bias_width), *refs
        ),
        out_shape=tuple(jax.ShapeDtypeStruct(*shape) for shape in shapes),
        grid=(1,),
        in_specs=[SMEM_SPEC]
        + [whole_block(array) for array in (*parts, *head_arrays, *tail_arrays)],
        out_specs=tuple(whole_shape(shape) for shape, _ in shapes),
        scratch_shapes=[pltpu.VMEM((count, head_arrays[0].shape[2]), jnp.float32)],
        compiler_params=KERNEL_PARAMS,
        cost_estimate=pl.CostEstimate(
            flops=2 * row_count * model_width * mix_width,
            bytes_accessed=8 * 1024 * 1024,
            transcendentals=0,
        ),
        name="first_part",
    )(own, *parts, *head_arrays, *tail_arrays)


def feed_grads_kernel(second_ref, grad_pre_ref, cot_ref, activated_ref, out_ref):
    half = grad_pre_ref.shape[1]
    out_ref[:, 0:half] = mm(second_ref[...], grad_pre_ref[...], TN).astype(jnp.bfloat16)
    out_ref[:, half:] = mm(cot_ref[...], activated_ref[...], TN).astype(jnp.bfloat16)


def feed_grads(second_all, grad_pre, cot_all, activated):
    row_count, model_width = second_all.shape
    hidden_local = grad_pre.shape[1]
    step = min(256, model_width)
    column = pl.BlockSpec((row_count, step), lambda i: (0, i))
    fixed = pl.BlockSpec((row_count, hidden_local), lambda i: (0, 0))
    return pl.pallas_call(
        feed_grads_kernel,
        grid=(model_width // step,),
        out_shape=jax.ShapeDtypeStruct((model_width, 2 * hidden_local), jnp.bfloat16),
        in_specs=[column, fixed, column, fixed],
        out_specs=pl.BlockSpec((step, 2 * hidden_local), lambda i: (i, 0)),
        compiler_params=KERNEL_PARAMS,
        cost_estimate=pl.CostEstimate(
            flops=4 * row_count * model_width * hidden_local,
            bytes_accessed=8 * 1024 * 1024,
            transcendentals=0,
        ),
        name="feed_grads",
    )(second_all, grad_pre, cot_all, activated)


def feed_finish_kernel(sum_ref, up_ref, down_ref):
    half = up_ref.shape[1]
    up_ref[...] = sum_ref[:, 0:half].astype(jnp.float32)
    down_ref[...] = sum_ref[:, half:].astype(jnp.float32).T


def feed_finish(total):
    shard, twice = total.shape
    shapes = ((shard, twice // 2), (twice // 2, shard))
    return pl.pallas_call(
        feed_finish_kernel,
        grid=(1,),
        out_shape=tuple(jax.ShapeDtypeStruct(shape, jnp.float32) for shape in shapes),
        in_specs=[whole_block(total)],
        out_specs=tuple(whole_shape(shape) for shape in shapes),
        compiler_params=KERNEL_PARAMS,
        name="feed_finish",
    )(total)


def mix_finish_kernel(mine_ref, came_ref, mix_ref, out_ref):
    total = mine_ref[...].astype(jnp.float32) + came_ref[...].astype(jnp.float32)
    parts, _, part_width = mix_ref.shape
    for part in range(parts):
        mix_ref[part] = total[:, part * part_width : (part + 1) * part_width]
    out_ref[...] = total[:, parts * part_width :].T


def mix_finish(mine, came, dim_local):
    shapes = ((3, came.shape[0], dim_local), (dim_local, came.shape[0]))
    return pl.pallas_call(
        mix_finish_kernel,
        grid=(1,),
        out_shape=tuple(jax.ShapeDtypeStruct(shape, jnp.float32) for shape in shapes),
        in_specs=[whole_block(mine), whole_block(came)],
        out_specs=tuple(whole_shape(shape) for shape in shapes),
        compiler_params=KERNEL_PARAMS,
        name="mix_finish",
    )(mine, came)


MLP_ROWS = 128


def branch_kernel(own_ref, attended_ref, weight_ref, mine_ref, other_ref):
    core = own_ref[0] & 1
    count, seq_rows, width = attended_ref.shape
    seqs = mine_ref.shape[0] // seq_rows
    groups = count // (2 * seqs)
    for half, out_ref in enumerate((mine_ref, other_ref)):
        for seq in range(seqs):
            first = ((core ^ half) * seqs + seq) * groups
            total = mm(attended_ref[first], weight_ref[0:width, :], NN)
            for group in range(1, groups):
                total += mm(
                    attended_ref[first + group],
                    weight_ref[group * width : (group + 1) * width, :],
                    NN,
                )
            out_ref[seq * seq_rows : (seq + 1) * seq_rows, :] = total.astype(jnp.bfloat16)


def branch_part(own, attended, out_full):
    count, seq_rows, width = attended.shape
    rows = count * seq_rows * width // out_full.shape[0]
    shape = (rows // 2, out_full.shape[1])
    return pl.pallas_call(
        branch_kernel,
        grid=(1,),
        out_shape=(jax.ShapeDtypeStruct(shape, jnp.bfloat16),) * 2,
        in_specs=[SMEM_SPEC, whole_block(attended), whole_block(out_full)],
        out_specs=(whole_shape(shape),) * 2,
        compiler_params=KERNEL_PARAMS,
        name="branch_part",
    )(own, attended, out_full)


def hidden_grad_kernel(
    own_ref,
    sum_ref,
    other_ref,
    cot_ref,
    hidden_ref,
    table_ref,
    weight_ref,
    send_ref,
    branch_ref,
    own_grad_ref,
    sums_ref,
    rows_ref,
):
    own_tp = own_ref[0]
    core = own_tp & 1
    count, seq_rows, width = send_ref.shape
    _, part_rows, model_width = own_grad_ref.shape
    seqs = sum_ref.shape[0] // seq_rows
    groups = count // (2 * seqs)
    block_rows = seq_rows // 2
    gain = table_ref[3:4, :]
    sums = [jnp.zeros((1, model_width), jnp.float32) for _ in range(3)]
    for half, grad_ref in enumerate((sum_ref, other_ref)):
        for chunk in range(seqs):
            seq = (core ^ half) * seqs + chunk
            rows = pl.ds(pl.multiple_of(seq * seq_rows, seq_rows), seq_rows)
            grad = grad_ref[chunk * seq_rows : (chunk + 1) * seq_rows, :].astype(jnp.float32)
            centered, scale = norm_parts(hidden_ref[rows, :])
            normal = centered * scale
            total = cot_ref[rows, :].astype(jnp.float32) + norm_backward(normal, scale, grad, gain)
            low = total.astype(jnp.bfloat16)
            branch_ref[rows, :] = low
            rows_ref[...] = total
            for block in range(2):
                first = pl.multiple_of(block * block_rows + own_tp * part_rows, part_rows)
                own_grad_ref[seq * 2 + block] = rows_ref[pl.ds(first, part_rows), :]
            attended = mm(low, weight_ref[...], NT).astype(jnp.bfloat16)
            for group in range(groups):
                send_ref[seq * groups + group] = attended[:, group * width : (group + 1) * width]
            sums[0] += jnp.sum(total, axis=0, keepdims=True)
            sums[1] += jnp.sum(grad * normal, axis=0, keepdims=True)
            sums[2] += jnp.sum(grad, axis=0, keepdims=True)
    sums_ref[...] = jnp.zeros(sums_ref.shape, jnp.float32)
    for number, total in enumerate(sums):
        sums_ref[number : number + 1, :] = total


def hidden_grad_part(own, grad_sum, grad_other, cot_all, hidden, table, out_full, sizes):
    count, seq_rows, width, part_rows = sizes
    row_count, model_width = hidden.shape
    low = jnp.bfloat16
    shapes = (
        ((count, seq_rows, width), low),
        ((row_count, model_width), low),
        ((2 * row_count // seq_rows, part_rows, model_width), jnp.float32),
        ((8, model_width), jnp.float32),
    )
    arrays = (grad_sum, grad_other, cot_all, hidden, table, out_full)
    return pl.pallas_call(
        hidden_grad_kernel,
        grid=(1,),
        out_shape=tuple(jax.ShapeDtypeStruct(*shape) for shape in shapes),
        in_specs=[SMEM_SPEC] + [whole_block(array) for array in arrays],
        out_specs=tuple(whole_shape(shape) for shape, _ in shapes),
        scratch_shapes=[pltpu.VMEM((seq_rows, model_width), jnp.float32)],
        compiler_params=KERNEL_PARAMS,
        name="hidden_grad_part",
    )(own, *arrays)


def place_mixed(source_ref, target, width):
    count, seq_rows, total = source_ref.shape
    parts = total // width
    groups = target.shape[1] // total
    for index in range(count):
        seq, group = index // groups, index % groups
        for part in range(parts):
            low = (part * groups + group) * width
            target[seq * seq_rows : (seq + 1) * seq_rows, low : low + width] = source_ref[
                index, :, part * width : (part + 1) * width
            ]


def mix_grads_kernel(keys, own_ref, grad_ref, branch_ref, attended_ref, *refs):
    pieces, (mine_ref, other_ref, normed, attended) = refs[:-4], refs[-4:]
    own_core, own_ctx = own_ref[0] & 1, own_ref[1]
    place_mixed(attended_ref, attended, attended_ref.shape[2])
    half, shard, _ = mine_ref.shape
    width = grad_ref.shape[1]
    for (piece_keys, core_key), piece in zip(keys, pieces):
        part_rows = piece.shape[1]
        for place, key in enumerate(piece_keys):
            start = (own_ctx ^ key) * 2 * part_rows + (own_core ^ core_key) * part_rows
            normed[pl.ds(pl.multiple_of(start, part_rows), part_rows), :] = piece[place]
    for flipped, out_ref in enumerate((mine_ref, other_ref)):
        for index in range(half):
            owner = 2 * index + ((own_ctx & 1) ^ flipped)
            columns = pl.ds(pl.multiple_of(owner * shard, shard), shard)
            out_ref[index, :, 0:width] = mm(normed[:, columns], grad_ref[...], TN).astype(
                jnp.bfloat16
            )
            out_ref[index, :, width:] = mm(branch_ref[:, columns], attended[...], TN).astype(
                jnp.bfloat16
            )


def mix_grads(own, grad_qkv, grad_branch, attended, held):
    keys = [(offsets, core_key) for offsets, core_key, _ in held]
    pieces = [piece for _, _, piece in held]
    length, width = grad_qkv.shape
    row_count, model_width = grad_branch.shape
    count, seq_rows, _ = attended.shape
    out_width = attended.size // row_count
    shape = (count // 2, model_width // count, width + out_width)
    low = jnp.bfloat16
    arrays = (grad_qkv, grad_branch, attended, *pieces)
    return pl.pallas_call(
        lambda *refs: mix_grads_kernel(keys, *refs),
        grid=(1,),
        out_shape=(jax.ShapeDtypeStruct(shape, low),) * 2,
        in_specs=[SMEM_SPEC] + [whole_block(array) for array in arrays],
        out_specs=(whole_shape(shape),) * 2,
        scratch_shapes=[
            pltpu.VMEM((length, model_width), low),
            pltpu.VMEM((row_count, out_width), low),
        ],
        compiler_params=KERNEL_PARAMS,
        cost_estimate=pl.CostEstimate(
            flops=2 * model_width * (length * width + row_count * out_width),
            bytes_accessed=8 * 1024 * 1024,
            transcendentals=0,
        ),
        name="mix_grads",
    )(own, *arrays)


def mix_join_kernel(own_ref, mine_ref, came_ref, keep_ref, send_ref):
    own_ctx = own_ref[1]
    is_first = (own_ctx & 1) == 0
    own_bit = (own_ctx >> 1) & 1
    total, wide_total = mine_ref.shape[2], keep_ref.shape[2]
    width = (wide_total - total) // 3
    for flipped, out_ref in enumerate((keep_ref, send_ref)):
        for index in range(out_ref.shape[0]):
            source = 2 * index + (own_bit ^ flipped)
            mine, came = mine_ref[source], came_ref[source]
            first = jnp.where(is_first, mine, came)
            second = jnp.where(is_first, came, mine)
            for part in range(3):
                lanes = slice(part * width, (part + 1) * width)
                low = 2 * part * width
                out_ref[index, :, low : low + width] = first[:, lanes]
                out_ref[index, :, low + width : low + 2 * width] = second[:, lanes]
            out_ref[index, :, 6 * width :] = (
                mine[:, 3 * width :].astype(jnp.float32) + came[:, 3 * width :].astype(jnp.float32)
            ).astype(jnp.bfloat16)


def mix_join(own, mine, came, width):
    half, shard, total = mine.shape
    shape = (half // 2, shard, total + 3 * width)
    return pl.pallas_call(
        mix_join_kernel,
        grid=(1,),
        out_shape=(jax.ShapeDtypeStruct(shape, jnp.bfloat16),) * 2,
        in_specs=[SMEM_SPEC, whole_block(mine), whole_block(came)],
        out_specs=(whole_shape(shape),) * 2,
        compiler_params=KERNEL_PARAMS,
        name="mix_join",
    )(own, mine, came)


def first_grad_kernel(own_ref, mixed_ref, weight_ref, x_ref, mine_ref, other_ref, sums_ref, *refs):
    mixed, rows_ref = refs
    own_tp = own_ref[0]
    core = own_tp & 1
    count, seq_rows, total = mixed_ref.shape
    groups = mixed.shape[1] // total
    place_mixed(mixed_ref, mixed, total // 3)
    part_rows = mine_ref.shape[2]
    model_width = x_ref.shape[1]
    block_rows = seq_rows // 2
    sums = [jnp.zeros((1, model_width), jnp.float32) for _ in range(2)]
    for seq in range(count // groups):
        rows = slice(seq * seq_rows, (seq + 1) * seq_rows)
        partial = mm(mixed[rows, :], weight_ref[...], NT)
        rows_ref[...] = partial.astype(jnp.bfloat16)
        for block in range(2):
            for row in range(2):
                for flipped, out_ref in enumerate((mine_ref, other_ref)):
                    owner = 2 * row + (core ^ flipped)
                    first = pl.multiple_of(block * block_rows + owner * part_rows, part_rows)
                    out_ref[2 * seq + block, row] = rows_ref[pl.ds(first, part_rows), :]
        centered, scale = norm_parts(x_ref[rows, :].astype(jnp.float32))
        sums[0] += jnp.sum(partial * (centered * scale), axis=0, keepdims=True)
        sums[1] += jnp.sum(partial, axis=0, keepdims=True)
    sums_ref[...] = jnp.zeros(sums_ref.shape, jnp.float32)
    for number, value in enumerate(sums):
        sums_ref[number : number + 1, :] = value
    mixed_ref_sum = jnp.sum(mixed[...].astype(jnp.float32), axis=0, keepdims=True)
    sums_ref[2:3, 0 : mixed.shape[1]] = mixed_ref_sum


def first_grads(own, grad_mixed, mix_full, x_all, part_rows):
    count, seq_rows, total = grad_mixed.shape
    row_count, model_width = x_all.shape
    shape = (2 * row_count // seq_rows, 2, part_rows, model_width)
    low = jnp.bfloat16
    arrays = (grad_mixed, mix_full, x_all)
    return pl.pallas_call(
        first_grad_kernel,
        grid=(1,),
        out_shape=(
            jax.ShapeDtypeStruct(shape, low),
            jax.ShapeDtypeStruct(shape, low),
            jax.ShapeDtypeStruct((8, model_width), jnp.float32),
        ),
        in_specs=[SMEM_SPEC] + [whole_block(array) for array in arrays],
        out_specs=(whole_shape(shape), whole_shape(shape), whole_shape((8, model_width))),
        scratch_shapes=[
            pltpu.VMEM((row_count, mix_full.shape[1]), low),
            pltpu.VMEM((seq_rows, model_width), low),
        ],
        compiler_params=KERNEL_PARAMS,
        name="first_grads",
    )(own, *arrays)


def gelu_both(value):
    root = (2.0 / jnp.pi) ** 0.5
    square = value * value
    inner = jnp.tanh(root * value * (1.0 + 0.044715 * square))
    slope = 0.5 * (1.0 + inner) + 0.5 * value * (1.0 - inner * inner) * root * (
        1.0 + 3.0 * 0.044715 * square
    )
    return 0.5 * value * (1.0 + inner), slope


def feed_kernel(part_count, own_ref, sum_ref, other_ref, x_ref, table_ref, late_ref, *refs):
    cot_parts, refs = refs[:part_count], refs[part_count:]
    (
        hidden_ref,
        second_ref,
        activated_ref,
        grad_pre_ref,
        mine_ref,
        partner_ref,
        cot_ref,
        sums_ref,
    ) = refs
    own_tp = own_ref[0]
    core = own_tp & 1
    hidden_local = activated_ref.shape[1]
    blocks, part_rows, _ = cot_parts[0].shape
    for key, part in enumerate(cot_parts):
        for block in range(blocks):
            row = block * part_count * part_rows + (own_tp ^ key) * part_rows
            cot_ref[pl.ds(pl.multiple_of(row, part_rows), part_rows), :] = part[block]
    half_rows = sum_ref.shape[0]
    up_sum = jnp.zeros((1, hidden_local), jnp.float32)
    cot_sum = jnp.zeros((1, cot_ref.shape[1]), jnp.float32)
    for half, (branch_ref, out_ref) in enumerate(((sum_ref, mine_ref), (other_ref, partner_ref))):
        for chunk in range(half_rows // MLP_ROWS):
            inside = slice(chunk * MLP_ROWS, (chunk + 1) * MLP_ROWS)
            start = (core ^ half) * half_rows + chunk * MLP_ROWS
            rows = pl.ds(pl.multiple_of(start, MLP_ROWS), MLP_ROWS)
            hidden = (
                x_ref[rows, :].astype(jnp.float32)
                + branch_ref[inside, :].astype(jnp.float32)
                + table_ref[2:3, :]
            )
            hidden_ref[rows, :] = hidden
            centered, scale = norm_parts(hidden)
            second = (centered * scale * table_ref[3:4, :] + table_ref[4:5, :]).astype(jnp.bfloat16)
            second_ref[rows, :] = second
            activated, slope = gelu_both(mm(second, late_ref[:, 0:hidden_local], NN) + table_ref[6:7, :])
            activated_ref[rows, :] = activated.astype(jnp.bfloat16)
            cot = cot_ref[rows, :]
            grad_pre = (mm(cot, late_ref[:, hidden_local:], NN) * slope).astype(jnp.bfloat16)
            grad_pre_ref[rows, :] = grad_pre
            out_ref[inside, :] = mm(grad_pre, late_ref[:, 0:hidden_local], NT).astype(jnp.bfloat16)
            up_sum += jnp.sum(grad_pre.astype(jnp.float32), axis=0, keepdims=True)
            cot_sum += jnp.sum(cot.astype(jnp.float32), axis=0, keepdims=True)
    sums_ref[...] = jnp.zeros(sums_ref.shape, jnp.float32)
    sums_ref[0:1, 0:hidden_local] = up_sum
    sums_ref[1:2, 0 : cot_ref.shape[1]] = cot_sum


def feed_part(own, branch_sum, branch_other, x_all, table, late_all, cot_parts):
    row_count, model_width = x_all.shape
    hidden_local = late_all.shape[1] // 2
    low = jnp.bfloat16
    shapes = (
        ((row_count, model_width), jnp.float32),
        ((row_count, model_width), low),
        ((row_count, hidden_local), low),
        ((row_count, hidden_local), low),
        ((row_count // 2, model_width), low),
        ((row_count // 2, model_width), low),
        ((row_count, model_width), low),
        ((8, max(model_width, hidden_local)), jnp.float32),
    )
    arrays = (branch_sum, branch_other, x_all, table, late_all, *cot_parts)
    return pl.pallas_call(
        lambda *refs: feed_kernel(len(cot_parts), *refs),
        grid=(1,),
        out_shape=tuple(jax.ShapeDtypeStruct(*shape) for shape in shapes),
        in_specs=[SMEM_SPEC] + [whole_block(array) for array in arrays],
        out_specs=tuple(whole_shape(shape) for shape, _ in shapes),
        compiler_params=KERNEL_PARAMS,
        cost_estimate=pl.CostEstimate(
            flops=6 * row_count * model_width * hidden_local,
            bytes_accessed=16 * 1024 * 1024,
            transcendentals=row_count * hidden_local,
        ),
        name="feed_part",
    )(own, *arrays)


def spread_tp(part):
    return [part] + [swap(part, "tp", key) for key in (1, 2, 3)]


def add_halves(mine, other, beside=None):
    arrived = swap(other, "tp", 1)
    chip_sum = (mine.astype(jnp.float32) + arrived.astype(jnp.float32)).astype(jnp.bfloat16)
    arrived = swap(chip_sum, "tp", 2)
    if beside is not None:
        arrived, beside = together(arrived, beside)
    whole = (chip_sum.astype(jnp.float32) + arrived.astype(jnp.float32)).astype(jnp.bfloat16)
    return whole, swap(whole, "tp", 1), beside


def owner_first(partial, part_rows):
    core = lax.axis_index("tp") & 1
    parts = partial.astype(jnp.bfloat16).reshape(-1, 2, 2, part_rows, partial.shape[-1])
    mine = lax.dynamic_index_in_dim(parts, core, 2, keepdims=False)
    return mine, swap(lax.dynamic_index_in_dim(parts, 1 - core, 2, keepdims=False), "tp", 1)


def owner_second(mine, arrived):
    row = lax.axis_index("tp") >> 1
    chip_sum = mine.astype(jnp.float32) + arrived.astype(jnp.float32)
    mine = lax.dynamic_index_in_dim(chip_sum, row, 1, keepdims=False)
    other = lax.dynamic_index_in_dim(chip_sum, 1 - row, 1, keepdims=False)
    return mine, swap(other.astype(jnp.bfloat16), "tp", 2)


def add_rows_to_owner(partial, part_rows):
    mine, arrived = owner_second(*owner_first(partial, part_rows))
    return mine + arrived.astype(jnp.float32)


def exchange(pieces):
    return lax.all_to_all(pieces, "ctx", 0, 0, tiled=True)


def norm_parts(rows):
    row_mean = jnp.mean(rows, axis=-1, keepdims=True)
    centered = rows - row_mean
    variance = jnp.mean(centered * centered, axis=-1, keepdims=True)
    return centered, lax.rsqrt(variance + epsilon)


def norm_backward(normal, scale, gradient, gain):
    scaled = gradient * gain
    return scale * (
        scaled
        - jnp.mean(scaled, axis=-1, keepdims=True)
        - normal * jnp.mean(scaled * normal, axis=-1, keepdims=True)
    )


def fast_body(
    inputs,
    pairing,
    first_gain,
    first_shift,
    query_key_value_weight,
    mix_bias,
    output_projection_weight,
    out_bias,
    second_gain,
    second_shift,
    up_projection_weight,
    up_projection_bias,
    down_projection_weight,
    down_bias,
    cotangent,
):
    low = jnp.bfloat16
    wide = jnp.float32
    seq_count, _, _, part_rows, model_width = inputs.shape
    tp_count = lax.axis_size("tp")
    ctx_count = lax.axis_size("ctx")
    block_rows = part_rows * tp_count
    seq_rows = 2 * block_rows
    row_count = seq_count * seq_rows
    shard = model_width // ctx_count
    dim_local = query_key_value_weight.shape[2]
    hidden_local = up_projection_weight.shape[1]
    groups = ctx_count // seq_count
    width = dim_local // groups
    own_tp = lax.axis_index("tp")

    vectors = [
        first_gain[None],
        first_shift[None],
        out_bias[None],
        second_gain[None],
        second_shift[None],
        down_bias[None],
        up_projection_bias,
        jnp.concatenate([mix_bias[0], mix_bias[1]], axis=1),
    ]
    head, tail = pack(
        jnp.transpose(query_key_value_weight, (1, 0, 2)), output_projection_weight, vectors
    )
    bits = [1 << place for place in range(ctx_count.bit_length() - 1)]
    head_bits, tail_bits = bits[::-1], bits[:1] + bits[:0:-1]
    heads, tails = [((0,), head)], [((0,), tail)]
    row_parts = spread_tp(inputs.reshape(-1, part_rows, model_width))
    cot_part = cotangent.reshape(-1, part_rows, model_width)
    late_shard = pack_late(up_projection_weight, down_projection_weight)
    for step, (head_bit, tail_bit) in enumerate(zip(head_bits, tail_bits)):
        heads = list(spread_step(heads, "ctx", head_bit))
        tails = list(spread_step(tails, "ctx", tail_bit))
        arrivals = (heads[1][1], tails[1][1])
        if step == 0:
            arrivals, row_parts, cot_part = together(arrivals, row_parts, cot_part)
            cot_parts = spread_tp(cot_part)
        elif step == 1:
            arrivals, cot_parts = together(arrivals, cot_parts)
        else:
            arrivals, late_shard = together(arrivals, late_shard)
        heads[1], tails[1] = (heads[1][0], arrivals[0]), (tails[1][0], arrivals[1])
    late_all = lax.all_gather(late_shard, "ctx", axis=0, tiled=True)
    own = jnp.stack([own_tp, lax.axis_index("ctx")]).astype(jnp.int32)
    row_all, first_all, mix_full, out_full, table, projected = first_part(
        own, row_parts, heads, tails, seq_count, groups, 7, mix_bias.shape[2]
    )
    gain_one, bias_down = table[0], table[5]

    sequence = lax.axis_index("ctx") // groups
    pairs = lax.dynamic_index_in_dim(pairing, sequence, 0, keepdims=False)
    blocks = jnp.stack([pairs, 2 * ctx_count - 1 - pairs], axis=-1).reshape(-1)
    places = jnp.arange(2 * ctx_count, dtype=jnp.int32)
    slots = jnp.sum(
        jnp.where(blocks[None, :] == places[:, None], places[None, :], 0), axis=1
    ).astype(jnp.int32)
    qkv = exchange(projected).reshape(ctx_count * seq_rows, 3 * width)
    attended_heads, log_total = attend_forward(slots, qkv, block_rows)
    attended = exchange(attended_heads.reshape(ctx_count, seq_rows, width))
    attended, normed_seqs = together(attended, first_all.reshape(seq_count, 2, block_rows, -1))
    normed_seqs = lax.dynamic_index_in_dim(normed_seqs, own_tp & 1, 1, keepdims=False)
    held = []
    for key in range(0, ctx_count, groups):
        their_seq = (lax.axis_index("ctx") ^ key) // groups
        piece = lax.dynamic_index_in_dim(normed_seqs, their_seq, 0)
        held.append(((key,), swap(piece, "ctx", key) if key else piece))
    branch_sum, branch_other, _ = add_halves(*branch_part(own, attended, out_full))
    hidden, second_all, activated, grad_pre, mine, other, cot_all, early_sums = feed_part(
        own, branch_sum, branch_other, row_all, table, late_all, cot_parts
    )

    grad_pre, *pieces = together(grad_pre, *(piece for _, piece in held))
    held = [(keys, piece) for (keys, _), piece in zip(held, pieces)]
    feed_terms = feed_grads(second_all, grad_pre, cot_all, activated)
    feed_total = lax.psum_scatter(feed_terms, "ctx", scatter_dimension=0, tiled=True)
    held = list(spread_step(held, "ctx", 1))
    grad_sum, grad_other, last_piece = add_halves(mine, other, held[1][1])
    held[1] = (held[1][0], last_piece)
    offsets = held[0][0] + held[1][0]
    sent = jnp.concatenate([held[0][1], held[1][1]], axis=0)
    held = [(offsets, 0, sent), (offsets, 1, swap(sent, "tp", 1))]
    grad_attended, grad_branch, own_grad, hidden_sums = hidden_grad_part(
        own,
        grad_sum,
        grad_other,
        cot_all,
        hidden,
        table,
        out_full,
        (ctx_count, seq_rows, width, part_rows),
    )
    grad_attended, last_piece = together(grad_attended, held[1][2])
    held[1] = (offsets, 1, last_piece)
    grad_heads = exchange(grad_attended).reshape(ctx_count * seq_rows, width)
    grad_qkv = attend_backward(slots, qkv, grad_heads, log_total, block_rows)
    down_sum = add_rows_to_owner(mm(activated, late_all[:, hidden_local:], NT), part_rows)
    own_hidden = lax.dynamic_index_in_dim(
        hidden.reshape(-1, tp_count, part_rows, model_width), own_tp, 1, keepdims=False
    )
    result = (own_hidden + down_sum + bias_down).astype(low)

    mix_mine, mix_other = mix_grads(own, grad_qkv, grad_branch, attended, held)
    grad_mixed, mix_mine, mix_came = together(
        exchange(grad_qkv.reshape(ctx_count, seq_rows, 3 * width)),
        mix_mine,
        swap(mix_other, "ctx", 1),
    )
    mix_mine, mix_other = mix_join(own, mix_mine, mix_came, width)
    mix_came = swap(mix_other, "ctx", 2)
    grad_mixed, mix_mine = together(grad_mixed, mix_mine)
    mine, other, first_sums = first_grads(own, grad_mixed, mix_full, row_all, part_rows)
    gain_shift = first_sums[:2]
    mix_came, came, sums_came = together(
        mix_came, swap(other, "tp", 1), swap(gain_shift, "tp", 1)
    )
    mine, came = owner_second(mine, came)
    gain_shift = gain_shift + sums_came
    gain_shift = gain_shift + swap(gain_shift, "tp", 2)
    for bit in bits[2:]:
        terms = mix_mine.astype(wide) + mix_came.astype(wide)
        terms = terms.reshape((-1, 2) + terms.shape[1:])
        at = jnp.where(lax.axis_index("ctx") & bit != 0, 1, 0)
        mix_mine = lax.dynamic_index_in_dim(terms, at, 1, keepdims=False)
        mix_other = lax.dynamic_index_in_dim(terms, 1 - at, 1, keepdims=False).astype(low)
        mix_came = swap(mix_other, "ctx", bit)
    up_shard, down_shard = feed_finish(feed_total)
    grad_first = mine + came.astype(wide)
    own_rows = inputs.reshape(-1, part_rows, model_width).astype(wide)
    own_centered, own_scale = norm_parts(own_rows)
    grad_inputs = own_grad + norm_backward(
        own_centered * own_scale, own_scale, grad_first, gain_one
    )
    mix_came, up_shard, down_shard, grad_inputs = together(
        mix_came, up_shard, down_shard, grad_inputs
    )
    mix_shard_sum, out_shard_sum = mix_finish(mix_mine[0], mix_came[0], dim_local)

    def by_shard(vector):
        return vector.reshape(ctx_count, -1)

    small = jnp.concatenate(
        [
            by_shard(gain_shift[0]),
            by_shard(gain_shift[1]),
            by_shard(hidden_sums[0]),
            by_shard(hidden_sums[1]),
            by_shard(hidden_sums[2]),
            by_shard(early_sums[1, :model_width]),
            by_shard(early_sums[0, :hidden_local]),
            by_shard(first_sums[2, :dim_local]),
            by_shard(first_sums[2, 2 * dim_local : 3 * dim_local]),
        ],
        axis=1,
    )
    small = jnp.sum(exchange(small), axis=0)
    piece = 0
    sums = []
    for length in [shard] * 6 + [hidden_local // ctx_count] + [dim_local // ctx_count] * 2:
        sums.append(small[piece : piece + length])
        piece += length
    return (
        result.reshape(inputs.shape),
        grad_inputs.reshape(inputs.shape),
        sums[0],
        sums[1],
        jnp.transpose(mix_shard_sum, (1, 0, 2)),
        jnp.stack(sums[7:9])[:, None, :],
        out_shard_sum,
        sums[2],
        sums[3],
        sums[4],
        up_shard,
        sums[6][None, :],
        down_shard,
        sums[5],
    )


def fits_exchange(inputs, query_key_value_weight):
    ctx_count, tp_count = lax.axis_size("ctx"), lax.axis_size("tp")
    seq_count = inputs.shape[0]
    if tp_count != 4 or ctx_count % seq_count or ctx_count & (ctx_count - 1):
        return False
    dim_local = query_key_value_weight.shape[2]
    groups = ctx_count // seq_count
    length = ctx_count * 2 * tp_count * inputs.shape[3]
    shard = inputs.shape[4] // ctx_count
    if groups != 2 or seq_count < 2:
        return False
    return dim_local % (groups * LANES) == 0 and length <= 2048 and shard % LANES == 0


def body(inputs, pairing, first_gain, first_shift, query_key_value_weight, *others):
    chosen = fast_body if fits_exchange(inputs, query_key_value_weight) else general_body
    return chosen(inputs, pairing, first_gain, first_shift, query_key_value_weight, *others)


def solution(mesh):
    return jax.shard_map(
        body,
        mesh=mesh,
        in_specs=(
            P(None, "ctx", None, "tp", None),
            P(),
            P("ctx"),
            P("ctx"),
            P("ctx", None, "tp"),
            P(None, "tp", "ctx"),
            P("tp", "ctx"),
            P("ctx"),
            P("ctx"),
            P("ctx"),
            P("ctx", "tp"),
            P("tp", "ctx"),
            P("tp", "ctx"),
            P("ctx"),
            P(None, "ctx", None, "tp", None),
        ),
        out_specs=(
            P(None, "ctx", None, "tp", None),
            P(None, "ctx", None, "tp", None),
            P("ctx"),
            P("ctx"),
            P("ctx", None, "tp"),
            P(None, "tp", "ctx"),
            P("tp", "ctx"),
            P("ctx"),
            P("ctx"),
            P("ctx"),
            P("ctx", "tp"),
            P("tp", "ctx"),
            P("tp", "ctx"),
            P("ctx"),
        ),
        check_vma=False,
    )
```

```python
import jax
import jax.numpy as jnp
from jax import lax
from jax.experimental import pallas as pl
from jax.experimental.pallas import tpu as pltpu
from jax.sharding import PartitionSpec as P

HD = 64


epsilon = 1e-05


def normalize(token_rows, scaling, offset):
    row_mean = jnp.mean(token_rows, axis=-1, keepdims=True)
    centered = token_rows - row_mean
    variance = jnp.mean(centered * centered, axis=-1, keepdims=True)
    return centered * lax.rsqrt(variance + epsilon) * scaling + offset


def gelu_tanh(values_in):
    return jax.nn.gelu(values_in, approximate=True)


def block_places(pairing_rows, block_rows):
    slot_count = pairing_rows.shape[-1]
    starts = jnp.stack([pairing_rows, 2 * slot_count - 1 - pairing_rows], axis=-1) * block_rows
    within = jnp.arange(block_rows, dtype=jnp.int32)
    return (starts[:, :, :, None] + within).reshape(pairing_rows.shape[0], -1)


def by_head(tensor, head_count):
    seq_span, row_span, model_width = tensor.shape
    return jnp.moveaxis(
        tensor.reshape(seq_span, row_span, head_count, model_width // head_count), 2, 0
    )


def from_head(tensor):
    head_count, seq_span, row_span, head_size = tensor.shape
    return jnp.moveaxis(tensor, 0, 2).reshape(seq_span, row_span, head_count * head_size)


def head_scores(queries, key_vectors, allowed, score_scale):
    scores = (
        jnp.einsum("gqd,gkd->gqk", queries, key_vectors, preferred_element_type=jnp.float32)
        * score_scale
    )
    return jnp.where(allowed, scores, -jnp.inf)


def recompute(queries, key_vectors, value_vectors, grad_out, log_total, allowed, score_scale):
    scores = head_scores(queries, key_vectors, allowed, score_scale)
    probabilities = jnp.exp(scores - log_total[:, :, None])
    grad_probs = jnp.einsum(
        "gqd,gkd->gqk", grad_out, value_vectors, preferred_element_type=jnp.float32
    )
    return (probabilities, grad_probs)


def spread_rows(normed):
    return lax.all_gather(normed, "tp", axis=2, tiled=True)


def collect_rows(partial_terms):
    return lax.psum_scatter(
        partial_terms.astype(jnp.bfloat16), "tp", scatter_dimension=2, tiled=True
    ).astype(jnp.float32)


def spread_grads(gradient_part):
    return lax.all_gather(gradient_part, "tp", axis=2, tiled=True)


def collect_grads(partial_terms):
    return lax.psum_scatter(
        partial_terms.astype(jnp.bfloat16), "tp", scatter_dimension=2, tiled=True
    ).astype(jnp.float32)


def fetch_keys(key_part, value_part):
    return (
        lax.all_gather(key_part, "ctx", axis=1, tiled=True),
        lax.all_gather(value_part, "ctx", axis=1, tiled=True),
    )


def general_body(
    inputs,
    pairing,
    first_gain,
    first_shift,
    query_key_value_weight,
    mix_bias,
    output_projection_weight,
    out_bias,
    second_gain,
    second_shift,
    up_projection_weight,
    up_projection_bias,
    down_projection_weight,
    down_bias,
    cotangent,
):
    seq_count = inputs.shape[0]
    part_rows = inputs.shape[3]
    model_width = inputs.shape[4]
    tp_count = lax.axis_size("tp")
    block_rows = part_rows * tp_count
    local_rows = 2 * block_rows
    ctx_index = lax.axis_index("ctx")
    score_scale = HD ** (-0.5)
    batch_seqs = seq_count
    for candidate in range(seq_count, 0, -1):
        if seq_count % candidate == 0 and candidate * local_rows >= 512:
            batch_seqs = candidate
    groups = seq_count // batch_seqs
    vector_stack = jnp.stack(
        [first_gain, first_shift, out_bias, second_gain, second_shift, down_bias]
    )
    fetched = (
        lax.all_gather(vector_stack, "ctx", axis=1, tiled=True),
        lax.all_gather(query_key_value_weight, "ctx", axis=0, tiled=True),
        lax.all_gather(mix_bias, "ctx", axis=2, tiled=True),
        lax.all_gather(output_projection_weight, "ctx", axis=1, tiled=True),
        lax.all_gather(up_projection_weight, "ctx", axis=0, tiled=True),
        lax.all_gather(up_projection_bias, "ctx", axis=1, tiled=True),
        lax.all_gather(down_projection_weight, "ctx", axis=1, tiled=True),
    )
    vectors_full = fetched[0].astype(jnp.float32)
    dim_local = fetched[2].shape[2]
    head_count = dim_local // HD
    token_rows = inputs.reshape(seq_count, 2, part_rows, model_width).astype(jnp.float32)
    first_norm_output = normalize(token_rows, vectors_full[0], vectors_full[1]).astype(jnp.bfloat16)
    first_all = spread_rows(first_norm_output)
    projected_output = jnp.einsum(
        "sabd,dkc->sabkc", first_all, fetched[1], preferred_element_type=jnp.float32
    )
    bias_full = fetched[2].astype(jnp.float32)
    bias_rows = jnp.stack([bias_full[0, 0], jnp.zeros((dim_local,), jnp.float32), bias_full[1, 0]])
    projected_output = (projected_output + bias_rows).astype(jnp.bfloat16)

    def grouped(tensor):
        return tensor.reshape(groups, batch_seqs, local_rows, tensor.shape[-1])

    def ungrouped(tensor):
        return tensor.reshape(seq_count, 2, block_rows, dim_local)

    query_groups = grouped(projected_output[:, :, :, 0])
    key_groups = grouped(projected_output[:, :, :, 1])
    value_groups = grouped(projected_output[:, :, :, 2])
    pairing_groups = pairing.reshape(groups, batch_seqs, pairing.shape[1])

    def forward_group(unused_carry, inputs_group):
        query_part, key_part, value_part, pairing_rows = inputs_group
        key_all, value_all = fetch_keys(key_part, value_part)
        places = block_places(pairing_rows, block_rows)
        own_places = lax.dynamic_slice_in_dim(places, ctx_index * local_rows, local_rows, 1)
        allowed = own_places[:, :, None] >= places[:, None, :]

        def head_forward(operands):
            queries, key_vectors, value_vectors = operands
            scores = head_scores(queries, key_vectors, allowed, score_scale)
            row_max = jnp.max(scores, axis=-1, keepdims=True)
            exponent = jnp.exp(scores - row_max)
            row_total = jnp.sum(exponent, axis=-1, keepdims=True)
            weights_low = (exponent / row_total).astype(jnp.bfloat16)
            attention_result = jnp.einsum(
                "gqk,gkd->gqd", weights_low, value_vectors, preferred_element_type=jnp.float32
            )
            return (attention_result.astype(jnp.bfloat16), (row_max + jnp.log(row_total))[:, :, 0])

        outputs, log_totals = lax.map(
            head_forward,
            (
                by_head(query_part, head_count),
                by_head(key_all, head_count),
                by_head(value_all, head_count),
            ),
        )
        return (unused_carry, (from_head(outputs), log_totals))

    unused_state, (output_groups, log_groups) = lax.scan(
        forward_group, None, (query_groups, key_groups, value_groups, pairing_groups)
    )
    attention_result = ungrouped(output_groups)
    residual_branch = collect_rows(
        jnp.einsum(
            "sabc,cd->sabd", attention_result, fetched[3], preferred_element_type=jnp.float32
        )
    )
    hidden = token_rows + residual_branch + vectors_full[2]
    second_norm_output = normalize(hidden, vectors_full[3], vectors_full[4]).astype(jnp.bfloat16)
    second_all = spread_rows(second_norm_output)
    before_activation = jnp.einsum(
        "sabd,df->sabf", second_all, fetched[4], preferred_element_type=jnp.float32
    ) + fetched[5][0].astype(jnp.float32)
    activation_rows = gelu_tanh(before_activation).astype(jnp.bfloat16)
    residual_branch_two = collect_rows(
        jnp.einsum("sabf,fd->sabd", activation_rows, fetched[6], preferred_element_type=jnp.float32)
    )
    result = (hidden + residual_branch_two + vectors_full[5]).astype(jnp.bfloat16)
    vectors_back = fetched[0].astype(jnp.float32)
    grad_result_low = cotangent.reshape(seq_count, 2, part_rows, model_width)
    grad_result = grad_result_low.astype(jnp.float32)
    grad_down_bias = jnp.sum(grad_result, axis=(0, 1, 2))
    grad_branch_two = spread_grads(grad_result_low)
    grad_down = jnp.einsum(
        "sabf,sabd->fd", activation_rows, grad_branch_two, preferred_element_type=jnp.float32
    )
    grad_activated = jnp.einsum(
        "sabd,fd->sabf", grad_branch_two, fetched[6], preferred_element_type=jnp.float32
    )
    gelu_pull = jax.vjp(gelu_tanh, before_activation)[1]
    grad_pre = gelu_pull(grad_activated)[0].astype(jnp.bfloat16)
    grad_up_bias = jnp.sum(grad_pre, axis=(0, 1, 2), dtype=jnp.float32)
    grad_up = jnp.einsum("sabd,sabf->df", second_all, grad_pre, preferred_element_type=jnp.float32)
    grad_second = collect_grads(
        jnp.einsum("sabf,df->sabd", grad_pre, fetched[4], preferred_element_type=jnp.float32)
    )
    second_pull = jax.vjp(normalize, hidden, vectors_back[3], vectors_back[4])[1]
    grad_hidden_norm, grad_second_gain, grad_second_shift = second_pull(grad_second)
    grad_hidden = grad_result + grad_hidden_norm
    grad_out_bias = jnp.sum(grad_hidden, axis=(0, 1, 2))
    grad_branch = spread_grads(grad_hidden.astype(jnp.bfloat16))
    grad_out_weight = jnp.einsum(
        "sabc,sabd->cd", attention_result, grad_branch, preferred_element_type=jnp.float32
    )
    grad_attended = jnp.einsum(
        "sabd,cd->sabc", grad_branch, fetched[3], preferred_element_type=jnp.float32
    ).astype(jnp.bfloat16)
    grad_groups = grouped(grad_attended)

    def backward_group(unused_carry, inputs_group):
        query_part, key_part, value_part, grad_part, log_part, pairing_rows = inputs_group
        key_all, value_all = fetch_keys(key_part, value_part)
        places = block_places(pairing_rows, block_rows)
        own_places = lax.dynamic_slice_in_dim(places, ctx_index * local_rows, local_rows, 1)
        allowed = own_places[:, :, None] >= places[:, None, :]

        def joint_pass(operands):
            queries, key_vectors, value_vectors, grad_out, log_total = operands
            probabilities, grad_probs = recompute(
                queries, key_vectors, value_vectors, grad_out, log_total, allowed, score_scale
            )
            row_delta = jnp.sum(probabilities * grad_probs, axis=-1, keepdims=True)
            grad_scores = (probabilities * (grad_probs - row_delta)).astype(jnp.bfloat16)
            grad_query = (
                jnp.einsum(
                    "gqk,gkd->gqd", grad_scores, key_vectors, preferred_element_type=jnp.float32
                )
                * score_scale
            )
            grad_key = (
                jnp.einsum("gqk,gqd->gkd", grad_scores, queries, preferred_element_type=jnp.float32)
                * score_scale
            )
            grad_value = jnp.einsum(
                "gqk,gqd->gkd",
                probabilities.astype(jnp.bfloat16),
                grad_out,
                preferred_element_type=jnp.float32,
            )
            return (grad_query, grad_key, grad_value)

        grad_queries, grad_keys, grad_values = lax.map(
            joint_pass,
            (
                by_head(query_part, head_count),
                by_head(key_all, head_count),
                by_head(value_all, head_count),
                by_head(grad_part, head_count),
                log_part,
            ),
        )
        grad_key_rows, grad_value_rows = (
            lax.psum_scatter(from_head(grad_keys), "ctx", scatter_dimension=1, tiled=True),
            lax.psum_scatter(from_head(grad_values), "ctx", scatter_dimension=1, tiled=True),
        )
        return (
            unused_carry,
            (
                from_head(grad_queries).astype(jnp.bfloat16),
                grad_key_rows.astype(jnp.bfloat16),
                grad_value_rows.astype(jnp.bfloat16),
            ),
        )

    unused_back, (query_grads, key_grads, value_grads) = lax.scan(
        backward_group,
        None,
        (query_groups, key_groups, value_groups, grad_groups, log_groups, pairing_groups),
    )
    grad_query_rows = ungrouped(query_grads)
    grad_value_rows = ungrouped(value_grads)
    grad_projected = jnp.stack([grad_query_rows, ungrouped(key_grads), grad_value_rows], axis=3)
    grad_mix_bias = jnp.stack(
        [
            jnp.sum(grad_query_rows, axis=(0, 1, 2), dtype=jnp.float32),
            jnp.sum(grad_value_rows, axis=(0, 1, 2), dtype=jnp.float32),
        ]
    )[:, None, :]
    grad_mix = jnp.einsum(
        "sabd,sabkc->dkc", first_all, grad_projected, preferred_element_type=jnp.float32
    )
    grad_first = collect_grads(
        jnp.einsum(
            "sabkc,dkc->sabd", grad_projected, fetched[1], preferred_element_type=jnp.float32
        )
    )
    first_pull = jax.vjp(normalize, token_rows, vectors_back[0], vectors_back[1])[1]
    grad_token_norm, grad_first_gain, grad_first_shift = first_pull(grad_first)
    grad_inputs = (grad_hidden + grad_token_norm).reshape(inputs.shape)
    vector_grads = jnp.stack(
        [
            grad_first_gain,
            grad_first_shift,
            grad_out_bias,
            grad_second_gain,
            grad_second_shift,
            grad_down_bias,
        ]
    )
    shards = (
        lax.psum_scatter(vector_grads, "ctx", scatter_dimension=1, tiled=True),
        lax.psum_scatter(grad_mix, "ctx", scatter_dimension=0, tiled=True),
        lax.psum_scatter(grad_mix_bias, "ctx", scatter_dimension=2, tiled=True),
        lax.psum_scatter(grad_out_weight, "ctx", scatter_dimension=1, tiled=True),
        lax.psum_scatter(grad_up, "ctx", scatter_dimension=0, tiled=True),
        lax.psum_scatter(grad_up_bias[None, :], "ctx", scatter_dimension=1, tiled=True),
        lax.psum_scatter(grad_down, "ctx", scatter_dimension=1, tiled=True),
    )
    vector_shard = lax.psum(shards[0], "tp")
    return (
        result.reshape(inputs.shape),
        grad_inputs,
        vector_shard[0],
        vector_shard[1],
        shards[1],
        shards[2],
        shards[3],
        vector_shard[2],
        vector_shard[3],
        vector_shard[4],
        shards[4],
        shards[5],
        shards[6],
        vector_shard[5],
    )


LANES = 128
CHUNK = 256
NT = (((1,), (1,)), ((), ()))
NN = (((1,), (0,)), ((), ()))
TN = (((0,), (0,)), ((), ()))


def mm(left, right, dims):
    return lax.dot_general(left, right, dims, preferred_element_type=jnp.float32)


def causal(span, chunk):
    key_place = lax.broadcasted_iota(jnp.int32, (span, chunk), 0)
    query_place = lax.broadcasted_iota(jnp.int32, (span, chunk), 1) + (span - chunk)
    return key_place <= query_place


def to_places(slots_ref, source, target, block_rows):
    for block in range(target.shape[0] // block_rows):
        start = pl.multiple_of(slots_ref[block] * block_rows, block_rows)
        target[pl.ds(block * block_rows, block_rows), :] = source[pl.ds(start, block_rows), :]


def to_slots(slots_ref, values, target, first_block, block_rows):
    for block in range(values.shape[0] // block_rows):
        start = pl.multiple_of(slots_ref[first_block + block] * block_rows, block_rows)
        target[pl.ds(start, block_rows), :] = values[block * block_rows : (block + 1) * block_rows]


def forward_kernel(block_rows, slots_ref, qkv_ref, out_ref, log_ref, rows):
    length, wide = rows.shape
    width = wide // 3
    chunk = min(CHUNK, length)
    to_places(slots_ref, qkv_ref, rows, block_rows)
    log_ref[...] = jnp.zeros(log_ref.shape, jnp.float32)
    for part in range(length // chunk):
        low, high = part * chunk, (part + 1) * chunk
        allowed = causal(high, chunk)
        columns = []
        for head in range(width // HD):
            lane = head * HD
            queries = rows[low:high, lane : lane + HD]
            keys = rows[0:high, width + lane : width + lane + HD]
            values = rows[0:high, 2 * width + lane : 2 * width + lane + HD]
            scores = jnp.where(allowed, mm(keys, queries, NT) * HD ** (-0.5), -1e30)
            top = jnp.max(scores, axis=0, keepdims=True)
            exponent = jnp.exp(scores - top)
            total = jnp.sum(exponent, axis=0, keepdims=True)
            weights = (exponent * (1.0 / total)).astype(jnp.bfloat16)
            columns.append(mm(values, weights, TN))
            log_ref[head : head + 1, low:high] = top + jnp.log(total)
        attended = jnp.concatenate(columns, axis=0).T.astype(jnp.bfloat16)
        to_slots(slots_ref, attended, out_ref, low // block_rows, block_rows)


def backward_kernel(
    block_rows, slots_ref, qkv_ref, grad_ref, log_ref, out_ref, rows, grads, key_sum, value_sum
):
    length, wide = rows.shape
    width = wide // 3
    chunk = min(CHUNK, length)
    scale = HD ** (-0.5)
    to_places(slots_ref, qkv_ref, rows, block_rows)
    to_places(slots_ref, grad_ref, grads, block_rows)
    key_sum[...] = jnp.zeros(key_sum.shape, jnp.float32)
    value_sum[...] = jnp.zeros(value_sum.shape, jnp.float32)
    for part in range(length // chunk):
        low, high = part * chunk, (part + 1) * chunk
        allowed = causal(high, chunk)
        query_columns, key_parts, value_parts = [], [], []
        for head in range(width // HD):
            lane = head * HD
            queries = rows[low:high, lane : lane + HD]
            keys = rows[0:high, width + lane : width + lane + HD]
            values = rows[0:high, 2 * width + lane : 2 * width + lane + HD]
            grad_out = grads[low:high, lane : lane + HD]
            scores = jnp.where(allowed, mm(keys, queries, NT) * scale, -1e30)
            probs = jnp.exp(scores - log_ref[head : head + 1, low:high])
            grad_probs = mm(values, grad_out, NT)
            delta = jnp.sum(probs * grad_probs, axis=0, keepdims=True)
            grad_scores = (probs * (grad_probs - delta)).astype(jnp.bfloat16)
            value_parts.append(mm(probs.astype(jnp.bfloat16), grad_out, NN))
            key_parts.append(mm(grad_scores, queries, NN))
            query_columns.append(mm(keys, grad_scores, TN))
        key_sum[0:high, :] += jnp.concatenate(key_parts, axis=1)
        value_sum[0:high, :] += jnp.concatenate(value_parts, axis=1)
        grad_query = (jnp.concatenate(query_columns, axis=0).T * scale).astype(jnp.bfloat16)
        to_slots(
            slots_ref, grad_query, out_ref.at[:, 0:width], low // block_rows, block_rows
        )
    to_slots(
        slots_ref,
        (key_sum[...] * scale).astype(jnp.bfloat16),
        out_ref.at[:, width : 2 * width],
        0,
        block_rows,
    )
    to_slots(
        slots_ref,
        value_sum[...].astype(jnp.bfloat16),
        out_ref.at[:, 2 * width : 3 * width],
        0,
        block_rows,
    )


def whole_shape(shape):
    return pl.BlockSpec(shape, lambda step: (0,) * len(shape))


def whole_block(array):
    return whole_shape(array.shape)


SMEM_SPEC = pl.BlockSpec(memory_space=pltpu.SMEM)
KERNEL_PARAMS = pltpu.CompilerParams(vmem_limit_bytes=60 * 1024 * 1024)


def attend_forward(slots, qkv, block_rows):
    length, wide = qkv.shape
    width = wide // 3
    area = length * length * width
    return pl.pallas_call(
        lambda *refs: forward_kernel(block_rows, *refs),
        out_shape=(
            jax.ShapeDtypeStruct((length, width), jnp.bfloat16),
            jax.ShapeDtypeStruct((8, length), jnp.float32),
        ),
        grid=(1,),
        in_specs=[SMEM_SPEC, whole_block(qkv)],
        out_specs=(whole_shape((length, width)), whole_shape((8, length))),
        scratch_shapes=[pltpu.VMEM((length, wide), jnp.bfloat16)],
        compiler_params=KERNEL_PARAMS,
        cost_estimate=pl.CostEstimate(
            flops=3 * area, bytes_accessed=8 * length * width, transcendentals=area // HD
        ),
        name="attend_forward",
    )(slots, qkv)


def attend_backward(slots, qkv, grad_out, log_total, block_rows):
    length, wide = qkv.shape
    width = wide // 3
    area = length * length * width
    return pl.pallas_call(
        lambda *refs: backward_kernel(block_rows, *refs),
        out_shape=jax.ShapeDtypeStruct((length, wide), jnp.bfloat16),
        grid=(1,),
        in_specs=[SMEM_SPEC, whole_block(qkv), whole_block(grad_out), whole_block(log_total)],
        out_specs=whole_shape((length, wide)),
        scratch_shapes=[
            pltpu.VMEM((length, wide), jnp.bfloat16),
            pltpu.VMEM((length, width), jnp.bfloat16),
            pltpu.VMEM((length, width), jnp.float32),
            pltpu.VMEM((length, width), jnp.float32),
        ],
        compiler_params=KERNEL_PARAMS,
        cost_estimate=pl.CostEstimate(
            flops=7 * area, bytes_accessed=14 * length * width, transcendentals=area // HD
        ),
        name="attend_backward",
    )(slots, qkv, grad_out, log_total)


def swap(values, axis, bit):
    count = lax.axis_size(axis)
    return lax.ppermute(values, axis, [(i, i ^ bit) for i in range(count)])


def together(*groups):
    return lax.optimization_barrier(groups)


def spread_step(held, axis, bit):
    keys = tuple(key for offsets, _ in held for key in offsets)
    arrays = [array for _, array in held]
    sent = arrays[0] if len(arrays) == 1 else jnp.concatenate(arrays, axis=0)
    return (keys, sent), (tuple(key ^ bit for key in keys), swap(sent, axis, bit))


def pack_kernel(pieces, mix_ref, out_weight_ref, *refs):
    vectors, (head_ref, tail_ref) = refs[:-2], refs[-2:]
    half = tail_ref.shape[1]
    parts, _, part_width = mix_ref.shape
    mix_width = parts * part_width
    shard = 2 * half
    for target, first in ((head_ref, 0), (tail_ref, half)):
        for part in range(parts):
            target[0, 0:half, part * part_width : (part + 1) * part_width] = mix_ref[
                part, first : first + half, :
            ]
        for piece in range(pieces):
            target[0, 0:half, mix_width + piece * shard : mix_width + (piece + 1) * shard] = (
                out_weight_ref[piece * shard + first : piece * shard + first + half, :]
            )
    extra = head_ref.shape[1] - half
    head_ref[0, half:, :] = jnp.zeros((extra, head_ref.shape[2]), jnp.bfloat16)
    for number, vector in enumerate(vectors):
        head_ref[0, half : half + 1, number * shard : number * shard + vector.shape[1]] = vector[...]


def late_kernel(up_ref, down_ref, late_ref):
    hidden_local = up_ref.shape[1]
    late_ref[:, 0:hidden_local] = up_ref[...]
    late_ref[:, hidden_local:] = down_ref[...].T


def pack_late(up_shard, down_shard):
    shard, hidden_local = up_shard.shape
    return pl.pallas_call(
        late_kernel,
        out_shape=jax.ShapeDtypeStruct((shard, 2 * hidden_local), jnp.bfloat16),
        grid=(1,),
        in_specs=[whole_block(up_shard), whole_block(down_shard)],
        out_specs=whole_shape((shard, 2 * hidden_local)),
        compiler_params=KERNEL_PARAMS,
        name="pack_late",
    )(up_shard, down_shard)


def pack(mix_shard, out_shard, vectors):
    parts, shard, part_width = mix_shard.shape
    pieces = out_shard.shape[0] // shard
    total = parts * part_width + out_shard.shape[0]
    return pl.pallas_call(
        lambda *refs: pack_kernel(pieces, *refs),
        out_shape=(
            jax.ShapeDtypeStruct((1, shard // 2 + 16, total), jnp.bfloat16),
            jax.ShapeDtypeStruct((1, shard // 2, total), jnp.bfloat16),
        ),
        grid=(1,),
        in_specs=[whole_block(array) for array in (mix_shard, out_shard, *vectors)],
        out_specs=(
            whole_shape((1, shard // 2 + 16, total)),
            whole_shape((1, shard // 2, total)),
        ),
        compiler_params=KERNEL_PARAMS,
        name="pack",
    )(mix_shard, out_shard, *vectors)


def first_kernel(head_keys, tail_keys, sizes, own_ref, *refs):
    groups, width, vector_count, bias_width = sizes
    tp_count = 4
    parts, refs = refs[:tp_count], refs[tp_count:]
    heads, refs = refs[: len(head_keys)], refs[len(head_keys) :]
    tails, refs = refs[: len(tail_keys)], refs[len(tail_keys) :]
    rows_ref, first_ref, weight_ref, out_weight_ref, table_ref, send_ref, gathered = refs
    own_tp, own_ctx = own_ref[0], own_ref[1]
    mix_width = weight_ref.shape[1]
    half = tails[0].shape[1]
    shard = 2 * half

    def put_out(piece, place, owner, first):
        columns = pl.ds(pl.multiple_of(owner * shard, shard), shard)
        for number in range(out_weight_ref.shape[0] // shard):
            low = mix_width + number * shard
            out_weight_ref[number * shard + first : number * shard + first + half, columns] = piece[
                place, 0:half, low : low + shard
            ]

    for keys, piece in zip(head_keys, heads):
        for place, key in enumerate(keys):
            owner = own_ctx ^ key
            rows = pl.ds(pl.multiple_of(owner * shard, shard), half)
            weight_ref[rows, :] = piece[place, 0:half, 0:mix_width]
            put_out(piece, place, owner, 0)
            extra = piece[place, half:, :].astype(jnp.float32)
            gathered[pl.ds(owner, 1), :] = extra[0:1, :]
    for keys, piece in zip(tail_keys, tails):
        for place, key in enumerate(keys):
            owner = own_ctx ^ key
            rows = pl.ds(pl.multiple_of(owner * shard + half, half), half)
            weight_ref[rows, :] = piece[place, :, 0:mix_width]
            put_out(piece, place, owner, half)
    count = gathered.shape[0]
    vectors = gathered[...]
    table_ref[...] = jnp.zeros(table_ref.shape, jnp.float32)
    for number in range(vector_count):
        lanes = slice(number * shard, (number + 1) * shard)
        for owner in range(count):
            table_ref[number : number + 1, owner * shard : (owner + 1) * shard] = vectors[
                owner : owner + 1, lanes
            ]
    bias_parts = []
    for number in range(2):
        low = vector_count * shard + number * bias_width
        bias_parts.append(
            jnp.concatenate(
                [vectors[owner : owner + 1, low : low + bias_width] for owner in range(count)],
                axis=1,
            )
        )
    bias = jnp.concatenate([bias_parts[0], jnp.zeros_like(bias_parts[0]), bias_parts[1]], axis=1)
    piece_count, part_rows, _ = parts[0].shape
    block_rows = tp_count * part_rows
    for key in range(tp_count):
        for piece in range(piece_count):
            row = pl.multiple_of(piece * block_rows + (own_tp ^ key) * part_rows, part_rows)
            rows_ref[pl.ds(row, part_rows), :] = parts[key][piece]
    seq_rows = send_ref.shape[1]
    dim_local = mix_width // 3
    gain, shift = table_ref[0:1, :], table_ref[1:2, :]
    for seq in range(rows_ref.shape[0] // seq_rows):
        rows = slice(seq * seq_rows, (seq + 1) * seq_rows)
        centered, scale = norm_parts(rows_ref[rows, :].astype(jnp.float32))
        normed = (centered * scale * gain + shift).astype(jnp.bfloat16)
        first_ref[rows, :] = normed
        projected = (mm(normed, weight_ref[...], NN) + bias).astype(jnp.bfloat16)
        for group in range(groups):
            for number in range(3):
                low = number * dim_local + group * width
                send_ref[seq * groups + group, :, number * width : (number + 1) * width] = (
                    projected[:, low : low + width]
                )


def first_part(own, parts, heads, tails, seq_count, groups, vector_count, bias_width):
    piece_count, part_rows, model_width = parts[0].shape
    row_count = piece_count * part_rows * 4
    count = seq_count * groups
    mix_width = 3 * model_width // 4
    head_keys, head_arrays = zip(*heads)
    tail_keys, tail_arrays = zip(*tails)
    seq_rows = row_count // seq_count
    width = mix_width // (3 * groups)
    low = jnp.bfloat16
    shapes = (
        ((row_count, model_width), low),
        ((row_count, model_width), low),
        ((model_width, mix_width), low),
        ((head_arrays[0].shape[2] - mix_width, model_width), low),
        ((8, model_width), jnp.float32),
        ((count, seq_rows, 3 * width), low),
    )
    return pl.pallas_call(
        lambda *refs: first_kernel(
            head_keys, tail_keys, (groups, width, vector_count, bias_width), *refs
        ),
        out_shape=tuple(jax.ShapeDtypeStruct(*shape) for shape in shapes),
        grid=(1,),
        in_specs=[SMEM_SPEC]
        + [whole_block(array) for array in (*parts, *head_arrays, *tail_arrays)],
        out_specs=tuple(whole_shape(shape) for shape, _ in shapes),
        scratch_shapes=[pltpu.VMEM((count, head_arrays[0].shape[2]), jnp.float32)],
        compiler_params=KERNEL_PARAMS,
        cost_estimate=pl.CostEstimate(
            flops=2 * row_count * model_width * mix_width,
            bytes_accessed=8 * 1024 * 1024,
            transcendentals=0,
        ),
        name="first_part",
    )(own, *parts, *head_arrays, *tail_arrays)


def feed_grads_kernel(second_ref, grad_pre_ref, cot_ref, activated_ref, out_ref):
    half = grad_pre_ref.shape[1]
    out_ref[:, 0:half] = mm(second_ref[...], grad_pre_ref[...], TN).astype(jnp.bfloat16)
    out_ref[:, half:] = mm(cot_ref[...], activated_ref[...], TN).astype(jnp.bfloat16)


def feed_grads(second_all, grad_pre, cot_all, activated):
    row_count, model_width = second_all.shape
    hidden_local = grad_pre.shape[1]
    step = min(256, model_width)
    column = pl.BlockSpec((row_count, step), lambda i: (0, i))
    fixed = pl.BlockSpec((row_count, hidden_local), lambda i: (0, 0))
    return pl.pallas_call(
        feed_grads_kernel,
        grid=(model_width // step,),
        out_shape=jax.ShapeDtypeStruct((model_width, 2 * hidden_local), jnp.bfloat16),
        in_specs=[column, fixed, column, fixed],
        out_specs=pl.BlockSpec((step, 2 * hidden_local), lambda i: (i, 0)),
        compiler_params=KERNEL_PARAMS,
        cost_estimate=pl.CostEstimate(
            flops=4 * row_count * model_width * hidden_local,
            bytes_accessed=8 * 1024 * 1024,
            transcendentals=0,
        ),
        name="feed_grads",
    )(second_all, grad_pre, cot_all, activated)


def feed_finish_kernel(sum_ref, up_ref, down_ref):
    half = up_ref.shape[1]
    up_ref[...] = sum_ref[:, 0:half].astype(jnp.float32)
    down_ref[...] = sum_ref[:, half:].astype(jnp.float32).T


def feed_finish(total):
    shard, twice = total.shape
    shapes = ((shard, twice // 2), (twice // 2, shard))
    return pl.pallas_call(
        feed_finish_kernel,
        grid=(1,),
        out_shape=tuple(jax.ShapeDtypeStruct(shape, jnp.float32) for shape in shapes),
        in_specs=[whole_block(total)],
        out_specs=tuple(whole_shape(shape) for shape in shapes),
        compiler_params=KERNEL_PARAMS,
        name="feed_finish",
    )(total)


def mix_finish_kernel(mine_ref, came_ref, out_mine_ref, out_came_ref, mix_ref, out_ref):
    total = mine_ref[...].astype(jnp.float32) + came_ref[...].astype(jnp.float32)
    parts, _, part_width = mix_ref.shape
    for part in range(parts):
        mix_ref[part] = total[:, part * part_width : (part + 1) * part_width]
    out_ref[...] = (out_mine_ref[...].astype(jnp.float32) + out_came_ref[...].astype(jnp.float32)).T


def mix_finish(mine, came, out_mine, out_came):
    shard, dim_local = out_came.shape
    shapes = ((3, shard, dim_local), (dim_local, shard))
    arrays = (mine, came, out_mine, out_came)
    return pl.pallas_call(
        mix_finish_kernel,
        grid=(1,),
        out_shape=tuple(jax.ShapeDtypeStruct(shape, jnp.float32) for shape in shapes),
        in_specs=[whole_block(array) for array in arrays],
        out_specs=tuple(whole_shape(shape) for shape in shapes),
        compiler_params=KERNEL_PARAMS,
        name="mix_finish",
    )(*arrays)


def small_kernel(own_ref, first_ref, hidden_ref, early_ref, out_ref):
    devices, _, shard = out_ref.shape
    tp_count = 4
    own_tp = own_ref[0]
    share = 1.0 / tp_count
    rows = [
        first_ref[0:1, :],
        first_ref[1:2, :],
        hidden_ref[0:1, :] * share,
        hidden_ref[1:2, :] * share,
        hidden_ref[2:3, :] * share,
        early_ref[1:2, :] * share,
    ]
    out_ref[...] = jnp.zeros(out_ref.shape, jnp.float32)
    piece = shard // tp_count
    count = devices // tp_count
    for owner in range(count):
        for place in range(tp_count):
            index = owner * tp_count + place
            for number, row in enumerate(rows):
                out_ref[index, number : number + 1, :] = row[:, owner * shard : (owner + 1) * shard]
            own = jnp.where(own_tp == place, 1.0, 0.0)
            out_ref[index, len(rows) : len(rows) + 1, :] = (
                early_ref[0:1, owner * shard : (owner + 1) * shard] * own
            )
            for number, part in enumerate((0, 2)):
                low = part * count * piece + owner * piece
                out_ref[
                    index, len(rows) + 1 : len(rows) + 2, number * piece : (number + 1) * piece
                ] = first_ref[2:3, low : low + piece] * own


def small_pack(own, first_sums, hidden_sums, early_sums, count):
    shape = (4 * count, 8, first_sums.shape[1] // count)
    arrays = (first_sums, hidden_sums, early_sums)
    return pl.pallas_call(
        small_kernel,
        grid=(1,),
        out_shape=jax.ShapeDtypeStruct(shape, jnp.float32),
        in_specs=[SMEM_SPEC] + [whole_block(array) for array in arrays],
        out_specs=whole_shape(shape),
        compiler_params=KERNEL_PARAMS,
        name="small_pack",
    )(own, *arrays)


def halve(mine, came, bit):
    terms = mine.astype(jnp.float32) + came.astype(jnp.float32)
    terms = terms.reshape((-1, 2) + terms.shape[1:])
    at = jnp.where(lax.axis_index("ctx") & bit != 0, 1, 0)
    mine = lax.dynamic_index_in_dim(terms, at, 1, keepdims=False)
    other = lax.dynamic_index_in_dim(terms, 1 - at, 1, keepdims=False)
    return mine, swap(other.astype(jnp.bfloat16), "ctx", bit)


MLP_ROWS = 128


def branch_kernel(own_ref, attended_ref, weight_ref, mine_ref, other_ref):
    core = own_ref[0] & 1
    count, seq_rows, width = attended_ref.shape
    seqs = mine_ref.shape[0] // seq_rows
    groups = count // (2 * seqs)
    for half, out_ref in enumerate((mine_ref, other_ref)):
        for seq in range(seqs):
            first = ((core ^ half) * seqs + seq) * groups
            total = mm(attended_ref[first], weight_ref[0:width, :], NN)
            for group in range(1, groups):
                total += mm(
                    attended_ref[first + group],
                    weight_ref[group * width : (group + 1) * width, :],
                    NN,
                )
            out_ref[seq * seq_rows : (seq + 1) * seq_rows, :] = total.astype(jnp.bfloat16)


def branch_part(own, attended, out_full):
    count, seq_rows, width = attended.shape
    rows = count * seq_rows * width // out_full.shape[0]
    shape = (rows // 2, out_full.shape[1])
    return pl.pallas_call(
        branch_kernel,
        grid=(1,),
        out_shape=(jax.ShapeDtypeStruct(shape, jnp.bfloat16),) * 2,
        in_specs=[SMEM_SPEC, whole_block(attended), whole_block(out_full)],
        out_specs=(whole_shape(shape),) * 2,
        compiler_params=KERNEL_PARAMS,
        name="branch_part",
    )(own, attended, out_full)


def hidden_grad_kernel(
    own_ref,
    sum_ref,
    other_ref,
    cot_ref,
    hidden_ref,
    table_ref,
    weight_ref,
    send_ref,
    branch_ref,
    own_grad_ref,
    sums_ref,
    rows_ref,
):
    own_tp = own_ref[0]
    core = own_tp & 1
    count, seq_rows, width = send_ref.shape
    _, part_rows, model_width = own_grad_ref.shape
    seqs = sum_ref.shape[0] // seq_rows
    groups = count // (2 * seqs)
    block_rows = seq_rows // 2
    gain = table_ref[3:4, :]
    sums = [jnp.zeros((1, model_width), jnp.float32) for _ in range(3)]
    for half, grad_ref in enumerate((sum_ref, other_ref)):
        for chunk in range(seqs):
            seq = (core ^ half) * seqs + chunk
            rows = pl.ds(pl.multiple_of(seq * seq_rows, seq_rows), seq_rows)
            grad = grad_ref[chunk * seq_rows : (chunk + 1) * seq_rows, :].astype(jnp.float32)
            centered, scale = norm_parts(hidden_ref[rows, :])
            normal = centered * scale
            total = cot_ref[rows, :].astype(jnp.float32) + norm_backward(normal, scale, grad, gain)
            low = total.astype(jnp.bfloat16)
            branch_ref[rows, :] = low
            rows_ref[...] = total
            for block in range(2):
                first = pl.multiple_of(block * block_rows + own_tp * part_rows, part_rows)
                own_grad_ref[seq * 2 + block] = rows_ref[pl.ds(first, part_rows), :]
            attended = mm(low, weight_ref[...], NT).astype(jnp.bfloat16)
            for group in range(groups):
                send_ref[seq * groups + group] = attended[:, group * width : (group + 1) * width]
            sums[0] += jnp.sum(total, axis=0, keepdims=True)
            sums[1] += jnp.sum(grad * normal, axis=0, keepdims=True)
            sums[2] += jnp.sum(grad, axis=0, keepdims=True)
    sums_ref[...] = jnp.zeros(sums_ref.shape, jnp.float32)
    for number, total in enumerate(sums):
        sums_ref[number : number + 1, :] = total


def hidden_grad_part(own, grad_sum, grad_other, cot_all, hidden, table, out_full, sizes):
    count, seq_rows, width, part_rows = sizes
    row_count, model_width = hidden.shape
    low = jnp.bfloat16
    shapes = (
        ((count, seq_rows, width), low),
        ((row_count, model_width), low),
        ((2 * row_count // seq_rows, part_rows, model_width), jnp.float32),
        ((8, model_width), jnp.float32),
    )
    arrays = (grad_sum, grad_other, cot_all, hidden, table, out_full)
    return pl.pallas_call(
        hidden_grad_kernel,
        grid=(1,),
        out_shape=tuple(jax.ShapeDtypeStruct(*shape) for shape in shapes),
        in_specs=[SMEM_SPEC] + [whole_block(array) for array in arrays],
        out_specs=tuple(whole_shape(shape) for shape, _ in shapes),
        scratch_shapes=[pltpu.VMEM((seq_rows, model_width), jnp.float32)],
        compiler_params=KERNEL_PARAMS,
        name="hidden_grad_part",
    )(own, *arrays)


def place_mixed(source_ref, target, width):
    count, seq_rows, total = source_ref.shape
    parts = total // width
    groups = target.shape[1] // total
    for index in range(count):
        seq, group = index // groups, index % groups
        for part in range(parts):
            low = (part * groups + group) * width
            target[seq * seq_rows : (seq + 1) * seq_rows, low : low + width] = source_ref[
                index, :, part * width : (part + 1) * width
            ]


def halved_grads_kernel(own_ref, left_ref, right_ref, mine_ref, other_ref, *placed):
    if placed:
        place_mixed(right_ref, placed[0], right_ref.shape[2])
        right_ref = placed[0]
    half, shard, _ = mine_ref.shape
    for flipped, out_ref in ((1, other_ref), (0, mine_ref)):
        for index in range(half):
            owner = 2 * index + ((own_ref[1] & 1) ^ flipped)
            columns = pl.ds(pl.multiple_of(owner * shard, shard), shard)
            out_ref[index] = mm(left_ref[:, columns], right_ref[...], TN).astype(jnp.bfloat16)


def halved_grads(own, left, right, count):
    row_count, model_width = left.shape
    width = right.size // row_count
    shape = (count // 2, model_width // count, width)
    placed = [pltpu.VMEM((row_count, width), jnp.bfloat16)] if len(right.shape) == 3 else []
    return pl.pallas_call(
        halved_grads_kernel,
        grid=(1,),
        out_shape=(jax.ShapeDtypeStruct(shape, jnp.bfloat16),) * 2,
        in_specs=[SMEM_SPEC, whole_block(left), whole_block(right)],
        out_specs=(whole_shape(shape),) * 2,
        scratch_shapes=placed,
        compiler_params=KERNEL_PARAMS,
        cost_estimate=pl.CostEstimate(
            flops=2 * model_width * row_count * width,
            bytes_accessed=2 * (left.size + right.size + model_width * width),
            transcendentals=0,
        ),
        name="halved_grads",
    )(own, left, right)


def mix_grads_kernel(keys, own_ref, grad_ref, *refs):
    pieces, (mine_ref, other_ref, normed) = refs[:-3], refs[-3:]
    own_core, own_ctx = own_ref[0] & 1, own_ref[1]
    half, shard, _ = mine_ref.shape
    for (piece_keys, core_key), piece in zip(keys, pieces):
        part_rows = piece.shape[1]
        for place, key in enumerate(piece_keys):
            start = (own_ctx ^ key) * 2 * part_rows + (own_core ^ core_key) * part_rows
            normed[pl.ds(pl.multiple_of(start, part_rows), part_rows), :] = piece[place]
    for flipped, out_ref in enumerate((mine_ref, other_ref)):
        for index in range(half):
            owner = 2 * index + ((own_ctx & 1) ^ flipped)
            columns = pl.ds(pl.multiple_of(owner * shard, shard), shard)
            out_ref[index] = mm(normed[:, columns], grad_ref[...], TN).astype(jnp.bfloat16)


def mix_grads(own, grad_qkv, count, held):
    keys = [(offsets, core_key) for offsets, core_key, _ in held]
    pieces = [piece for _, _, piece in held]
    length, width = grad_qkv.shape
    model_width = pieces[0].shape[2]
    shape = (count // 2, model_width // count, width)
    low = jnp.bfloat16
    arrays = (grad_qkv, *pieces)
    return pl.pallas_call(
        lambda *refs: mix_grads_kernel(keys, *refs),
        grid=(1,),
        out_shape=(jax.ShapeDtypeStruct(shape, low),) * 2,
        in_specs=[SMEM_SPEC] + [whole_block(array) for array in arrays],
        out_specs=(whole_shape(shape),) * 2,
        scratch_shapes=[pltpu.VMEM((length, model_width), low)],
        compiler_params=KERNEL_PARAMS,
        cost_estimate=pl.CostEstimate(
            flops=2 * model_width * length * width,
            bytes_accessed=8 * 1024 * 1024,
            transcendentals=0,
        ),
        name="mix_grads",
    )(own, *arrays)


def mix_join_kernel(own_ref, mine_ref, came_ref, keep_ref, send_ref):
    own_ctx = own_ref[1]
    is_first = (own_ctx & 1) == 0
    own_bit = (own_ctx >> 1) & 1
    width = mine_ref.shape[2] // 3
    for flipped, out_ref in enumerate((keep_ref, send_ref)):
        for index in range(out_ref.shape[0]):
            source = 2 * index + (own_bit ^ flipped)
            mine, came = mine_ref[source], came_ref[source]
            first = jnp.where(is_first, mine, came)
            second = jnp.where(is_first, came, mine)
            for part in range(3):
                lanes = slice(part * width, (part + 1) * width)
                low = 2 * part * width
                out_ref[index, :, low : low + width] = first[:, lanes]
                out_ref[index, :, low + width : low + 2 * width] = second[:, lanes]


def mix_join(own, mine, came):
    half, shard, total = mine.shape
    shape = (half // 2, shard, 2 * total)
    return pl.pallas_call(
        mix_join_kernel,
        grid=(1,),
        out_shape=(jax.ShapeDtypeStruct(shape, jnp.bfloat16),) * 2,
        in_specs=[SMEM_SPEC, whole_block(mine), whole_block(came)],
        out_specs=(whole_shape(shape),) * 2,
        compiler_params=KERNEL_PARAMS,
        name="mix_join",
    )(own, mine, came)


def first_grad_kernel(own_ref, mixed_ref, weight_ref, x_ref, mine_ref, other_ref, sums_ref, *refs):
    mixed, rows_ref = refs
    own_tp = own_ref[0]
    core = own_tp & 1
    count, seq_rows, total = mixed_ref.shape
    groups = mixed.shape[1] // total
    place_mixed(mixed_ref, mixed, total // 3)
    part_rows = mine_ref.shape[2]
    model_width = x_ref.shape[1]
    block_rows = seq_rows // 2
    sums = [jnp.zeros((1, model_width), jnp.float32) for _ in range(2)]
    for seq in range(count // groups):
        rows = slice(seq * seq_rows, (seq + 1) * seq_rows)
        partial = mm(mixed[rows, :], weight_ref[...], NT)
        rows_ref[...] = partial.astype(jnp.bfloat16)
        for block in range(2):
            for row in range(2):
                for flipped, out_ref in enumerate((mine_ref, other_ref)):
                    owner = 2 * row + (core ^ flipped)
                    first = pl.multiple_of(block * block_rows + owner * part_rows, part_rows)
                    out_ref[2 * seq + block, row] = rows_ref[pl.ds(first, part_rows), :]
        centered, scale = norm_parts(x_ref[rows, :].astype(jnp.float32))
        sums[0] += jnp.sum(partial * (centered * scale), axis=0, keepdims=True)
        sums[1] += jnp.sum(partial, axis=0, keepdims=True)
    sums_ref[...] = jnp.zeros(sums_ref.shape, jnp.float32)
    for number, value in enumerate(sums):
        sums_ref[number : number + 1, :] = value
    mixed_ref_sum = jnp.sum(mixed[...].astype(jnp.float32), axis=0, keepdims=True)
    sums_ref[2:3, 0 : mixed.shape[1]] = mixed_ref_sum


def first_grads(own, grad_mixed, mix_full, x_all, part_rows):
    count, seq_rows, total = grad_mixed.shape
    row_count, model_width = x_all.shape
    shape = (2 * row_count // seq_rows, 2, part_rows, model_width)
    low = jnp.bfloat16
    arrays = (grad_mixed, mix_full, x_all)
    return pl.pallas_call(
        first_grad_kernel,
        grid=(1,),
        out_shape=(
            jax.ShapeDtypeStruct(shape, low),
            jax.ShapeDtypeStruct(shape, low),
            jax.ShapeDtypeStruct((8, model_width), jnp.float32),
        ),
        in_specs=[SMEM_SPEC] + [whole_block(array) for array in arrays],
        out_specs=(whole_shape(shape), whole_shape(shape), whole_shape((8, model_width))),
        scratch_shapes=[
            pltpu.VMEM((row_count, mix_full.shape[1]), low),
            pltpu.VMEM((seq_rows, model_width), low),
        ],
        compiler_params=KERNEL_PARAMS,
        name="first_grads",
    )(own, *arrays)


def gelu_both(value):
    root = (2.0 / jnp.pi) ** 0.5
    square = value * value
    inner = jnp.tanh(root * value * (1.0 + 0.044715 * square))
    slope = 0.5 * (1.0 + inner) + 0.5 * value * (1.0 - inner * inner) * root * (
        1.0 + 3.0 * 0.044715 * square
    )
    return 0.5 * value * (1.0 + inner), slope


def feed_kernel(part_count, own_ref, sum_ref, other_ref, x_ref, table_ref, late_ref, *refs):
    cot_parts, refs = refs[:part_count], refs[part_count:]
    (
        hidden_ref,
        second_ref,
        activated_ref,
        grad_pre_ref,
        mine_ref,
        partner_ref,
        cot_ref,
        sums_ref,
    ) = refs
    own_tp = own_ref[0]
    core = own_tp & 1
    hidden_local = activated_ref.shape[1]
    blocks, part_rows, _ = cot_parts[0].shape
    for key, part in enumerate(cot_parts):
        for block in range(blocks):
            row = block * part_count * part_rows + (own_tp ^ key) * part_rows
            cot_ref[pl.ds(pl.multiple_of(row, part_rows), part_rows), :] = part[block]
    half_rows = sum_ref.shape[0]
    up_sum = jnp.zeros((1, hidden_local), jnp.float32)
    cot_sum = jnp.zeros((1, cot_ref.shape[1]), jnp.float32)
    for half, (branch_ref, out_ref) in enumerate(((sum_ref, mine_ref), (other_ref, partner_ref))):
        for chunk in range(half_rows // MLP_ROWS):
            inside = slice(chunk * MLP_ROWS, (chunk + 1) * MLP_ROWS)
            start = (core ^ half) * half_rows + chunk * MLP_ROWS
            rows = pl.ds(pl.multiple_of(start, MLP_ROWS), MLP_ROWS)
            hidden = (
                x_ref[rows, :].astype(jnp.float32)
                + branch_ref[inside, :].astype(jnp.float32)
                + table_ref[2:3, :]
            )
            hidden_ref[rows, :] = hidden
            centered, scale = norm_parts(hidden)
            second = (centered * scale * table_ref[3:4, :] + table_ref[4:5, :]).astype(jnp.bfloat16)
            second_ref[rows, :] = second
            activated, slope = gelu_both(mm(second, late_ref[:, 0:hidden_local], NN) + table_ref[6:7, :])
            activated_ref[rows, :] = activated.astype(jnp.bfloat16)
            cot = cot_ref[rows, :]
            grad_pre = (mm(cot, late_ref[:, hidden_local:], NN) * slope).astype(jnp.bfloat16)
            grad_pre_ref[rows, :] = grad_pre
            out_ref[inside, :] = mm(grad_pre, late_ref[:, 0:hidden_local], NT).astype(jnp.bfloat16)
            up_sum += jnp.sum(grad_pre.astype(jnp.float32), axis=0, keepdims=True)
            cot_sum += jnp.sum(cot.astype(jnp.float32), axis=0, keepdims=True)
    sums_ref[...] = jnp.zeros(sums_ref.shape, jnp.float32)
    sums_ref[0:1, 0:hidden_local] = up_sum
    sums_ref[1:2, 0 : cot_ref.shape[1]] = cot_sum


def feed_part(own, branch_sum, branch_other, x_all, table, late_all, cot_parts):
    row_count, model_width = x_all.shape
    hidden_local = late_all.shape[1] // 2
    low = jnp.bfloat16
    shapes = (
        ((row_count, model_width), jnp.float32),
        ((row_count, model_width), low),
        ((row_count, hidden_local), low),
        ((row_count, hidden_local), low),
        ((row_count // 2, model_width), low),
        ((row_count // 2, model_width), low),
        ((row_count, model_width), low),
        ((8, max(model_width, hidden_local)), jnp.float32),
    )
    arrays = (branch_sum, branch_other, x_all, table, late_all, *cot_parts)
    return pl.pallas_call(
        lambda *refs: feed_kernel(len(cot_parts), *refs),
        grid=(1,),
        out_shape=tuple(jax.ShapeDtypeStruct(*shape) for shape in shapes),
        in_specs=[SMEM_SPEC] + [whole_block(array) for array in arrays],
        out_specs=tuple(whole_shape(shape) for shape, _ in shapes),
        compiler_params=KERNEL_PARAMS,
        cost_estimate=pl.CostEstimate(
            flops=6 * row_count * model_width * hidden_local,
            bytes_accessed=16 * 1024 * 1024,
            transcendentals=row_count * hidden_local,
        ),
        name="feed_part",
    )(own, *arrays)


def spread_tp(part):
    return [part] + [swap(part, "tp", key) for key in (1, 2, 3)]


def add_halves(mine, other, beside=None):
    arrived = swap(other, "tp", 1)
    chip_sum = (mine.astype(jnp.float32) + arrived.astype(jnp.float32)).astype(jnp.bfloat16)
    arrived = swap(chip_sum, "tp", 2)
    if beside is not None:
        arrived, beside = together(arrived, beside)
    whole = (chip_sum.astype(jnp.float32) + arrived.astype(jnp.float32)).astype(jnp.bfloat16)
    return whole, swap(whole, "tp", 1), beside


def owner_first(partial, part_rows):
    core = lax.axis_index("tp") & 1
    parts = partial.astype(jnp.bfloat16).reshape(-1, 2, 2, part_rows, partial.shape[-1])
    mine = lax.dynamic_index_in_dim(parts, core, 2, keepdims=False)
    return mine, swap(lax.dynamic_index_in_dim(parts, 1 - core, 2, keepdims=False), "tp", 1)


def owner_second(mine, arrived):
    row = lax.axis_index("tp") >> 1
    chip_sum = mine.astype(jnp.float32) + arrived.astype(jnp.float32)
    mine = lax.dynamic_index_in_dim(chip_sum, row, 1, keepdims=False)
    other = lax.dynamic_index_in_dim(chip_sum, 1 - row, 1, keepdims=False)
    return mine, swap(other.astype(jnp.bfloat16), "tp", 2)


def add_rows_to_owner(partial, part_rows):
    mine, arrived = owner_second(*owner_first(partial, part_rows))
    return mine + arrived.astype(jnp.float32)


def exchange(pieces):
    return lax.all_to_all(pieces, "ctx", 0, 0, tiled=True)


def norm_parts(rows):
    row_mean = jnp.mean(rows, axis=-1, keepdims=True)
    centered = rows - row_mean
    variance = jnp.mean(centered * centered, axis=-1, keepdims=True)
    return centered, lax.rsqrt(variance + epsilon)


def norm_backward(normal, scale, gradient, gain):
    scaled = gradient * gain
    return scale * (
        scaled
        - jnp.mean(scaled, axis=-1, keepdims=True)
        - normal * jnp.mean(scaled * normal, axis=-1, keepdims=True)
    )


def fast_body(
    inputs,
    pairing,
    first_gain,
    first_shift,
    query_key_value_weight,
    mix_bias,
    output_projection_weight,
    out_bias,
    second_gain,
    second_shift,
    up_projection_weight,
    up_projection_bias,
    down_projection_weight,
    down_bias,
    cotangent,
):
    low = jnp.bfloat16
    wide = jnp.float32
    seq_count, _, _, part_rows, model_width = inputs.shape
    tp_count = lax.axis_size("tp")
    ctx_count = lax.axis_size("ctx")
    block_rows = part_rows * tp_count
    seq_rows = 2 * block_rows
    row_count = seq_count * seq_rows
    shard = model_width // ctx_count
    dim_local = query_key_value_weight.shape[2]
    hidden_local = up_projection_weight.shape[1]
    groups = ctx_count // seq_count
    width = dim_local // groups
    own_tp = lax.axis_index("tp")

    vectors = [
        first_gain[None],
        first_shift[None],
        out_bias[None],
        second_gain[None],
        second_shift[None],
        down_bias[None],
        up_projection_bias,
        jnp.concatenate([mix_bias[0], mix_bias[1]], axis=1),
    ]
    head, tail = pack(
        jnp.transpose(query_key_value_weight, (1, 0, 2)), output_projection_weight, vectors
    )
    bits = [1 << place for place in range(ctx_count.bit_length() - 1)]
    head_bits, tail_bits = bits[::-1], bits[:1] + bits[:0:-1]
    heads, tails = [((0,), head)], [((0,), tail)]
    row_parts = spread_tp(inputs.reshape(-1, part_rows, model_width))
    cot_part = cotangent.reshape(-1, part_rows, model_width)
    late_shard = pack_late(up_projection_weight, down_projection_weight)
    for step, (head_bit, tail_bit) in enumerate(zip(head_bits, tail_bits)):
        heads = list(spread_step(heads, "ctx", head_bit))
        tails = list(spread_step(tails, "ctx", tail_bit))
        arrivals = (heads[1][1], tails[1][1])
        if step == 0:
            arrivals, row_parts, cot_part = together(arrivals, row_parts, cot_part)
            cot_parts = spread_tp(cot_part)
        elif step == 1:
            arrivals, cot_parts = together(arrivals, cot_parts)
        else:
            arrivals, late_shard = together(arrivals, late_shard)
        heads[1], tails[1] = (heads[1][0], arrivals[0]), (tails[1][0], arrivals[1])
    late_all = lax.all_gather(late_shard, "ctx", axis=0, tiled=True)
    own = jnp.stack([own_tp, lax.axis_index("ctx")]).astype(jnp.int32)
    row_all, first_all, mix_full, out_full, table, projected = first_part(
        own, row_parts, heads, tails, seq_count, groups, 7, mix_bias.shape[2]
    )
    gain_one, bias_down = table[0], table[5]

    sequence = lax.axis_index("ctx") // groups
    pairs = lax.dynamic_index_in_dim(pairing, sequence, 0, keepdims=False)
    blocks = jnp.stack([pairs, 2 * ctx_count - 1 - pairs], axis=-1).reshape(-1)
    places = jnp.arange(2 * ctx_count, dtype=jnp.int32)
    slots = jnp.sum(
        jnp.where(blocks[None, :] == places[:, None], places[None, :], 0), axis=1
    ).astype(jnp.int32)
    qkv = exchange(projected).reshape(ctx_count * seq_rows, 3 * width)
    attended_heads, log_total = attend_forward(slots, qkv, block_rows)
    attended = exchange(attended_heads.reshape(ctx_count, seq_rows, width))
    attended, normed_seqs = together(attended, first_all.reshape(seq_count, 2, block_rows, -1))
    normed_seqs = lax.dynamic_index_in_dim(normed_seqs, own_tp & 1, 1, keepdims=False)
    held = []
    for key in range(0, ctx_count, groups):
        their_seq = (lax.axis_index("ctx") ^ key) // groups
        piece = lax.dynamic_index_in_dim(normed_seqs, their_seq, 0)
        held.append(((key,), swap(piece, "ctx", key) if key else piece))
    branch_sum, branch_other, _ = add_halves(*branch_part(own, attended, out_full))
    hidden, second_all, activated, grad_pre, mine, other, cot_all, early_sums = feed_part(
        own, branch_sum, branch_other, row_all, table, late_all, cot_parts
    )

    grad_pre, *pieces = together(grad_pre, *(piece for _, piece in held))
    held = [(keys, piece) for (keys, _), piece in zip(held, pieces)]
    feed_terms = feed_grads(second_all, grad_pre, cot_all, activated)
    feed_total = lax.psum_scatter(feed_terms, "ctx", scatter_dimension=0, tiled=True)
    held = list(spread_step(held, "ctx", 1))
    grad_sum, grad_other, last_piece = add_halves(mine, other, held[1][1])
    held[1] = (held[1][0], last_piece)
    offsets = held[0][0] + held[1][0]
    sent = jnp.concatenate([held[0][1], held[1][1]], axis=0)
    held = [(offsets, 0, sent), (offsets, 1, swap(sent, "tp", 1))]
    grad_attended, grad_branch, own_grad, hidden_sums = hidden_grad_part(
        own,
        grad_sum,
        grad_other,
        cot_all,
        hidden,
        table,
        out_full,
        (ctx_count, seq_rows, width, part_rows),
    )
    grad_attended, last_piece = together(grad_attended, held[1][2])
    held[1] = (offsets, 1, last_piece)
    out_mine, out_other = halved_grads(own, grad_branch, attended, ctx_count)
    grad_heads, out_came = together(exchange(grad_attended), swap(out_other, "ctx", 1))
    out_mine, out_came = halve(out_mine, out_came, 2)
    grad_heads = grad_heads.reshape(ctx_count * seq_rows, width)
    grad_qkv = attend_backward(slots, qkv, grad_heads, log_total, block_rows)
    grad_qkv, out_came = together(grad_qkv, out_came)
    for bit in bits[2:]:
        out_mine, out_came = halve(out_mine, out_came, bit)
    down_sum = add_rows_to_owner(mm(activated, late_all[:, hidden_local:], NT), part_rows)
    own_hidden = lax.dynamic_index_in_dim(
        hidden.reshape(-1, tp_count, part_rows, model_width), own_tp, 1, keepdims=False
    )
    result = (own_hidden + down_sum + bias_down).astype(low)

    mix_mine, mix_other = mix_grads(own, grad_qkv, ctx_count, held)
    grad_mixed, mix_mine, mix_came, out_came, result = together(
        exchange(grad_qkv.reshape(ctx_count, seq_rows, 3 * width)),
        mix_mine,
        swap(mix_other, "ctx", 1),
        out_came,
        result,
    )
    mix_mine, mix_other = mix_join(own, mix_mine, mix_came)
    mix_came = swap(mix_other, "ctx", 2)
    grad_mixed, mix_mine = together(grad_mixed, mix_mine)
    mine, other, first_sums = first_grads(own, grad_mixed, mix_full, row_all, part_rows)
    small = lax.all_to_all(
        small_pack(own, first_sums, hidden_sums, early_sums, ctx_count),
        ("ctx", "tp"),
        0,
        0,
        tiled=True,
    )
    mix_came, came = together(mix_came, swap(other, "tp", 1))
    mine, came = owner_second(mine, came)
    for bit in bits[2:]:
        mix_mine, mix_came = halve(mix_mine, mix_came, bit)
    up_shard, down_shard = feed_finish(feed_total)
    came, up_shard, down_shard = together(came, up_shard, down_shard)
    grad_first = mine + came.astype(wide)
    own_rows = inputs.reshape(-1, part_rows, model_width).astype(wide)
    own_centered, own_scale = norm_parts(own_rows)
    grad_inputs = own_grad + norm_backward(
        own_centered * own_scale, own_scale, grad_first, gain_one
    )
    mix_came, grad_inputs, small = together(mix_came, grad_inputs, small)
    mix_shard_sum, out_shard_sum = mix_finish(mix_mine[0], mix_came[0], out_mine[0], out_came[0])
    sums = jnp.sum(small, axis=0)
    piece = dim_local // ctx_count
    return (
        result.reshape(inputs.shape),
        grad_inputs.reshape(inputs.shape),
        sums[0],
        sums[1],
        jnp.transpose(mix_shard_sum, (1, 0, 2)),
        jnp.stack([sums[7, :piece], sums[7, piece : 2 * piece]])[:, None, :],
        out_shard_sum,
        sums[2],
        sums[3],
        sums[4],
        up_shard,
        sums[6][None, :],
        down_shard,
        sums[5],
    )


def fits_exchange(inputs, query_key_value_weight, up_projection_weight):
    ctx_count, tp_count = lax.axis_size("ctx"), lax.axis_size("tp")
    seq_count = inputs.shape[0]
    if tp_count != 4 or ctx_count % seq_count or ctx_count & (ctx_count - 1):
        return False
    dim_local = query_key_value_weight.shape[2]
    groups = ctx_count // seq_count
    length = ctx_count * 2 * tp_count * inputs.shape[3]
    shard = inputs.shape[4] // ctx_count
    if groups != 2 or seq_count < 2 or dim_local * 4 != inputs.shape[4]:
        return False
    if up_projection_weight.shape[1] != inputs.shape[4]:
        return False
    return dim_local % (groups * LANES) == 0 and length <= 2048 and shard % LANES == 0


def body(inputs, pairing, first_gain, first_shift, query_key_value_weight, *others):
    fits = fits_exchange(inputs, query_key_value_weight, others[5])
    chosen = fast_body if fits else general_body
    return chosen(inputs, pairing, first_gain, first_shift, query_key_value_weight, *others)


def solution(mesh):
    return jax.shard_map(
        body,
        mesh=mesh,
        in_specs=(
            P(None, "ctx", None, "tp", None),
            P(),
            P("ctx"),
            P("ctx"),
            P("ctx", None, "tp"),
            P(None, "tp", "ctx"),
            P("tp", "ctx"),
            P("ctx"),
            P("ctx"),
            P("ctx"),
            P("ctx", "tp"),
            P("tp", "ctx"),
            P("tp", "ctx"),
            P("ctx"),
            P(None, "ctx", None, "tp", None),
        ),
        out_specs=(
            P(None, "ctx", None, "tp", None),
            P(None, "ctx", None, "tp", None),
            P("ctx"),
            P("ctx"),
            P("ctx", None, "tp"),
            P(None, "tp", "ctx"),
            P("tp", "ctx"),
            P("ctx"),
            P("ctx"),
            P("ctx"),
            P("ctx", "tp"),
            P("tp", "ctx"),
            P("tp", "ctx"),
            P("ctx"),
        ),
        check_vma=False,
    )
```

```python
import jax
import jax.numpy as jnp
from jax import lax
from jax.experimental import pallas as pl
from jax.experimental.pallas import tpu as pltpu
from jax.sharding import PartitionSpec as P

HD = 64


epsilon = 1e-05


def normalize(token_rows, scaling, offset):
    row_mean = jnp.mean(token_rows, axis=-1, keepdims=True)
    centered = token_rows - row_mean
    variance = jnp.mean(centered * centered, axis=-1, keepdims=True)
    return centered * lax.rsqrt(variance + epsilon) * scaling + offset


def gelu_tanh(values_in):
    return jax.nn.gelu(values_in, approximate=True)


def block_places(pairing_rows, block_rows):
    slot_count = pairing_rows.shape[-1]
    starts = jnp.stack([pairing_rows, 2 * slot_count - 1 - pairing_rows], axis=-1) * block_rows
    within = jnp.arange(block_rows, dtype=jnp.int32)
    return (starts[:, :, :, None] + within).reshape(pairing_rows.shape[0], -1)


def by_head(tensor, head_count):
    seq_span, row_span, model_width = tensor.shape
    return jnp.moveaxis(
        tensor.reshape(seq_span, row_span, head_count, model_width // head_count), 2, 0
    )


def from_head(tensor):
    head_count, seq_span, row_span, head_size = tensor.shape
    return jnp.moveaxis(tensor, 0, 2).reshape(seq_span, row_span, head_count * head_size)


def head_scores(queries, key_vectors, allowed, score_scale):
    scores = (
        jnp.einsum("gqd,gkd->gqk", queries, key_vectors, preferred_element_type=jnp.float32)
        * score_scale
    )
    return jnp.where(allowed, scores, -jnp.inf)


def recompute(queries, key_vectors, value_vectors, grad_out, log_total, allowed, score_scale):
    scores = head_scores(queries, key_vectors, allowed, score_scale)
    probabilities = jnp.exp(scores - log_total[:, :, None])
    grad_probs = jnp.einsum(
        "gqd,gkd->gqk", grad_out, value_vectors, preferred_element_type=jnp.float32
    )
    return (probabilities, grad_probs)


def spread_rows(normed):
    return lax.all_gather(normed, "tp", axis=2, tiled=True)


def collect_rows(partial_terms):
    return lax.psum_scatter(
        partial_terms.astype(jnp.bfloat16), "tp", scatter_dimension=2, tiled=True
    ).astype(jnp.float32)


def spread_grads(gradient_part):
    return lax.all_gather(gradient_part, "tp", axis=2, tiled=True)


def collect_grads(partial_terms):
    return lax.psum_scatter(
        partial_terms.astype(jnp.bfloat16), "tp", scatter_dimension=2, tiled=True
    ).astype(jnp.float32)


def fetch_keys(key_part, value_part):
    return (
        lax.all_gather(key_part, "ctx", axis=1, tiled=True),
        lax.all_gather(value_part, "ctx", axis=1, tiled=True),
    )


def general_body(
    inputs,
    pairing,
    first_gain,
    first_shift,
    query_key_value_weight,
    mix_bias,
    output_projection_weight,
    out_bias,
    second_gain,
    second_shift,
    up_projection_weight,
    up_projection_bias,
    down_projection_weight,
    down_bias,
    cotangent,
):
    seq_count = inputs.shape[0]
    part_rows = inputs.shape[3]
    model_width = inputs.shape[4]
    tp_count = lax.axis_size("tp")
    block_rows = part_rows * tp_count
    local_rows = 2 * block_rows
    ctx_index = lax.axis_index("ctx")
    score_scale = HD ** (-0.5)
    batch_seqs = seq_count
    for candidate in range(seq_count, 0, -1):
        if seq_count % candidate == 0 and candidate * local_rows >= 512:
            batch_seqs = candidate
    groups = seq_count // batch_seqs
    vector_stack = jnp.stack(
        [first_gain, first_shift, out_bias, second_gain, second_shift, down_bias]
    )
    fetched = (
        lax.all_gather(vector_stack, "ctx", axis=1, tiled=True),
        lax.all_gather(query_key_value_weight, "ctx", axis=0, tiled=True),
        lax.all_gather(mix_bias, "ctx", axis=2, tiled=True),
        lax.all_gather(output_projection_weight, "ctx", axis=1, tiled=True),
        lax.all_gather(up_projection_weight, "ctx", axis=0, tiled=True),
        lax.all_gather(up_projection_bias, "ctx", axis=1, tiled=True),
        lax.all_gather(down_projection_weight, "ctx", axis=1, tiled=True),
    )
    vectors_full = fetched[0].astype(jnp.float32)
    dim_local = fetched[2].shape[2]
    head_count = dim_local // HD
    token_rows = inputs.reshape(seq_count, 2, part_rows, model_width).astype(jnp.float32)
    first_norm_output = normalize(token_rows, vectors_full[0], vectors_full[1]).astype(jnp.bfloat16)
    first_all = spread_rows(first_norm_output)
    projected_output = jnp.einsum(
        "sabd,dkc->sabkc", first_all, fetched[1], preferred_element_type=jnp.float32
    )
    bias_full = fetched[2].astype(jnp.float32)
    bias_rows = jnp.stack([bias_full[0, 0], jnp.zeros((dim_local,), jnp.float32), bias_full[1, 0]])
    projected_output = (projected_output + bias_rows).astype(jnp.bfloat16)

    def grouped(tensor):
        return tensor.reshape(groups, batch_seqs, local_rows, tensor.shape[-1])

    def ungrouped(tensor):
        return tensor.reshape(seq_count, 2, block_rows, dim_local)

    query_groups = grouped(projected_output[:, :, :, 0])
    key_groups = grouped(projected_output[:, :, :, 1])
    value_groups = grouped(projected_output[:, :, :, 2])
    pairing_groups = pairing.reshape(groups, batch_seqs, pairing.shape[1])

    def forward_group(unused_carry, inputs_group):
        query_part, key_part, value_part, pairing_rows = inputs_group
        key_all, value_all = fetch_keys(key_part, value_part)
        places = block_places(pairing_rows, block_rows)
        own_places = lax.dynamic_slice_in_dim(places, ctx_index * local_rows, local_rows, 1)
        allowed = own_places[:, :, None] >= places[:, None, :]

        def head_forward(operands):
            queries, key_vectors, value_vectors = operands
            scores = head_scores(queries, key_vectors, allowed, score_scale)
            row_max = jnp.max(scores, axis=-1, keepdims=True)
            exponent = jnp.exp(scores - row_max)
            row_total = jnp.sum(exponent, axis=-1, keepdims=True)
            weights_low = (exponent / row_total).astype(jnp.bfloat16)
            attention_result = jnp.einsum(
                "gqk,gkd->gqd", weights_low, value_vectors, preferred_element_type=jnp.float32
            )
            return (attention_result.astype(jnp.bfloat16), (row_max + jnp.log(row_total))[:, :, 0])

        outputs, log_totals = lax.map(
            head_forward,
            (
                by_head(query_part, head_count),
                by_head(key_all, head_count),
                by_head(value_all, head_count),
            ),
        )
        return (unused_carry, (from_head(outputs), log_totals))

    unused_state, (output_groups, log_groups) = lax.scan(
        forward_group, None, (query_groups, key_groups, value_groups, pairing_groups)
    )
    attention_result = ungrouped(output_groups)
    residual_branch = collect_rows(
        jnp.einsum(
            "sabc,cd->sabd", attention_result, fetched[3], preferred_element_type=jnp.float32
        )
    )
    hidden = token_rows + residual_branch + vectors_full[2]
    second_norm_output = normalize(hidden, vectors_full[3], vectors_full[4]).astype(jnp.bfloat16)
    second_all = spread_rows(second_norm_output)
    before_activation = jnp.einsum(
        "sabd,df->sabf", second_all, fetched[4], preferred_element_type=jnp.float32
    ) + fetched[5][0].astype(jnp.float32)
    activation_rows = gelu_tanh(before_activation).astype(jnp.bfloat16)
    residual_branch_two = collect_rows(
        jnp.einsum("sabf,fd->sabd", activation_rows, fetched[6], preferred_element_type=jnp.float32)
    )
    result = (hidden + residual_branch_two + vectors_full[5]).astype(jnp.bfloat16)
    vectors_back = fetched[0].astype(jnp.float32)
    grad_result_low = cotangent.reshape(seq_count, 2, part_rows, model_width)
    grad_result = grad_result_low.astype(jnp.float32)
    grad_down_bias = jnp.sum(grad_result, axis=(0, 1, 2))
    grad_branch_two = spread_grads(grad_result_low)
    grad_down = jnp.einsum(
        "sabf,sabd->fd", activation_rows, grad_branch_two, preferred_element_type=jnp.float32
    )
    grad_activated = jnp.einsum(
        "sabd,fd->sabf", grad_branch_two, fetched[6], preferred_element_type=jnp.float32
    )
    gelu_pull = jax.vjp(gelu_tanh, before_activation)[1]
    grad_pre = gelu_pull(grad_activated)[0].astype(jnp.bfloat16)
    grad_up_bias = jnp.sum(grad_pre, axis=(0, 1, 2), dtype=jnp.float32)
    grad_up = jnp.einsum("sabd,sabf->df", second_all, grad_pre, preferred_element_type=jnp.float32)
    grad_second = collect_grads(
        jnp.einsum("sabf,df->sabd", grad_pre, fetched[4], preferred_element_type=jnp.float32)
    )
    second_pull = jax.vjp(normalize, hidden, vectors_back[3], vectors_back[4])[1]
    grad_hidden_norm, grad_second_gain, grad_second_shift = second_pull(grad_second)
    grad_hidden = grad_result + grad_hidden_norm
    grad_out_bias = jnp.sum(grad_hidden, axis=(0, 1, 2))
    grad_branch = spread_grads(grad_hidden.astype(jnp.bfloat16))
    grad_out_weight = jnp.einsum(
        "sabc,sabd->cd", attention_result, grad_branch, preferred_element_type=jnp.float32
    )
    grad_attended = jnp.einsum(
        "sabd,cd->sabc", grad_branch, fetched[3], preferred_element_type=jnp.float32
    ).astype(jnp.bfloat16)
    grad_groups = grouped(grad_attended)

    def backward_group(unused_carry, inputs_group):
        query_part, key_part, value_part, grad_part, log_part, pairing_rows = inputs_group
        key_all, value_all = fetch_keys(key_part, value_part)
        places = block_places(pairing_rows, block_rows)
        own_places = lax.dynamic_slice_in_dim(places, ctx_index * local_rows, local_rows, 1)
        allowed = own_places[:, :, None] >= places[:, None, :]

        def joint_pass(operands):
            queries, key_vectors, value_vectors, grad_out, log_total = operands
            probabilities, grad_probs = recompute(
                queries, key_vectors, value_vectors, grad_out, log_total, allowed, score_scale
            )
            row_delta = jnp.sum(probabilities * grad_probs, axis=-1, keepdims=True)
            grad_scores = (probabilities * (grad_probs - row_delta)).astype(jnp.bfloat16)
            grad_query = (
                jnp.einsum(
                    "gqk,gkd->gqd", grad_scores, key_vectors, preferred_element_type=jnp.float32
                )
                * score_scale
            )
            grad_key = (
                jnp.einsum("gqk,gqd->gkd", grad_scores, queries, preferred_element_type=jnp.float32)
                * score_scale
            )
            grad_value = jnp.einsum(
                "gqk,gqd->gkd",
                probabilities.astype(jnp.bfloat16),
                grad_out,
                preferred_element_type=jnp.float32,
            )
            return (grad_query, grad_key, grad_value)

        grad_queries, grad_keys, grad_values = lax.map(
            joint_pass,
            (
                by_head(query_part, head_count),
                by_head(key_all, head_count),
                by_head(value_all, head_count),
                by_head(grad_part, head_count),
                log_part,
            ),
        )
        grad_key_rows, grad_value_rows = (
            lax.psum_scatter(from_head(grad_keys), "ctx", scatter_dimension=1, tiled=True),
            lax.psum_scatter(from_head(grad_values), "ctx", scatter_dimension=1, tiled=True),
        )
        return (
            unused_carry,
            (
                from_head(grad_queries).astype(jnp.bfloat16),
                grad_key_rows.astype(jnp.bfloat16),
                grad_value_rows.astype(jnp.bfloat16),
            ),
        )

    unused_back, (query_grads, key_grads, value_grads) = lax.scan(
        backward_group,
        None,
        (query_groups, key_groups, value_groups, grad_groups, log_groups, pairing_groups),
    )
    grad_query_rows = ungrouped(query_grads)
    grad_value_rows = ungrouped(value_grads)
    grad_projected = jnp.stack([grad_query_rows, ungrouped(key_grads), grad_value_rows], axis=3)
    grad_mix_bias = jnp.stack(
        [
            jnp.sum(grad_query_rows, axis=(0, 1, 2), dtype=jnp.float32),
            jnp.sum(grad_value_rows, axis=(0, 1, 2), dtype=jnp.float32),
        ]
    )[:, None, :]
    grad_mix = jnp.einsum(
        "sabd,sabkc->dkc", first_all, grad_projected, preferred_element_type=jnp.float32
    )
    grad_first = collect_grads(
        jnp.einsum(
            "sabkc,dkc->sabd", grad_projected, fetched[1], preferred_element_type=jnp.float32
        )
    )
    first_pull = jax.vjp(normalize, token_rows, vectors_back[0], vectors_back[1])[1]
    grad_token_norm, grad_first_gain, grad_first_shift = first_pull(grad_first)
    grad_inputs = (grad_hidden + grad_token_norm).reshape(inputs.shape)
    vector_grads = jnp.stack(
        [
            grad_first_gain,
            grad_first_shift,
            grad_out_bias,
            grad_second_gain,
            grad_second_shift,
            grad_down_bias,
        ]
    )
    shards = (
        lax.psum_scatter(vector_grads, "ctx", scatter_dimension=1, tiled=True),
        lax.psum_scatter(grad_mix, "ctx", scatter_dimension=0, tiled=True),
        lax.psum_scatter(grad_mix_bias, "ctx", scatter_dimension=2, tiled=True),
        lax.psum_scatter(grad_out_weight, "ctx", scatter_dimension=1, tiled=True),
        lax.psum_scatter(grad_up, "ctx", scatter_dimension=0, tiled=True),
        lax.psum_scatter(grad_up_bias[None, :], "ctx", scatter_dimension=1, tiled=True),
        lax.psum_scatter(grad_down, "ctx", scatter_dimension=1, tiled=True),
    )
    vector_shard = lax.psum(shards[0], "tp")
    return (
        result.reshape(inputs.shape),
        grad_inputs,
        vector_shard[0],
        vector_shard[1],
        shards[1],
        shards[2],
        shards[3],
        vector_shard[2],
        vector_shard[3],
        vector_shard[4],
        shards[4],
        shards[5],
        shards[6],
        vector_shard[5],
    )


LANES = 128
CHUNK = 256
NT = (((1,), (1,)), ((), ()))
NN = (((1,), (0,)), ((), ()))
TN = (((0,), (0,)), ((), ()))


def mm(left, right, dims):
    return lax.dot_general(left, right, dims, preferred_element_type=jnp.float32)


def causal(span, chunk):
    key_place = lax.broadcasted_iota(jnp.int32, (span, chunk), 0)
    query_place = lax.broadcasted_iota(jnp.int32, (span, chunk), 1) + (span - chunk)
    return key_place <= query_place


def to_places(slots_ref, source, target, block_rows):
    for block in range(target.shape[0] // block_rows):
        start = pl.multiple_of(slots_ref[block] * block_rows, block_rows)
        target[pl.ds(block * block_rows, block_rows), :] = source[pl.ds(start, block_rows), :]


def to_slots(slots_ref, values, target, first_block, block_rows):
    for block in range(values.shape[0] // block_rows):
        start = pl.multiple_of(slots_ref[first_block + block] * block_rows, block_rows)
        target[pl.ds(start, block_rows), :] = values[block * block_rows : (block + 1) * block_rows]


def forward_kernel(block_rows, slots_ref, qkv_ref, out_ref, log_ref, rows):
    length, wide = rows.shape
    width = wide // 3
    chunk = min(CHUNK, length)
    to_places(slots_ref, qkv_ref, rows, block_rows)
    log_ref[...] = jnp.zeros(log_ref.shape, jnp.float32)
    for part in range(length // chunk):
        low, high = part * chunk, (part + 1) * chunk
        allowed = causal(high, chunk)
        columns = []
        for head in range(width // HD):
            lane = head * HD
            queries = rows[low:high, lane : lane + HD]
            keys = rows[0:high, width + lane : width + lane + HD]
            values = rows[0:high, 2 * width + lane : 2 * width + lane + HD]
            scores = jnp.where(allowed, mm(keys, queries, NT) * HD ** (-0.5), -1e30)
            top = jnp.max(scores, axis=0, keepdims=True)
            exponent = jnp.exp(scores - top)
            total = jnp.sum(exponent, axis=0, keepdims=True)
            weights = (exponent * (1.0 / total)).astype(jnp.bfloat16)
            columns.append(mm(values, weights, TN))
            log_ref[head : head + 1, low:high] = top + jnp.log(total)
        attended = jnp.concatenate(columns, axis=0).T.astype(jnp.bfloat16)
        to_slots(slots_ref, attended, out_ref, low // block_rows, block_rows)


def backward_kernel(
    block_rows, slots_ref, qkv_ref, grad_ref, log_ref, out_ref, rows, grads, key_sum, value_sum
):
    length, wide = rows.shape
    width = wide // 3
    chunk = min(CHUNK, length)
    scale = HD ** (-0.5)
    to_places(slots_ref, qkv_ref, rows, block_rows)
    to_places(slots_ref, grad_ref, grads, block_rows)
    key_sum[...] = jnp.zeros(key_sum.shape, jnp.float32)
    value_sum[...] = jnp.zeros(value_sum.shape, jnp.float32)
    for part in range(length // chunk):
        low, high = part * chunk, (part + 1) * chunk
        allowed = causal(high, chunk)
        query_columns, key_parts, value_parts = [], [], []
        for head in range(width // HD):
            lane = head * HD
            queries = rows[low:high, lane : lane + HD]
            keys = rows[0:high, width + lane : width + lane + HD]
            values = rows[0:high, 2 * width + lane : 2 * width + lane + HD]
            grad_out = grads[low:high, lane : lane + HD]
            scores = jnp.where(allowed, mm(keys, queries, NT) * scale, -1e30)
            probs = jnp.exp(scores - log_ref[head : head + 1, low:high])
            grad_probs = mm(values, grad_out, NT)
            delta = jnp.sum(probs * grad_probs, axis=0, keepdims=True)
            grad_scores = (probs * (grad_probs - delta)).astype(jnp.bfloat16)
            value_parts.append(mm(probs.astype(jnp.bfloat16), grad_out, NN))
            key_parts.append(mm(grad_scores, queries, NN))
            query_columns.append(mm(keys, grad_scores, TN))
        key_sum[0:high, :] += jnp.concatenate(key_parts, axis=1)
        value_sum[0:high, :] += jnp.concatenate(value_parts, axis=1)
        grad_query = (jnp.concatenate(query_columns, axis=0).T * scale).astype(jnp.bfloat16)
        to_slots(
            slots_ref, grad_query, out_ref.at[:, 0:width], low // block_rows, block_rows
        )
    to_slots(
        slots_ref,
        (key_sum[...] * scale).astype(jnp.bfloat16),
        out_ref.at[:, width : 2 * width],
        0,
        block_rows,
    )
    to_slots(
        slots_ref,
        value_sum[...].astype(jnp.bfloat16),
        out_ref.at[:, 2 * width : 3 * width],
        0,
        block_rows,
    )


def whole_shape(shape):
    return pl.BlockSpec(shape, lambda step: (0,) * len(shape))


def whole_block(array):
    return whole_shape(array.shape)


SMEM_SPEC = pl.BlockSpec(memory_space=pltpu.SMEM)
KERNEL_PARAMS = pltpu.CompilerParams(vmem_limit_bytes=60 * 1024 * 1024)


def attend_forward(slots, qkv, block_rows):
    length, wide = qkv.shape
    width = wide // 3
    area = length * length * width
    return pl.pallas_call(
        lambda *refs: forward_kernel(block_rows, *refs),
        out_shape=(
            jax.ShapeDtypeStruct((length, width), jnp.bfloat16),
            jax.ShapeDtypeStruct((8, length), jnp.float32),
        ),
        grid=(1,),
        in_specs=[SMEM_SPEC, whole_block(qkv)],
        out_specs=(whole_shape((length, width)), whole_shape((8, length))),
        scratch_shapes=[pltpu.VMEM((length, wide), jnp.bfloat16)],
        compiler_params=KERNEL_PARAMS,
        cost_estimate=pl.CostEstimate(
            flops=3 * area, bytes_accessed=8 * length * width, transcendentals=area // HD
        ),
        name="attend_forward",
    )(slots, qkv)


def attend_backward(slots, qkv, grad_out, log_total, block_rows):
    length, wide = qkv.shape
    width = wide // 3
    area = length * length * width
    return pl.pallas_call(
        lambda *refs: backward_kernel(block_rows, *refs),
        out_shape=jax.ShapeDtypeStruct((length, wide), jnp.bfloat16),
        grid=(1,),
        in_specs=[SMEM_SPEC, whole_block(qkv), whole_block(grad_out), whole_block(log_total)],
        out_specs=whole_shape((length, wide)),
        scratch_shapes=[
            pltpu.VMEM((length, wide), jnp.bfloat16),
            pltpu.VMEM((length, width), jnp.bfloat16),
            pltpu.VMEM((length, width), jnp.float32),
            pltpu.VMEM((length, width), jnp.float32),
        ],
        compiler_params=KERNEL_PARAMS,
        cost_estimate=pl.CostEstimate(
            flops=7 * area, bytes_accessed=14 * length * width, transcendentals=area // HD
        ),
        name="attend_backward",
    )(slots, qkv, grad_out, log_total)


def swap(values, axis, bit):
    count = lax.axis_size(axis)
    return lax.ppermute(values, axis, [(i, i ^ bit) for i in range(count)])


def together(*groups):
    return lax.optimization_barrier(groups)


def spread_step(held, axis, bit):
    keys = tuple(key for offsets, _ in held for key in offsets)
    arrays = [array for _, array in held]
    sent = arrays[0] if len(arrays) == 1 else jnp.concatenate(arrays, axis=0)
    return (keys, sent), (tuple(key ^ bit for key in keys), swap(sent, axis, bit))


def pack_kernel(pieces, mix_ref, out_weight_ref, *refs):
    vectors, (head_ref, tail_ref) = refs[:-2], refs[-2:]
    half = tail_ref.shape[1]
    parts, _, part_width = mix_ref.shape
    mix_width = parts * part_width
    shard = 2 * half
    for target, first in ((head_ref, 0), (tail_ref, half)):
        for part in range(parts):
            target[0, 0:half, part * part_width : (part + 1) * part_width] = mix_ref[
                part, first : first + half, :
            ]
        for piece in range(pieces):
            target[0, 0:half, mix_width + piece * shard : mix_width + (piece + 1) * shard] = (
                out_weight_ref[piece * shard + first : piece * shard + first + half, :]
            )
    extra = head_ref.shape[1] - half
    head_ref[0, half:, :] = jnp.zeros((extra, head_ref.shape[2]), jnp.bfloat16)
    for number, vector in enumerate(vectors):
        head_ref[0, half : half + 1, number * shard : number * shard + vector.shape[1]] = vector[...]


def late_kernel(up_ref, down_ref, late_ref):
    hidden_local = up_ref.shape[1]
    late_ref[:, 0:hidden_local] = up_ref[...]
    late_ref[:, hidden_local:] = down_ref[...].T


def pack_late(up_shard, down_shard):
    shard, hidden_local = up_shard.shape
    return pl.pallas_call(
        late_kernel,
        out_shape=jax.ShapeDtypeStruct((shard, 2 * hidden_local), jnp.bfloat16),
        grid=(1,),
        in_specs=[whole_block(up_shard), whole_block(down_shard)],
        out_specs=whole_shape((shard, 2 * hidden_local)),
        compiler_params=KERNEL_PARAMS,
        name="pack_late",
    )(up_shard, down_shard)


def pack(mix_shard, out_shard, vectors):
    parts, shard, part_width = mix_shard.shape
    pieces = out_shard.shape[0] // shard
    total = parts * part_width + out_shard.shape[0]
    return pl.pallas_call(
        lambda *refs: pack_kernel(pieces, *refs),
        out_shape=(
            jax.ShapeDtypeStruct((1, shard // 2 + 16, total), jnp.bfloat16),
            jax.ShapeDtypeStruct((1, shard // 2, total), jnp.bfloat16),
        ),
        grid=(1,),
        in_specs=[whole_block(array) for array in (mix_shard, out_shard, *vectors)],
        out_specs=(
            whole_shape((1, shard // 2 + 16, total)),
            whole_shape((1, shard // 2, total)),
        ),
        compiler_params=KERNEL_PARAMS,
        name="pack",
    )(mix_shard, out_shard, *vectors)


def first_kernel(head_keys, tail_keys, sizes, own_ref, *refs):
    groups, width, vector_count, bias_width = sizes
    tp_count = 4
    parts, refs = refs[:tp_count], refs[tp_count:]
    heads, refs = refs[: len(head_keys)], refs[len(head_keys) :]
    tails, refs = refs[: len(tail_keys)], refs[len(tail_keys) :]
    rows_ref, first_ref, weight_ref, out_weight_ref, table_ref, send_ref, gathered = refs
    own_tp, own_ctx = own_ref[0], own_ref[1]
    mix_width = weight_ref.shape[1]
    half = tails[0].shape[1]
    shard = 2 * half

    def put_out(piece, place, owner, first):
        columns = pl.ds(pl.multiple_of(owner * shard, shard), shard)
        for number in range(out_weight_ref.shape[0] // shard):
            low = mix_width + number * shard
            out_weight_ref[number * shard + first : number * shard + first + half, columns] = piece[
                place, 0:half, low : low + shard
            ]

    for keys, piece in zip(head_keys, heads):
        for place, key in enumerate(keys):
            owner = own_ctx ^ key
            rows = pl.ds(pl.multiple_of(owner * shard, shard), half)
            weight_ref[rows, :] = piece[place, 0:half, 0:mix_width]
            put_out(piece, place, owner, 0)
            extra = piece[place, half:, :].astype(jnp.float32)
            gathered[pl.ds(owner, 1), :] = extra[0:1, :]
    for keys, piece in zip(tail_keys, tails):
        for place, key in enumerate(keys):
            owner = own_ctx ^ key
            rows = pl.ds(pl.multiple_of(owner * shard + half, half), half)
            weight_ref[rows, :] = piece[place, :, 0:mix_width]
            put_out(piece, place, owner, half)
    count = gathered.shape[0]
    vectors = gathered[...]
    table_ref[...] = jnp.zeros(table_ref.shape, jnp.float32)
    for number in range(vector_count):
        lanes = slice(number * shard, (number + 1) * shard)
        for owner in range(count):
            table_ref[number : number + 1, owner * shard : (owner + 1) * shard] = vectors[
                owner : owner + 1, lanes
            ]
    bias_parts = []
    for number in range(2):
        low = vector_count * shard + number * bias_width
        bias_parts.append(
            jnp.concatenate(
                [vectors[owner : owner + 1, low : low + bias_width] for owner in range(count)],
                axis=1,
            )
        )
    bias = jnp.concatenate([bias_parts[0], jnp.zeros_like(bias_parts[0]), bias_parts[1]], axis=1)
    piece_count, part_rows, _ = parts[0].shape
    block_rows = tp_count * part_rows
    for key in range(tp_count):
        for piece in range(piece_count):
            row = pl.multiple_of(piece * block_rows + (own_tp ^ key) * part_rows, part_rows)
            rows_ref[pl.ds(row, part_rows), :] = parts[key][piece]
    seq_rows = send_ref.shape[1]
    dim_local = mix_width // 3
    gain, shift = table_ref[0:1, :], table_ref[1:2, :]
    for seq in range(rows_ref.shape[0] // seq_rows):
        rows = slice(seq * seq_rows, (seq + 1) * seq_rows)
        centered, scale = norm_parts(rows_ref[rows, :].astype(jnp.float32))
        normed = (centered * scale * gain + shift).astype(jnp.bfloat16)
        first_ref[rows, :] = normed
    projected_all = (mm(first_ref[...], weight_ref[...], NN) + bias).astype(jnp.bfloat16)
    for seq in range(rows_ref.shape[0] // seq_rows):
        projected = projected_all[seq * seq_rows : (seq + 1) * seq_rows, :]
        for group in range(groups):
            for number in range(3):
                low = number * dim_local + group * width
                send_ref[seq * groups + group, :, number * width : (number + 1) * width] = (
                    projected[:, low : low + width]
                )


def first_part(own, parts, heads, tails, seq_count, groups, vector_count, bias_width):
    piece_count, part_rows, model_width = parts[0].shape
    row_count = piece_count * part_rows * 4
    count = seq_count * groups
    mix_width = 3 * model_width // 4
    head_keys, head_arrays = zip(*heads)
    tail_keys, tail_arrays = zip(*tails)
    seq_rows = row_count // seq_count
    width = mix_width // (3 * groups)
    low = jnp.bfloat16
    shapes = (
        ((row_count, model_width), low),
        ((row_count, model_width), low),
        ((model_width, mix_width), low),
        ((head_arrays[0].shape[2] - mix_width, model_width), low),
        ((8, model_width), jnp.float32),
        ((count, seq_rows, 3 * width), low),
    )
    return pl.pallas_call(
        lambda *refs: first_kernel(
            head_keys, tail_keys, (groups, width, vector_count, bias_width), *refs
        ),
        out_shape=tuple(jax.ShapeDtypeStruct(*shape) for shape in shapes),
        grid=(1,),
        in_specs=[SMEM_SPEC]
        + [whole_block(array) for array in (*parts, *head_arrays, *tail_arrays)],
        out_specs=tuple(whole_shape(shape) for shape, _ in shapes),
        scratch_shapes=[pltpu.VMEM((count, head_arrays[0].shape[2]), jnp.float32)],
        compiler_params=KERNEL_PARAMS,
        cost_estimate=pl.CostEstimate(
            flops=2 * row_count * model_width * mix_width,
            bytes_accessed=8 * 1024 * 1024,
            transcendentals=0,
        ),
        name="first_part",
    )(own, *parts, *head_arrays, *tail_arrays)


def feed_grads_kernel(second_ref, grad_pre_ref, cot_ref, activated_ref, out_ref):
    half = grad_pre_ref.shape[1]
    out_ref[:, 0:half] = mm(second_ref[...], grad_pre_ref[...], TN).astype(jnp.bfloat16)
    out_ref[:, half:] = mm(cot_ref[...], activated_ref[...], TN).astype(jnp.bfloat16)


def feed_grads(second_all, grad_pre, cot_all, activated):
    row_count, model_width = second_all.shape
    hidden_local = grad_pre.shape[1]
    step = min(256, model_width)
    column = pl.BlockSpec((row_count, step), lambda i: (0, i))
    fixed = pl.BlockSpec((row_count, hidden_local), lambda i: (0, 0))
    return pl.pallas_call(
        feed_grads_kernel,
        grid=(model_width // step,),
        out_shape=jax.ShapeDtypeStruct((model_width, 2 * hidden_local), jnp.bfloat16),
        in_specs=[column, fixed, column, fixed],
        out_specs=pl.BlockSpec((step, 2 * hidden_local), lambda i: (i, 0)),
        compiler_params=KERNEL_PARAMS,
        cost_estimate=pl.CostEstimate(
            flops=4 * row_count * model_width * hidden_local,
            bytes_accessed=8 * 1024 * 1024,
            transcendentals=0,
        ),
        name="feed_grads",
    )(second_all, grad_pre, cot_all, activated)


def feed_finish_kernel(sum_ref, up_ref, down_ref):
    half = up_ref.shape[1]
    up_ref[...] = sum_ref[:, 0:half].astype(jnp.float32)
    down_ref[...] = sum_ref[:, half:].astype(jnp.float32).T


def feed_finish(total):
    shard, twice = total.shape
    shapes = ((shard, twice // 2), (twice // 2, shard))
    return pl.pallas_call(
        feed_finish_kernel,
        grid=(1,),
        out_shape=tuple(jax.ShapeDtypeStruct(shape, jnp.float32) for shape in shapes),
        in_specs=[whole_block(total)],
        out_specs=tuple(whole_shape(shape) for shape in shapes),
        compiler_params=KERNEL_PARAMS,
        name="feed_finish",
    )(total)


def mix_finish_kernel(mine_ref, came_ref, out_mine_ref, out_came_ref, mix_ref, out_ref):
    total = mine_ref[...].astype(jnp.float32) + came_ref[...].astype(jnp.float32)
    parts, _, part_width = mix_ref.shape
    for part in range(parts):
        mix_ref[part] = total[:, part * part_width : (part + 1) * part_width]
    out_ref[...] = (out_mine_ref[...].astype(jnp.float32) + out_came_ref[...].astype(jnp.float32)).T


def mix_finish(mine, came, out_mine, out_came):
    shard, dim_local = out_came.shape
    shapes = ((3, shard, dim_local), (dim_local, shard))
    arrays = (mine, came, out_mine, out_came)
    return pl.pallas_call(
        mix_finish_kernel,
        grid=(1,),
        out_shape=tuple(jax.ShapeDtypeStruct(shape, jnp.float32) for shape in shapes),
        in_specs=[whole_block(array) for array in arrays],
        out_specs=tuple(whole_shape(shape) for shape in shapes),
        compiler_params=KERNEL_PARAMS,
        name="mix_finish",
    )(*arrays)


def small_kernel(own_ref, first_ref, hidden_ref, early_ref, out_ref):
    devices, _, shard = out_ref.shape
    tp_count = 4
    own_tp = own_ref[0]
    share = 1.0 / tp_count
    rows = [
        first_ref[0:1, :],
        first_ref[1:2, :],
        hidden_ref[0:1, :] * share,
        hidden_ref[1:2, :] * share,
        hidden_ref[2:3, :] * share,
        early_ref[1:2, :] * share,
    ]
    out_ref[...] = jnp.zeros(out_ref.shape, jnp.float32)
    piece = shard // tp_count
    count = devices // tp_count
    for owner in range(count):
        for place in range(tp_count):
            index = owner * tp_count + place
            for number, row in enumerate(rows):
                out_ref[index, number : number + 1, :] = row[:, owner * shard : (owner + 1) * shard]
            own = jnp.where(own_tp == place, 1.0, 0.0)
            out_ref[index, len(rows) : len(rows) + 1, :] = (
                early_ref[0:1, owner * shard : (owner + 1) * shard] * own
            )
            for number, part in enumerate((0, 2)):
                low = part * count * piece + owner * piece
                out_ref[
                    index, len(rows) + 1 : len(rows) + 2, number * piece : (number + 1) * piece
                ] = first_ref[2:3, low : low + piece] * own


def small_pack(own, first_sums, hidden_sums, early_sums, count):
    shape = (4 * count, 8, first_sums.shape[1] // count)
    arrays = (first_sums, hidden_sums, early_sums)
    return pl.pallas_call(
        small_kernel,
        grid=(1,),
        out_shape=jax.ShapeDtypeStruct(shape, jnp.float32),
        in_specs=[SMEM_SPEC] + [whole_block(array) for array in arrays],
        out_specs=whole_shape(shape),
        compiler_params=KERNEL_PARAMS,
        name="small_pack",
    )(own, *arrays)


def halve(mine, came, bit):
    terms = mine.astype(jnp.float32) + came.astype(jnp.float32)
    terms = terms.reshape((-1, 2) + terms.shape[1:])
    at = jnp.where(lax.axis_index("ctx") & bit != 0, 1, 0)
    mine = lax.dynamic_index_in_dim(terms, at, 1, keepdims=False)
    other = lax.dynamic_index_in_dim(terms, 1 - at, 1, keepdims=False)
    return mine, swap(other.astype(jnp.bfloat16), "ctx", bit)


MLP_ROWS = 256


def branch_kernel(own_ref, attended_ref, weight_ref, mine_ref, other_ref, attended):
    core = own_ref[0] & 1
    count, seq_rows, width = attended_ref.shape
    seqs = mine_ref.shape[0] // seq_rows
    groups = count // (2 * seqs)
    for half, out_ref in ((1, other_ref), (0, mine_ref)):
        for seq in range(seqs):
            for group in range(groups):
                source = ((core ^ half) * seqs + seq) * groups + group
                attended[
                    seq * seq_rows : (seq + 1) * seq_rows, group * width : (group + 1) * width
                ] = attended_ref[source]
        out_ref[...] = mm(attended[...], weight_ref[...], NN).astype(jnp.bfloat16)


def branch_part(own, attended, out_full):
    count, seq_rows, width = attended.shape
    rows = count * seq_rows * width // out_full.shape[0]
    shape = (rows // 2, out_full.shape[1])
    return pl.pallas_call(
        branch_kernel,
        grid=(1,),
        out_shape=(jax.ShapeDtypeStruct(shape, jnp.bfloat16),) * 2,
        in_specs=[SMEM_SPEC, whole_block(attended), whole_block(out_full)],
        out_specs=(whole_shape(shape),) * 2,
        scratch_shapes=[pltpu.VMEM((rows // 2, out_full.shape[0]), jnp.bfloat16)],
        compiler_params=KERNEL_PARAMS,
        name="branch_part",
    )(own, attended, out_full)


def hidden_grad_kernel(
    own_ref,
    sum_ref,
    other_ref,
    cot_ref,
    hidden_ref,
    table_ref,
    weight_ref,
    send_ref,
    branch_ref,
    own_grad_ref,
    sums_ref,
    rows_ref,
):
    own_tp = own_ref[0]
    core = own_tp & 1
    count, seq_rows, width = send_ref.shape
    _, part_rows, model_width = own_grad_ref.shape
    seqs = sum_ref.shape[0] // seq_rows
    groups = count // (2 * seqs)
    block_rows = seq_rows // 2
    gain = table_ref[3:4, :]
    sums = [jnp.zeros((1, model_width), jnp.float32) for _ in range(3)]
    for half, grad_ref in enumerate((sum_ref, other_ref)):
        for chunk in range(seqs):
            seq = (core ^ half) * seqs + chunk
            rows = pl.ds(pl.multiple_of(seq * seq_rows, seq_rows), seq_rows)
            grad = grad_ref[chunk * seq_rows : (chunk + 1) * seq_rows, :].astype(jnp.float32)
            centered, scale = norm_parts(hidden_ref[rows, :])
            normal = centered * scale
            total = cot_ref[rows, :].astype(jnp.float32) + norm_backward(normal, scale, grad, gain)
            low = total.astype(jnp.bfloat16)
            branch_ref[rows, :] = low
            rows_ref[...] = total
            for block in range(2):
                first = pl.multiple_of(block * block_rows + own_tp * part_rows, part_rows)
                own_grad_ref[seq * 2 + block] = rows_ref[pl.ds(first, part_rows), :]
            sums[0] += jnp.sum(total, axis=0, keepdims=True)
            sums[1] += jnp.sum(grad * normal, axis=0, keepdims=True)
            sums[2] += jnp.sum(grad, axis=0, keepdims=True)
    attended = mm(branch_ref[...], weight_ref[...], NT).astype(jnp.bfloat16)
    for index in range(count):
        seq, group = index // groups, index % groups
        send_ref[index] = attended[
            seq * seq_rows : (seq + 1) * seq_rows, group * width : (group + 1) * width
        ]
    sums_ref[...] = jnp.zeros(sums_ref.shape, jnp.float32)
    for number, total in enumerate(sums):
        sums_ref[number : number + 1, :] = total


def hidden_grad_part(own, grad_sum, grad_other, cot_all, hidden, table, out_full, sizes):
    count, seq_rows, width, part_rows = sizes
    row_count, model_width = hidden.shape
    low = jnp.bfloat16
    shapes = (
        ((count, seq_rows, width), low),
        ((row_count, model_width), low),
        ((2 * row_count // seq_rows, part_rows, model_width), jnp.float32),
        ((8, model_width), jnp.float32),
    )
    arrays = (grad_sum, grad_other, cot_all, hidden, table, out_full)
    return pl.pallas_call(
        hidden_grad_kernel,
        grid=(1,),
        out_shape=tuple(jax.ShapeDtypeStruct(*shape) for shape in shapes),
        in_specs=[SMEM_SPEC] + [whole_block(array) for array in arrays],
        out_specs=tuple(whole_shape(shape) for shape, _ in shapes),
        scratch_shapes=[pltpu.VMEM((seq_rows, model_width), jnp.float32)],
        compiler_params=KERNEL_PARAMS,
        name="hidden_grad_part",
    )(own, *arrays)


def place_mixed(source_ref, target, width):
    count, seq_rows, total = source_ref.shape
    parts = total // width
    groups = target.shape[1] // total
    for index in range(count):
        seq, group = index // groups, index % groups
        for part in range(parts):
            low = (part * groups + group) * width
            target[seq * seq_rows : (seq + 1) * seq_rows, low : low + width] = source_ref[
                index, :, part * width : (part + 1) * width
            ]


def halved_grads_kernel(own_ref, left_ref, right_ref, mine_ref, other_ref, *placed):
    if placed:
        place_mixed(right_ref, placed[0], right_ref.shape[2])
        right_ref = placed[0]
    half, shard, _ = mine_ref.shape
    for flipped, out_ref in ((1, other_ref), (0, mine_ref)):
        for index in range(half):
            owner = 2 * index + ((own_ref[1] & 1) ^ flipped)
            columns = pl.ds(pl.multiple_of(owner * shard, shard), shard)
            out_ref[index] = mm(left_ref[:, columns], right_ref[...], TN).astype(jnp.bfloat16)


def halved_grads(own, left, right, count):
    row_count, model_width = left.shape
    width = right.size // row_count
    shape = (count // 2, model_width // count, width)
    placed = [pltpu.VMEM((row_count, width), jnp.bfloat16)] if len(right.shape) == 3 else []
    return pl.pallas_call(
        halved_grads_kernel,
        grid=(1,),
        out_shape=(jax.ShapeDtypeStruct(shape, jnp.bfloat16),) * 2,
        in_specs=[SMEM_SPEC, whole_block(left), whole_block(right)],
        out_specs=(whole_shape(shape),) * 2,
        scratch_shapes=placed,
        compiler_params=KERNEL_PARAMS,
        cost_estimate=pl.CostEstimate(
            flops=2 * model_width * row_count * width,
            bytes_accessed=2 * (left.size + right.size + model_width * width),
            transcendentals=0,
        ),
        name="halved_grads",
    )(own, left, right)


def mix_grads_kernel(keys, own_ref, grad_ref, *refs):
    pieces, (mine_ref, other_ref, normed) = refs[:-3], refs[-3:]
    own_core, own_ctx = own_ref[0] & 1, own_ref[1]
    half, shard, _ = mine_ref.shape
    for (piece_keys, core_key), piece in zip(keys, pieces):
        part_rows = piece.shape[1]
        for place, key in enumerate(piece_keys):
            start = (own_ctx ^ key) * 2 * part_rows + (own_core ^ core_key) * part_rows
            normed[pl.ds(pl.multiple_of(start, part_rows), part_rows), :] = piece[place]
    for flipped, out_ref in enumerate((mine_ref, other_ref)):
        for index in range(half):
            owner = 2 * index + ((own_ctx & 1) ^ flipped)
            columns = pl.ds(pl.multiple_of(owner * shard, shard), shard)
            out_ref[index] = mm(normed[:, columns], grad_ref[...], TN).astype(jnp.bfloat16)


def mix_grads(own, grad_qkv, count, held):
    keys = [(offsets, core_key) for offsets, core_key, _ in held]
    pieces = [piece for _, _, piece in held]
    length, width = grad_qkv.shape
    model_width = pieces[0].shape[2]
    shape = (count // 2, model_width // count, width)
    low = jnp.bfloat16
    arrays = (grad_qkv, *pieces)
    return pl.pallas_call(
        lambda *refs: mix_grads_kernel(keys, *refs),
        grid=(1,),
        out_shape=(jax.ShapeDtypeStruct(shape, low),) * 2,
        in_specs=[SMEM_SPEC] + [whole_block(array) for array in arrays],
        out_specs=(whole_shape(shape),) * 2,
        scratch_shapes=[pltpu.VMEM((length, model_width), low)],
        compiler_params=KERNEL_PARAMS,
        cost_estimate=pl.CostEstimate(
            flops=2 * model_width * length * width,
            bytes_accessed=8 * 1024 * 1024,
            transcendentals=0,
        ),
        name="mix_grads",
    )(own, *arrays)


def mix_join_kernel(own_ref, mine_ref, came_ref, keep_ref, send_ref):
    own_ctx = own_ref[1]
    is_first = (own_ctx & 1) == 0
    own_bit = (own_ctx >> 1) & 1
    width = mine_ref.shape[2] // 3
    for flipped, out_ref in enumerate((keep_ref, send_ref)):
        for index in range(out_ref.shape[0]):
            source = 2 * index + (own_bit ^ flipped)
            mine, came = mine_ref[source], came_ref[source]
            first = jnp.where(is_first, mine, came)
            second = jnp.where(is_first, came, mine)
            for part in range(3):
                lanes = slice(part * width, (part + 1) * width)
                low = 2 * part * width
                out_ref[index, :, low : low + width] = first[:, lanes]
                out_ref[index, :, low + width : low + 2 * width] = second[:, lanes]


def mix_join(own, mine, came):
    half, shard, total = mine.shape
    shape = (half // 2, shard, 2 * total)
    return pl.pallas_call(
        mix_join_kernel,
        grid=(1,),
        out_shape=(jax.ShapeDtypeStruct(shape, jnp.bfloat16),) * 2,
        in_specs=[SMEM_SPEC, whole_block(mine), whole_block(came)],
        out_specs=(whole_shape(shape),) * 2,
        compiler_params=KERNEL_PARAMS,
        name="mix_join",
    )(own, mine, came)


def first_grad_kernel(own_ref, mixed_ref, weight_ref, x_ref, mine_ref, other_ref, sums_ref, *refs):
    mixed, rows_ref = refs
    own_tp = own_ref[0]
    core = own_tp & 1
    count, seq_rows, total = mixed_ref.shape
    groups = mixed.shape[1] // total
    place_mixed(mixed_ref, mixed, total // 3)
    part_rows = mine_ref.shape[2]
    model_width = x_ref.shape[1]
    block_rows = seq_rows // 2
    sums = [jnp.zeros((1, model_width), jnp.float32) for _ in range(2)]
    partial_all = mm(mixed[...], weight_ref[...], NT)
    for seq in range(count // groups):
        rows = slice(seq * seq_rows, (seq + 1) * seq_rows)
        partial = partial_all[rows, :]
        rows_ref[...] = partial.astype(jnp.bfloat16)
        for block in range(2):
            for row in range(2):
                for flipped, out_ref in enumerate((mine_ref, other_ref)):
                    owner = 2 * row + (core ^ flipped)
                    first = pl.multiple_of(block * block_rows + owner * part_rows, part_rows)
                    out_ref[2 * seq + block, row] = rows_ref[pl.ds(first, part_rows), :]
        centered, scale = norm_parts(x_ref[rows, :].astype(jnp.float32))
        sums[0] += jnp.sum(partial * (centered * scale), axis=0, keepdims=True)
        sums[1] += jnp.sum(partial, axis=0, keepdims=True)
    sums_ref[...] = jnp.zeros(sums_ref.shape, jnp.float32)
    for number, value in enumerate(sums):
        sums_ref[number : number + 1, :] = value
    mixed_ref_sum = jnp.sum(mixed[...].astype(jnp.float32), axis=0, keepdims=True)
    sums_ref[2:3, 0 : mixed.shape[1]] = mixed_ref_sum


def first_grads(own, grad_mixed, mix_full, x_all, part_rows):
    count, seq_rows, total = grad_mixed.shape
    row_count, model_width = x_all.shape
    shape = (2 * row_count // seq_rows, 2, part_rows, model_width)
    low = jnp.bfloat16
    arrays = (grad_mixed, mix_full, x_all)
    return pl.pallas_call(
        first_grad_kernel,
        grid=(1,),
        out_shape=(
            jax.ShapeDtypeStruct(shape, low),
            jax.ShapeDtypeStruct(shape, low),
            jax.ShapeDtypeStruct((8, model_width), jnp.float32),
        ),
        in_specs=[SMEM_SPEC] + [whole_block(array) for array in arrays],
        out_specs=(whole_shape(shape), whole_shape(shape), whole_shape((8, model_width))),
        scratch_shapes=[
            pltpu.VMEM((row_count, mix_full.shape[1]), low),
            pltpu.VMEM((seq_rows, model_width), low),
        ],
        compiler_params=KERNEL_PARAMS,
        name="first_grads",
    )(own, *arrays)


def gelu_both(value):
    root = (2.0 / jnp.pi) ** 0.5
    square = value * value
    inner = jnp.tanh(root * value * (1.0 + 0.044715 * square))
    slope = 0.5 * (1.0 + inner) + 0.5 * value * (1.0 - inner * inner) * root * (
        1.0 + 3.0 * 0.044715 * square
    )
    return 0.5 * value * (1.0 + inner), slope


def feed_kernel(part_count, own_ref, sum_ref, other_ref, x_ref, table_ref, late_ref, *refs):
    cot_parts, refs = refs[:part_count], refs[part_count:]
    (
        hidden_ref,
        second_ref,
        activated_ref,
        grad_pre_ref,
        mine_ref,
        partner_ref,
        cot_ref,
        sums_ref,
    ) = refs
    own_tp = own_ref[0]
    core = own_tp & 1
    hidden_local = activated_ref.shape[1]
    blocks, part_rows, _ = cot_parts[0].shape
    for key, part in enumerate(cot_parts):
        for block in range(blocks):
            row = block * part_count * part_rows + (own_tp ^ key) * part_rows
            cot_ref[pl.ds(pl.multiple_of(row, part_rows), part_rows), :] = part[block]
    half_rows = sum_ref.shape[0]
    up_sum = jnp.zeros((1, hidden_local), jnp.float32)
    cot_sum = jnp.zeros((1, cot_ref.shape[1]), jnp.float32)
    for half, (branch_ref, out_ref) in enumerate(((sum_ref, mine_ref), (other_ref, partner_ref))):
        for chunk in range(half_rows // MLP_ROWS):
            inside = slice(chunk * MLP_ROWS, (chunk + 1) * MLP_ROWS)
            start = (core ^ half) * half_rows + chunk * MLP_ROWS
            rows = pl.ds(pl.multiple_of(start, MLP_ROWS), MLP_ROWS)
            hidden = (
                x_ref[rows, :].astype(jnp.float32)
                + branch_ref[inside, :].astype(jnp.float32)
                + table_ref[2:3, :]
            )
            hidden_ref[rows, :] = hidden
            centered, scale = norm_parts(hidden)
            second = (centered * scale * table_ref[3:4, :] + table_ref[4:5, :]).astype(jnp.bfloat16)
            second_ref[rows, :] = second
            activated, slope = gelu_both(mm(second, late_ref[:, 0:hidden_local], NN) + table_ref[6:7, :])
            activated_ref[rows, :] = activated.astype(jnp.bfloat16)
            cot = cot_ref[rows, :]
            grad_pre = (mm(cot, late_ref[:, hidden_local:], NN) * slope).astype(jnp.bfloat16)
            grad_pre_ref[rows, :] = grad_pre
            out_ref[inside, :] = mm(grad_pre, late_ref[:, 0:hidden_local], NT).astype(jnp.bfloat16)
            up_sum += jnp.sum(grad_pre.astype(jnp.float32), axis=0, keepdims=True)
            cot_sum += jnp.sum(cot.astype(jnp.float32), axis=0, keepdims=True)
    sums_ref[...] = jnp.zeros(sums_ref.shape, jnp.float32)
    sums_ref[0:1, 0:hidden_local] = up_sum
    sums_ref[1:2, 0 : cot_ref.shape[1]] = cot_sum


def feed_part(own, branch_sum, branch_other, x_all, table, late_all, cot_parts):
    row_count, model_width = x_all.shape
    hidden_local = late_all.shape[1] // 2
    low = jnp.bfloat16
    shapes = (
        ((row_count, model_width), jnp.float32),
        ((row_count, model_width), low),
        ((row_count, hidden_local), low),
        ((row_count, hidden_local), low),
        ((row_count // 2, model_width), low),
        ((row_count // 2, model_width), low),
        ((row_count, model_width), low),
        ((8, max(model_width, hidden_local)), jnp.float32),
    )
    arrays = (branch_sum, branch_other, x_all, table, late_all, *cot_parts)
    return pl.pallas_call(
        lambda *refs: feed_kernel(len(cot_parts), *refs),
        grid=(1,),
        out_shape=tuple(jax.ShapeDtypeStruct(*shape) for shape in shapes),
        in_specs=[SMEM_SPEC] + [whole_block(array) for array in arrays],
        out_specs=tuple(whole_shape(shape) for shape, _ in shapes),
        compiler_params=KERNEL_PARAMS,
        cost_estimate=pl.CostEstimate(
            flops=6 * row_count * model_width * hidden_local,
            bytes_accessed=16 * 1024 * 1024,
            transcendentals=row_count * hidden_local,
        ),
        name="feed_part",
    )(own, *arrays)


def spread_tp(part):
    return [part] + [swap(part, "tp", key) for key in (1, 2, 3)]


def add_halves(mine, other, beside=None):
    arrived = swap(other, "tp", 1)
    chip_sum = (mine.astype(jnp.float32) + arrived.astype(jnp.float32)).astype(jnp.bfloat16)
    arrived = swap(chip_sum, "tp", 2)
    if beside is not None:
        arrived, beside = together(arrived, beside)
    whole = (chip_sum.astype(jnp.float32) + arrived.astype(jnp.float32)).astype(jnp.bfloat16)
    return whole, swap(whole, "tp", 1), beside


def owner_first(partial, part_rows):
    core = lax.axis_index("tp") & 1
    parts = partial.astype(jnp.bfloat16).reshape(-1, 2, 2, part_rows, partial.shape[-1])
    mine = lax.dynamic_index_in_dim(parts, core, 2, keepdims=False)
    return mine, swap(lax.dynamic_index_in_dim(parts, 1 - core, 2, keepdims=False), "tp", 1)


def owner_second(mine, arrived):
    row = lax.axis_index("tp") >> 1
    chip_sum = mine.astype(jnp.float32) + arrived.astype(jnp.float32)
    mine = lax.dynamic_index_in_dim(chip_sum, row, 1, keepdims=False)
    other = lax.dynamic_index_in_dim(chip_sum, 1 - row, 1, keepdims=False)
    return mine, swap(other.astype(jnp.bfloat16), "tp", 2)


def add_rows_to_owner(partial, part_rows):
    mine, arrived = owner_second(*owner_first(partial, part_rows))
    return mine + arrived.astype(jnp.float32)


def exchange(pieces):
    return lax.all_to_all(pieces, "ctx", 0, 0, tiled=True)


def norm_parts(rows):
    row_mean = jnp.mean(rows, axis=-1, keepdims=True)
    centered = rows - row_mean
    variance = jnp.mean(centered * centered, axis=-1, keepdims=True)
    return centered, lax.rsqrt(variance + epsilon)


def norm_backward(normal, scale, gradient, gain):
    scaled = gradient * gain
    return scale * (
        scaled
        - jnp.mean(scaled, axis=-1, keepdims=True)
        - normal * jnp.mean(scaled * normal, axis=-1, keepdims=True)
    )


def fast_body(
    inputs,
    pairing,
    first_gain,
    first_shift,
    query_key_value_weight,
    mix_bias,
    output_projection_weight,
    out_bias,
    second_gain,
    second_shift,
    up_projection_weight,
    up_projection_bias,
    down_projection_weight,
    down_bias,
    cotangent,
):
    low = jnp.bfloat16
    wide = jnp.float32
    seq_count, _, _, part_rows, model_width = inputs.shape
    tp_count = lax.axis_size("tp")
    ctx_count = lax.axis_size("ctx")
    block_rows = part_rows * tp_count
    seq_rows = 2 * block_rows
    row_count = seq_count * seq_rows
    shard = model_width // ctx_count
    dim_local = query_key_value_weight.shape[2]
    hidden_local = up_projection_weight.shape[1]
    groups = ctx_count // seq_count
    width = dim_local // groups
    own_tp = lax.axis_index("tp")

    vectors = [
        first_gain[None],
        first_shift[None],
        out_bias[None],
        second_gain[None],
        second_shift[None],
        down_bias[None],
        up_projection_bias,
        jnp.concatenate([mix_bias[0], mix_bias[1]], axis=1),
    ]
    head, tail = pack(
        jnp.transpose(query_key_value_weight, (1, 0, 2)), output_projection_weight, vectors
    )
    bits = [1 << place for place in range(ctx_count.bit_length() - 1)]
    head_bits, tail_bits = bits[::-1], bits[:1] + bits[:0:-1]
    heads, tails = [((0,), head)], [((0,), tail)]
    row_parts = spread_tp(inputs.reshape(-1, part_rows, model_width))
    cot_part = cotangent.reshape(-1, part_rows, model_width)
    late_shard = pack_late(up_projection_weight, down_projection_weight)
    for step, (head_bit, tail_bit) in enumerate(zip(head_bits, tail_bits)):
        heads = list(spread_step(heads, "ctx", head_bit))
        tails = list(spread_step(tails, "ctx", tail_bit))
        arrivals = (heads[1][1], tails[1][1])
        if step == 0:
            arrivals, row_parts, cot_part = together(arrivals, row_parts, cot_part)
            cot_parts = spread_tp(cot_part)
        elif step == 1:
            arrivals, cot_parts = together(arrivals, cot_parts)
        else:
            arrivals, late_shard = together(arrivals, late_shard)
        heads[1], tails[1] = (heads[1][0], arrivals[0]), (tails[1][0], arrivals[1])
    late_all = lax.all_gather(late_shard, "ctx", axis=0, tiled=True)
    own = jnp.stack([own_tp, lax.axis_index("ctx")]).astype(jnp.int32)
    row_all, first_all, mix_full, out_full, table, projected = first_part(
        own, row_parts, heads, tails, seq_count, groups, 7, mix_bias.shape[2]
    )
    gain_one, bias_down = table[0], table[5]

    sequence = lax.axis_index("ctx") // groups
    pairs = lax.dynamic_index_in_dim(pairing, sequence, 0, keepdims=False)
    blocks = jnp.stack([pairs, 2 * ctx_count - 1 - pairs], axis=-1).reshape(-1)
    places = jnp.arange(2 * ctx_count, dtype=jnp.int32)
    slots = jnp.sum(
        jnp.where(blocks[None, :] == places[:, None], places[None, :], 0), axis=1
    ).astype(jnp.int32)
    qkv = exchange(projected).reshape(ctx_count * seq_rows, 3 * width)
    attended_heads, log_total = attend_forward(slots, qkv, block_rows)
    attended = exchange(attended_heads.reshape(ctx_count, seq_rows, width))
    attended, normed_seqs = together(attended, first_all.reshape(seq_count, 2, block_rows, -1))
    normed_seqs = lax.dynamic_index_in_dim(normed_seqs, own_tp & 1, 1, keepdims=False)
    held = []
    for key in range(0, ctx_count, groups):
        their_seq = (lax.axis_index("ctx") ^ key) // groups
        piece = lax.dynamic_index_in_dim(normed_seqs, their_seq, 0)
        held.append(((key,), swap(piece, "ctx", key) if key else piece))
    branch_sum, branch_other, _ = add_halves(*branch_part(own, attended, out_full))
    hidden, second_all, activated, grad_pre, mine, other, cot_all, early_sums = feed_part(
        own, branch_sum, branch_other, row_all, table, late_all, cot_parts
    )

    grad_pre, *pieces = together(grad_pre, *(piece for _, piece in held))
    held = [(keys, piece) for (keys, _), piece in zip(held, pieces)]
    feed_terms = feed_grads(second_all, grad_pre, cot_all, activated)
    feed_total = lax.psum_scatter(feed_terms, "ctx", scatter_dimension=0, tiled=True)
    held = list(spread_step(held, "ctx", 1))
    grad_sum, grad_other, last_piece = add_halves(mine, other, held[1][1])
    held[1] = (held[1][0], last_piece)
    offsets = held[0][0] + held[1][0]
    sent = jnp.concatenate([held[0][1], held[1][1]], axis=0)
    held = [(offsets, 0, sent), (offsets, 1, swap(sent, "tp", 1))]
    grad_attended, grad_branch, own_grad, hidden_sums = hidden_grad_part(
        own,
        grad_sum,
        grad_other,
        cot_all,
        hidden,
        table,
        out_full,
        (ctx_count, seq_rows, width, part_rows),
    )
    grad_attended, last_piece = together(grad_attended, held[1][2])
    held[1] = (offsets, 1, last_piece)
    out_mine, out_other = halved_grads(own, grad_branch, attended, ctx_count)
    out_came = swap(out_other, "ctx", 1)
    grad_heads = exchange(grad_attended).reshape(ctx_count * seq_rows, width)
    grad_qkv = attend_backward(slots, qkv, grad_heads, log_total, block_rows)
    grad_qkv, out_came = together(grad_qkv, out_came)
    mix_mine, mix_other = mix_grads(own, grad_qkv, ctx_count, held)
    mix_other, out_came = together(mix_other, out_came)
    out_mine, out_came = halve(out_mine, out_came, 2)
    down_sum = add_rows_to_owner(mm(activated, late_all[:, hidden_local:], NT), part_rows)
    own_hidden = lax.dynamic_index_in_dim(
        hidden.reshape(-1, tp_count, part_rows, model_width), own_tp, 1, keepdims=False
    )
    result = (own_hidden + down_sum + bias_down).astype(low)

    grad_mixed, mix_mine, mix_came, out_came, result = together(
        exchange(grad_qkv.reshape(ctx_count, seq_rows, 3 * width)),
        mix_mine,
        swap(mix_other, "ctx", 1),
        out_came,
        result,
    )
    mix_mine, mix_other = mix_join(own, mix_mine, mix_came)
    mix_came = swap(mix_other, "ctx", 2)
    grad_mixed, mix_mine = together(grad_mixed, mix_mine)
    for bit in bits[2:]:
        out_mine, out_came = halve(out_mine, out_came, bit)
    mine, other, first_sums = first_grads(own, grad_mixed, mix_full, row_all, part_rows)
    small_terms = small_pack(own, first_sums, hidden_sums, early_sums, ctx_count)
    other, small_terms = together(other, small_terms)
    small = lax.all_to_all(small_terms, ("ctx", "tp"), 0, 0, tiled=True)
    mine, came = owner_second(mine, swap(other, "tp", 1))
    mix_came, came, out_came = together(mix_came, came, out_came)
    for bit in bits[2:]:
        mix_mine, mix_came = halve(mix_mine, mix_came, bit)
    up_shard, down_shard = feed_finish(feed_total)
    grad_first = mine + came.astype(wide)
    own_rows = inputs.reshape(-1, part_rows, model_width).astype(wide)
    own_centered, own_scale = norm_parts(own_rows)
    grad_inputs = own_grad + norm_backward(
        own_centered * own_scale, own_scale, grad_first, gain_one
    )
    mix_came, grad_inputs, small, up_shard, down_shard = together(
        mix_came, grad_inputs, small, up_shard, down_shard
    )
    mix_shard_sum, out_shard_sum = mix_finish(mix_mine[0], mix_came[0], out_mine[0], out_came[0])
    sums = jnp.sum(small, axis=0)
    piece = dim_local // ctx_count
    return (
        result.reshape(inputs.shape),
        grad_inputs.reshape(inputs.shape),
        sums[0],
        sums[1],
        jnp.transpose(mix_shard_sum, (1, 0, 2)),
        jnp.stack([sums[7, :piece], sums[7, piece : 2 * piece]])[:, None, :],
        out_shard_sum,
        sums[2],
        sums[3],
        sums[4],
        up_shard,
        sums[6][None, :],
        down_shard,
        sums[5],
    )


def fits_exchange(inputs, query_key_value_weight, up_projection_weight):
    ctx_count, tp_count = lax.axis_size("ctx"), lax.axis_size("tp")
    seq_count = inputs.shape[0]
    if tp_count != 4 or ctx_count % seq_count or ctx_count & (ctx_count - 1):
        return False
    dim_local = query_key_value_weight.shape[2]
    groups = ctx_count // seq_count
    length = ctx_count * 2 * tp_count * inputs.shape[3]
    shard = inputs.shape[4] // ctx_count
    if groups != 2 or seq_count < 2 or dim_local * 4 != inputs.shape[4]:
        return False
    if up_projection_weight.shape[1] != inputs.shape[4]:
        return False
    return dim_local % (groups * LANES) == 0 and length <= 2048 and shard % LANES == 0


def body(inputs, pairing, first_gain, first_shift, query_key_value_weight, *others):
    fits = fits_exchange(inputs, query_key_value_weight, others[5])
    chosen = fast_body if fits else general_body
    return chosen(inputs, pairing, first_gain, first_shift, query_key_value_weight, *others)


def solution(mesh):
    return jax.shard_map(
        body,
        mesh=mesh,
        in_specs=(
            P(None, "ctx", None, "tp", None),
            P(),
            P("ctx"),
            P("ctx"),
            P("ctx", None, "tp"),
            P(None, "tp", "ctx"),
            P("tp", "ctx"),
            P("ctx"),
            P("ctx"),
            P("ctx"),
            P("ctx", "tp"),
            P("tp", "ctx"),
            P("tp", "ctx"),
            P("ctx"),
            P(None, "ctx", None, "tp", None),
        ),
        out_specs=(
            P(None, "ctx", None, "tp", None),
            P(None, "ctx", None, "tp", None),
            P("ctx"),
            P("ctx"),
            P("ctx", None, "tp"),
            P(None, "tp", "ctx"),
            P("tp", "ctx"),
            P("ctx"),
            P("ctx"),
            P("ctx"),
            P("ctx", "tp"),
            P("tp", "ctx"),
            P("tp", "ctx"),
            P("ctx"),
        ),
        check_vma=False,
    )
```

```python
import jax
import jax.numpy as jnp
from jax import lax
from jax.experimental import pallas as pl
from jax.experimental.pallas import tpu as pltpu
from jax.sharding import PartitionSpec as P

HD = 64


epsilon = 1e-05


def normalize(token_rows, scaling, offset):
    row_mean = jnp.mean(token_rows, axis=-1, keepdims=True)
    centered = token_rows - row_mean
    variance = jnp.mean(centered * centered, axis=-1, keepdims=True)
    return centered * lax.rsqrt(variance + epsilon) * scaling + offset


def gelu_tanh(values_in):
    return jax.nn.gelu(values_in, approximate=True)


def block_places(pairing_rows, block_rows):
    slot_count = pairing_rows.shape[-1]
    starts = jnp.stack([pairing_rows, 2 * slot_count - 1 - pairing_rows], axis=-1) * block_rows
    within = jnp.arange(block_rows, dtype=jnp.int32)
    return (starts[:, :, :, None] + within).reshape(pairing_rows.shape[0], -1)


def by_head(tensor, head_count):
    seq_span, row_span, model_width = tensor.shape
    return jnp.moveaxis(
        tensor.reshape(seq_span, row_span, head_count, model_width // head_count), 2, 0
    )


def from_head(tensor):
    head_count, seq_span, row_span, head_size = tensor.shape
    return jnp.moveaxis(tensor, 0, 2).reshape(seq_span, row_span, head_count * head_size)


def head_scores(queries, key_vectors, allowed, score_scale):
    scores = (
        jnp.einsum("gqd,gkd->gqk", queries, key_vectors, preferred_element_type=jnp.float32)
        * score_scale
    )
    return jnp.where(allowed, scores, -jnp.inf)


def recompute(queries, key_vectors, value_vectors, grad_out, log_total, allowed, score_scale):
    scores = head_scores(queries, key_vectors, allowed, score_scale)
    probabilities = jnp.exp(scores - log_total[:, :, None])
    grad_probs = jnp.einsum(
        "gqd,gkd->gqk", grad_out, value_vectors, preferred_element_type=jnp.float32
    )
    return (probabilities, grad_probs)


def spread_rows(normed):
    return lax.all_gather(normed, "tp", axis=2, tiled=True)


def collect_rows(partial_terms):
    return lax.psum_scatter(
        partial_terms.astype(jnp.bfloat16), "tp", scatter_dimension=2, tiled=True
    ).astype(jnp.float32)


def spread_grads(gradient_part):
    return lax.all_gather(gradient_part, "tp", axis=2, tiled=True)


def collect_grads(partial_terms):
    return lax.psum_scatter(
        partial_terms.astype(jnp.bfloat16), "tp", scatter_dimension=2, tiled=True
    ).astype(jnp.float32)


def fetch_keys(key_part, value_part):
    return (
        lax.all_gather(key_part, "ctx", axis=1, tiled=True),
        lax.all_gather(value_part, "ctx", axis=1, tiled=True),
    )


def general_body(
    inputs,
    pairing,
    first_gain,
    first_shift,
    query_key_value_weight,
    mix_bias,
    output_projection_weight,
    out_bias,
    second_gain,
    second_shift,
    up_projection_weight,
    up_projection_bias,
    down_projection_weight,
    down_bias,
    cotangent,
):
    seq_count = inputs.shape[0]
    part_rows = inputs.shape[3]
    model_width = inputs.shape[4]
    tp_count = lax.axis_size("tp")
    block_rows = part_rows * tp_count
    local_rows = 2 * block_rows
    ctx_index = lax.axis_index("ctx")
    score_scale = HD ** (-0.5)
    batch_seqs = seq_count
    for candidate in range(seq_count, 0, -1):
        if seq_count % candidate == 0 and candidate * local_rows >= 512:
            batch_seqs = candidate
    groups = seq_count // batch_seqs
    vector_stack = jnp.stack(
        [first_gain, first_shift, out_bias, second_gain, second_shift, down_bias]
    )
    fetched = (
        lax.all_gather(vector_stack, "ctx", axis=1, tiled=True),
        lax.all_gather(query_key_value_weight, "ctx", axis=0, tiled=True),
        lax.all_gather(mix_bias, "ctx", axis=2, tiled=True),
        lax.all_gather(output_projection_weight, "ctx", axis=1, tiled=True),
        lax.all_gather(up_projection_weight, "ctx", axis=0, tiled=True),
        lax.all_gather(up_projection_bias, "ctx", axis=1, tiled=True),
        lax.all_gather(down_projection_weight, "ctx", axis=1, tiled=True),
    )
    vectors_full = fetched[0].astype(jnp.float32)
    dim_local = fetched[2].shape[2]
    head_count = dim_local // HD
    token_rows = inputs.reshape(seq_count, 2, part_rows, model_width).astype(jnp.float32)
    first_norm_output = normalize(token_rows, vectors_full[0], vectors_full[1]).astype(jnp.bfloat16)
    first_all = spread_rows(first_norm_output)
    projected_output = jnp.einsum(
        "sabd,dkc->sabkc", first_all, fetched[1], preferred_element_type=jnp.float32
    )
    bias_full = fetched[2].astype(jnp.float32)
    bias_rows = jnp.stack([bias_full[0, 0], jnp.zeros((dim_local,), jnp.float32), bias_full[1, 0]])
    projected_output = (projected_output + bias_rows).astype(jnp.bfloat16)

    def grouped(tensor):
        return tensor.reshape(groups, batch_seqs, local_rows, tensor.shape[-1])

    def ungrouped(tensor):
        return tensor.reshape(seq_count, 2, block_rows, dim_local)

    query_groups = grouped(projected_output[:, :, :, 0])
    key_groups = grouped(projected_output[:, :, :, 1])
    value_groups = grouped(projected_output[:, :, :, 2])
    pairing_groups = pairing.reshape(groups, batch_seqs, pairing.shape[1])

    def forward_group(unused_carry, inputs_group):
        query_part, key_part, value_part, pairing_rows = inputs_group
        key_all, value_all = fetch_keys(key_part, value_part)
        places = block_places(pairing_rows, block_rows)
        own_places = lax.dynamic_slice_in_dim(places, ctx_index * local_rows, local_rows, 1)
        allowed = own_places[:, :, None] >= places[:, None, :]

        def head_forward(operands):
            queries, key_vectors, value_vectors = operands
            scores = head_scores(queries, key_vectors, allowed, score_scale)
            row_max = jnp.max(scores, axis=-1, keepdims=True)
            exponent = jnp.exp(scores - row_max)
            row_total = jnp.sum(exponent, axis=-1, keepdims=True)
            weights_low = (exponent / row_total).astype(jnp.bfloat16)
            attention_result = jnp.einsum(
                "gqk,gkd->gqd", weights_low, value_vectors, preferred_element_type=jnp.float32
            )
            return (attention_result.astype(jnp.bfloat16), (row_max + jnp.log(row_total))[:, :, 0])

        outputs, log_totals = lax.map(
            head_forward,
            (
                by_head(query_part, head_count),
                by_head(key_all, head_count),
                by_head(value_all, head_count),
            ),
        )
        return (unused_carry, (from_head(outputs), log_totals))

    unused_state, (output_groups, log_groups) = lax.scan(
        forward_group, None, (query_groups, key_groups, value_groups, pairing_groups)
    )
    attention_result = ungrouped(output_groups)
    residual_branch = collect_rows(
        jnp.einsum(
            "sabc,cd->sabd", attention_result, fetched[3], preferred_element_type=jnp.float32
        )
    )
    hidden = token_rows + residual_branch + vectors_full[2]
    second_norm_output = normalize(hidden, vectors_full[3], vectors_full[4]).astype(jnp.bfloat16)
    second_all = spread_rows(second_norm_output)
    before_activation = jnp.einsum(
        "sabd,df->sabf", second_all, fetched[4], preferred_element_type=jnp.float32
    ) + fetched[5][0].astype(jnp.float32)
    activation_rows = gelu_tanh(before_activation).astype(jnp.bfloat16)
    residual_branch_two = collect_rows(
        jnp.einsum("sabf,fd->sabd", activation_rows, fetched[6], preferred_element_type=jnp.float32)
    )
    result = (hidden + residual_branch_two + vectors_full[5]).astype(jnp.bfloat16)
    vectors_back = fetched[0].astype(jnp.float32)
    grad_result_low = cotangent.reshape(seq_count, 2, part_rows, model_width)
    grad_result = grad_result_low.astype(jnp.float32)
    grad_down_bias = jnp.sum(grad_result, axis=(0, 1, 2))
    grad_branch_two = spread_grads(grad_result_low)
    grad_down = jnp.einsum(
        "sabf,sabd->fd", activation_rows, grad_branch_two, preferred_element_type=jnp.float32
    )
    grad_activated = jnp.einsum(
        "sabd,fd->sabf", grad_branch_two, fetched[6], preferred_element_type=jnp.float32
    )
    gelu_pull = jax.vjp(gelu_tanh, before_activation)[1]
    grad_pre = gelu_pull(grad_activated)[0].astype(jnp.bfloat16)
    grad_up_bias = jnp.sum(grad_pre, axis=(0, 1, 2), dtype=jnp.float32)
    grad_up = jnp.einsum("sabd,sabf->df", second_all, grad_pre, preferred_element_type=jnp.float32)
    grad_second = collect_grads(
        jnp.einsum("sabf,df->sabd", grad_pre, fetched[4], preferred_element_type=jnp.float32)
    )
    second_pull = jax.vjp(normalize, hidden, vectors_back[3], vectors_back[4])[1]
    grad_hidden_norm, grad_second_gain, grad_second_shift = second_pull(grad_second)
    grad_hidden = grad_result + grad_hidden_norm
    grad_out_bias = jnp.sum(grad_hidden, axis=(0, 1, 2))
    grad_branch = spread_grads(grad_hidden.astype(jnp.bfloat16))
    grad_out_weight = jnp.einsum(
        "sabc,sabd->cd", attention_result, grad_branch, preferred_element_type=jnp.float32
    )
    grad_attended = jnp.einsum(
        "sabd,cd->sabc", grad_branch, fetched[3], preferred_element_type=jnp.float32
    ).astype(jnp.bfloat16)
    grad_groups = grouped(grad_attended)

    def backward_group(unused_carry, inputs_group):
        query_part, key_part, value_part, grad_part, log_part, pairing_rows = inputs_group
        key_all, value_all = fetch_keys(key_part, value_part)
        places = block_places(pairing_rows, block_rows)
        own_places = lax.dynamic_slice_in_dim(places, ctx_index * local_rows, local_rows, 1)
        allowed = own_places[:, :, None] >= places[:, None, :]

        def joint_pass(operands):
            queries, key_vectors, value_vectors, grad_out, log_total = operands
            probabilities, grad_probs = recompute(
                queries, key_vectors, value_vectors, grad_out, log_total, allowed, score_scale
            )
            row_delta = jnp.sum(probabilities * grad_probs, axis=-1, keepdims=True)
            grad_scores = (probabilities * (grad_probs - row_delta)).astype(jnp.bfloat16)
            grad_query = (
                jnp.einsum(
                    "gqk,gkd->gqd", grad_scores, key_vectors, preferred_element_type=jnp.float32
                )
                * score_scale
            )
            grad_key = (
                jnp.einsum("gqk,gqd->gkd", grad_scores, queries, preferred_element_type=jnp.float32)
                * score_scale
            )
            grad_value = jnp.einsum(
                "gqk,gqd->gkd",
                probabilities.astype(jnp.bfloat16),
                grad_out,
                preferred_element_type=jnp.float32,
            )
            return (grad_query, grad_key, grad_value)

        grad_queries, grad_keys, grad_values = lax.map(
            joint_pass,
            (
                by_head(query_part, head_count),
                by_head(key_all, head_count),
                by_head(value_all, head_count),
                by_head(grad_part, head_count),
                log_part,
            ),
        )
        grad_key_rows, grad_value_rows = (
            lax.psum_scatter(from_head(grad_keys), "ctx", scatter_dimension=1, tiled=True),
            lax.psum_scatter(from_head(grad_values), "ctx", scatter_dimension=1, tiled=True),
        )
        return (
            unused_carry,
            (
                from_head(grad_queries).astype(jnp.bfloat16),
                grad_key_rows.astype(jnp.bfloat16),
                grad_value_rows.astype(jnp.bfloat16),
            ),
        )

    unused_back, (query_grads, key_grads, value_grads) = lax.scan(
        backward_group,
        None,
        (query_groups, key_groups, value_groups, grad_groups, log_groups, pairing_groups),
    )
    grad_query_rows = ungrouped(query_grads)
    grad_value_rows = ungrouped(value_grads)
    grad_projected = jnp.stack([grad_query_rows, ungrouped(key_grads), grad_value_rows], axis=3)
    grad_mix_bias = jnp.stack(
        [
            jnp.sum(grad_query_rows, axis=(0, 1, 2), dtype=jnp.float32),
            jnp.sum(grad_value_rows, axis=(0, 1, 2), dtype=jnp.float32),
        ]
    )[:, None, :]
    grad_mix = jnp.einsum(
        "sabd,sabkc->dkc", first_all, grad_projected, preferred_element_type=jnp.float32
    )
    grad_first = collect_grads(
        jnp.einsum(
            "sabkc,dkc->sabd", grad_projected, fetched[1], preferred_element_type=jnp.float32
        )
    )
    first_pull = jax.vjp(normalize, token_rows, vectors_back[0], vectors_back[1])[1]
    grad_token_norm, grad_first_gain, grad_first_shift = first_pull(grad_first)
    grad_inputs = (grad_hidden + grad_token_norm).reshape(inputs.shape)
    vector_grads = jnp.stack(
        [
            grad_first_gain,
            grad_first_shift,
            grad_out_bias,
            grad_second_gain,
            grad_second_shift,
            grad_down_bias,
        ]
    )
    shards = (
        lax.psum_scatter(vector_grads, "ctx", scatter_dimension=1, tiled=True),
        lax.psum_scatter(grad_mix, "ctx", scatter_dimension=0, tiled=True),
        lax.psum_scatter(grad_mix_bias, "ctx", scatter_dimension=2, tiled=True),
        lax.psum_scatter(grad_out_weight, "ctx", scatter_dimension=1, tiled=True),
        lax.psum_scatter(grad_up, "ctx", scatter_dimension=0, tiled=True),
        lax.psum_scatter(grad_up_bias[None, :], "ctx", scatter_dimension=1, tiled=True),
        lax.psum_scatter(grad_down, "ctx", scatter_dimension=1, tiled=True),
    )
    vector_shard = lax.psum(shards[0], "tp")
    return (
        result.reshape(inputs.shape),
        grad_inputs,
        vector_shard[0],
        vector_shard[1],
        shards[1],
        shards[2],
        shards[3],
        vector_shard[2],
        vector_shard[3],
        vector_shard[4],
        shards[4],
        shards[5],
        shards[6],
        vector_shard[5],
    )


LANES = 128
CHUNK = 256
NT = (((1,), (1,)), ((), ()))
NN = (((1,), (0,)), ((), ()))
TN = (((0,), (0,)), ((), ()))


def mm(left, right, dims):
    return lax.dot_general(left, right, dims, preferred_element_type=jnp.float32)


def causal(span, chunk):
    key_place = lax.broadcasted_iota(jnp.int32, (span, chunk), 0)
    query_place = lax.broadcasted_iota(jnp.int32, (span, chunk), 1) + (span - chunk)
    return key_place <= query_place


def to_places(slots_ref, source, target, block_rows):
    for block in range(target.shape[0] // block_rows):
        start = pl.multiple_of(slots_ref[block] * block_rows, block_rows)
        target[pl.ds(block * block_rows, block_rows), :] = source[pl.ds(start, block_rows), :]


def to_slots(slots_ref, values, target, first_block, block_rows):
    for block in range(values.shape[0] // block_rows):
        start = pl.multiple_of(slots_ref[first_block + block] * block_rows, block_rows)
        target[pl.ds(start, block_rows), :] = values[block * block_rows : (block + 1) * block_rows]


def forward_kernel(block_rows, slots_ref, qkv_ref, out_ref, log_ref, rows):
    length, wide = rows.shape
    width = wide // 3
    chunk = min(CHUNK, length)
    to_places(slots_ref, qkv_ref, rows, block_rows)
    log_ref[...] = jnp.zeros(log_ref.shape, jnp.float32)
    for part in range(length // chunk):
        low, high = part * chunk, (part + 1) * chunk
        allowed = causal(high, chunk)
        columns = []
        for head in range(width // HD):
            lane = head * HD
            queries = rows[low:high, lane : lane + HD]
            keys = rows[0:high, width + lane : width + lane + HD]
            values = rows[0:high, 2 * width + lane : 2 * width + lane + HD]
            scores = jnp.where(allowed, mm(keys, queries * jnp.bfloat16(HD ** (-0.5)), NT), -1e30)
            top = jnp.max(scores, axis=0, keepdims=True)
            exponent = jnp.exp(scores - top)
            total = jnp.sum(exponent, axis=0, keepdims=True)
            weights = (exponent * (1.0 / total)).astype(jnp.bfloat16)
            columns.append(mm(values, weights, TN))
            log_ref[head : head + 1, low:high] = top + jnp.log(total)
        attended = jnp.concatenate(columns, axis=0).T.astype(jnp.bfloat16)
        to_slots(slots_ref, attended, out_ref, low // block_rows, block_rows)


def backward_kernel(
    block_rows, slots_ref, qkv_ref, grad_ref, log_ref, out_ref, rows, grads, key_sum, value_sum
):
    length, wide = rows.shape
    width = wide // 3
    chunk = min(CHUNK, length)
    scale = HD ** (-0.5)
    to_places(slots_ref, qkv_ref, rows, block_rows)
    to_places(slots_ref, grad_ref, grads, block_rows)
    key_sum[...] = jnp.zeros(key_sum.shape, jnp.float32)
    value_sum[...] = jnp.zeros(value_sum.shape, jnp.float32)
    for part in range(length // chunk):
        low, high = part * chunk, (part + 1) * chunk
        allowed = causal(high, chunk)
        query_columns, key_parts, value_parts = [], [], []
        for head in range(width // HD):
            lane = head * HD
            queries = rows[low:high, lane : lane + HD]
            keys = rows[0:high, width + lane : width + lane + HD]
            values = rows[0:high, 2 * width + lane : 2 * width + lane + HD]
            grad_out = grads[low:high, lane : lane + HD]
            scores = jnp.where(allowed, mm(keys, queries * jnp.bfloat16(scale), NT), -1e30)
            probs = jnp.exp(scores - log_ref[head : head + 1, low:high])
            grad_probs = mm(values, grad_out, NT)
            delta = jnp.sum(probs * grad_probs, axis=0, keepdims=True)
            grad_scores = (probs * (grad_probs - delta)).astype(jnp.bfloat16)
            value_parts.append(mm(probs.astype(jnp.bfloat16), grad_out, NN))
            key_parts.append(mm(grad_scores, queries, NN))
            query_columns.append(mm(keys, grad_scores, TN))
        key_sum[0:high, :] += jnp.concatenate(key_parts, axis=1)
        value_sum[0:high, :] += jnp.concatenate(value_parts, axis=1)
        grad_query = (jnp.concatenate(query_columns, axis=0).T * scale).astype(jnp.bfloat16)
        to_slots(
            slots_ref, grad_query, out_ref.at[:, 0:width], low // block_rows, block_rows
        )
    to_slots(
        slots_ref,
        (key_sum[...] * scale).astype(jnp.bfloat16),
        out_ref.at[:, width : 2 * width],
        0,
        block_rows,
    )
    to_slots(
        slots_ref,
        value_sum[...].astype(jnp.bfloat16),
        out_ref.at[:, 2 * width : 3 * width],
        0,
        block_rows,
    )


def whole_shape(shape):
    return pl.BlockSpec(shape, lambda step: (0,) * len(shape))


def whole_block(array):
    return whole_shape(array.shape)


SMEM_SPEC = pl.BlockSpec(memory_space=pltpu.SMEM)
KERNEL_PARAMS = pltpu.CompilerParams(vmem_limit_bytes=60 * 1024 * 1024)


def attend_forward(slots, qkv, block_rows):
    length, wide = qkv.shape
    width = wide // 3
    area = length * length * width
    return pl.pallas_call(
        lambda *refs: forward_kernel(block_rows, *refs),
        out_shape=(
            jax.ShapeDtypeStruct((length, width), jnp.bfloat16),
            jax.ShapeDtypeStruct((8, length), jnp.float32),
        ),
        grid=(1,),
        in_specs=[SMEM_SPEC, whole_block(qkv)],
        out_specs=(whole_shape((length, width)), whole_shape((8, length))),
        scratch_shapes=[pltpu.VMEM((length, wide), jnp.bfloat16)],
        compiler_params=KERNEL_PARAMS,
        cost_estimate=pl.CostEstimate(
            flops=3 * area, bytes_accessed=8 * length * width, transcendentals=area // HD
        ),
        name="attend_forward",
    )(slots, qkv)


def attend_backward(slots, qkv, grad_out, log_total, block_rows):
    length, wide = qkv.shape
    width = wide // 3
    area = length * length * width
    return pl.pallas_call(
        lambda *refs: backward_kernel(block_rows, *refs),
        out_shape=jax.ShapeDtypeStruct((length, wide), jnp.bfloat16),
        grid=(1,),
        in_specs=[SMEM_SPEC, whole_block(qkv), whole_block(grad_out), whole_block(log_total)],
        out_specs=whole_shape((length, wide)),
        scratch_shapes=[
            pltpu.VMEM((length, wide), jnp.bfloat16),
            pltpu.VMEM((length, width), jnp.bfloat16),
            pltpu.VMEM((length, width), jnp.float32),
            pltpu.VMEM((length, width), jnp.float32),
        ],
        compiler_params=KERNEL_PARAMS,
        cost_estimate=pl.CostEstimate(
            flops=7 * area, bytes_accessed=14 * length * width, transcendentals=area // HD
        ),
        name="attend_backward",
    )(slots, qkv, grad_out, log_total)


def swap(values, axis, bit):
    count = lax.axis_size(axis)
    return lax.ppermute(values, axis, [(i, i ^ bit) for i in range(count)])


def together(*groups):
    return lax.optimization_barrier(groups)


def spread_step(held, axis, bit):
    keys = tuple(key for offsets, _ in held for key in offsets)
    arrays = [array for _, array in held]
    sent = arrays[0] if len(arrays) == 1 else jnp.concatenate(arrays, axis=0)
    return (keys, sent), (tuple(key ^ bit for key in keys), swap(sent, axis, bit))


def pack_kernel(pieces, mix_ref, out_weight_ref, *refs):
    vectors, (head_ref, tail_ref) = refs[:-2], refs[-2:]
    half = tail_ref.shape[1]
    parts, _, part_width = mix_ref.shape
    mix_width = parts * part_width
    shard = 2 * half
    for target, first in ((head_ref, 0), (tail_ref, half)):
        for part in range(parts):
            target[0, 0:half, part * part_width : (part + 1) * part_width] = mix_ref[
                part, first : first + half, :
            ]
        for piece in range(pieces):
            target[0, 0:half, mix_width + piece * shard : mix_width + (piece + 1) * shard] = (
                out_weight_ref[piece * shard + first : piece * shard + first + half, :]
            )
    extra = head_ref.shape[1] - half
    head_ref[0, half:, :] = jnp.zeros((extra, head_ref.shape[2]), jnp.bfloat16)
    for number, vector in enumerate(vectors):
        head_ref[0, half : half + 1, number * shard : number * shard + vector.shape[1]] = vector[...]


def late_kernel(up_ref, down_ref, late_ref):
    hidden_local = up_ref.shape[1]
    late_ref[:, 0:hidden_local] = up_ref[...]
    late_ref[:, hidden_local:] = down_ref[...].T


def pack_late(up_shard, down_shard):
    shard, hidden_local = up_shard.shape
    return pl.pallas_call(
        late_kernel,
        out_shape=jax.ShapeDtypeStruct((shard, 2 * hidden_local), jnp.bfloat16),
        grid=(1,),
        in_specs=[whole_block(up_shard), whole_block(down_shard)],
        out_specs=whole_shape((shard, 2 * hidden_local)),
        compiler_params=KERNEL_PARAMS,
        name="pack_late",
    )(up_shard, down_shard)


def pack(mix_shard, out_shard, vectors):
    parts, shard, part_width = mix_shard.shape
    pieces = out_shard.shape[0] // shard
    total = parts * part_width + out_shard.shape[0]
    return pl.pallas_call(
        lambda *refs: pack_kernel(pieces, *refs),
        out_shape=(
            jax.ShapeDtypeStruct((1, shard // 2 + 16, total), jnp.bfloat16),
            jax.ShapeDtypeStruct((1, shard // 2, total), jnp.bfloat16),
        ),
        grid=(1,),
        in_specs=[whole_block(array) for array in (mix_shard, out_shard, *vectors)],
        out_specs=(
            whole_shape((1, shard // 2 + 16, total)),
            whole_shape((1, shard // 2, total)),
        ),
        compiler_params=KERNEL_PARAMS,
        name="pack",
    )(mix_shard, out_shard, *vectors)


def first_kernel(head_keys, tail_keys, sizes, own_ref, *refs):
    groups, width, vector_count, bias_width = sizes
    tp_count = 4
    parts, refs = refs[:tp_count], refs[tp_count:]
    heads, refs = refs[: len(head_keys)], refs[len(head_keys) :]
    tails, refs = refs[: len(tail_keys)], refs[len(tail_keys) :]
    rows_ref, first_ref, weight_ref, out_weight_ref, table_ref, send_ref, gathered = refs
    own_tp, own_ctx = own_ref[0], own_ref[1]
    mix_width = weight_ref.shape[1]
    half = tails[0].shape[1]
    shard = 2 * half

    def put_out(piece, place, owner, first):
        columns = pl.ds(pl.multiple_of(owner * shard, shard), shard)
        for number in range(out_weight_ref.shape[0] // shard):
            low = mix_width + number * shard
            out_weight_ref[number * shard + first : number * shard + first + half, columns] = piece[
                place, 0:half, low : low + shard
            ]

    for keys, piece in zip(head_keys, heads):
        for place, key in enumerate(keys):
            owner = own_ctx ^ key
            rows = pl.ds(pl.multiple_of(owner * shard, shard), half)
            weight_ref[rows, :] = piece[place, 0:half, 0:mix_width]
            put_out(piece, place, owner, 0)
            extra = piece[place, half:, :].astype(jnp.float32)
            gathered[pl.ds(owner, 1), :] = extra[0:1, :]
    for keys, piece in zip(tail_keys, tails):
        for place, key in enumerate(keys):
            owner = own_ctx ^ key
            rows = pl.ds(pl.multiple_of(owner * shard + half, half), half)
            weight_ref[rows, :] = piece[place, :, 0:mix_width]
            put_out(piece, place, owner, half)
    count = gathered.shape[0]
    vectors = gathered[...]
    table_ref[...] = jnp.zeros(table_ref.shape, jnp.float32)
    for number in range(vector_count):
        lanes = slice(number * shard, (number + 1) * shard)
        for owner in range(count):
            table_ref[number : number + 1, owner * shard : (owner + 1) * shard] = vectors[
                owner : owner + 1, lanes
            ]
    bias_parts = []
    for number in range(2):
        low = vector_count * shard + number * bias_width
        bias_parts.append(
            jnp.concatenate(
                [vectors[owner : owner + 1, low : low + bias_width] for owner in range(count)],
                axis=1,
            )
        )
    bias = jnp.concatenate([bias_parts[0], jnp.zeros_like(bias_parts[0]), bias_parts[1]], axis=1)
    piece_count, part_rows, _ = parts[0].shape
    block_rows = tp_count * part_rows
    for key in range(tp_count):
        for piece in range(piece_count):
            row = pl.multiple_of(piece * block_rows + (own_tp ^ key) * part_rows, part_rows)
            rows_ref[pl.ds(row, part_rows), :] = parts[key][piece]
    seq_rows = send_ref.shape[1]
    dim_local = mix_width // 3
    gain, shift = table_ref[0:1, :], table_ref[1:2, :]
    for seq in range(rows_ref.shape[0] // seq_rows):
        rows = slice(seq * seq_rows, (seq + 1) * seq_rows)
        centered, scale = norm_parts(rows_ref[rows, :].astype(jnp.float32))
        normed = (centered * scale * gain + shift).astype(jnp.bfloat16)
        first_ref[rows, :] = normed
    projected_all = (mm(first_ref[...], weight_ref[...], NN) + bias).astype(jnp.bfloat16)
    for seq in range(rows_ref.shape[0] // seq_rows):
        projected = projected_all[seq * seq_rows : (seq + 1) * seq_rows, :]
        for group in range(groups):
            for number in range(3):
                low = number * dim_local + group * width
                send_ref[seq * groups + group, :, number * width : (number + 1) * width] = (
                    projected[:, low : low + width]
                )


def first_part(own, parts, heads, tails, seq_count, groups, vector_count, bias_width):
    piece_count, part_rows, model_width = parts[0].shape
    row_count = piece_count * part_rows * 4
    count = seq_count * groups
    mix_width = 3 * model_width // 4
    head_keys, head_arrays = zip(*heads)
    tail_keys, tail_arrays = zip(*tails)
    seq_rows = row_count // seq_count
    width = mix_width // (3 * groups)
    low = jnp.bfloat16
    shapes = (
        ((row_count, model_width), low),
        ((row_count, model_width), low),
        ((model_width, mix_width), low),
        ((head_arrays[0].shape[2] - mix_width, model_width), low),
        ((8, model_width), jnp.float32),
        ((count, seq_rows, 3 * width), low),
    )
    return pl.pallas_call(
        lambda *refs: first_kernel(
            head_keys, tail_keys, (groups, width, vector_count, bias_width), *refs
        ),
        out_shape=tuple(jax.ShapeDtypeStruct(*shape) for shape in shapes),
        grid=(1,),
        in_specs=[SMEM_SPEC]
        + [whole_block(array) for array in (*parts, *head_arrays, *tail_arrays)],
        out_specs=tuple(whole_shape(shape) for shape, _ in shapes),
        scratch_shapes=[pltpu.VMEM((count, head_arrays[0].shape[2]), jnp.float32)],
        compiler_params=KERNEL_PARAMS,
        cost_estimate=pl.CostEstimate(
            flops=2 * row_count * model_width * mix_width,
            bytes_accessed=8 * 1024 * 1024,
            transcendentals=0,
        ),
        name="first_part",
    )(own, *parts, *head_arrays, *tail_arrays)


def feed_grads_kernel(second_ref, grad_pre_ref, cot_ref, activated_ref, out_ref):
    half = grad_pre_ref.shape[1]
    out_ref[:, 0:half] = mm(second_ref[...], grad_pre_ref[...], TN).astype(jnp.bfloat16)
    out_ref[:, half:] = mm(cot_ref[...], activated_ref[...], TN).astype(jnp.bfloat16)


def feed_grads(second_all, grad_pre, cot_all, activated):
    row_count, model_width = second_all.shape
    hidden_local = grad_pre.shape[1]
    step = min(256, model_width)
    column = pl.BlockSpec((row_count, step), lambda i: (0, i))
    fixed = pl.BlockSpec((row_count, hidden_local), lambda i: (0, 0))
    return pl.pallas_call(
        feed_grads_kernel,
        grid=(model_width // step,),
        out_shape=jax.ShapeDtypeStruct((model_width, 2 * hidden_local), jnp.bfloat16),
        in_specs=[column, fixed, column, fixed],
        out_specs=pl.BlockSpec((step, 2 * hidden_local), lambda i: (i, 0)),
        compiler_params=KERNEL_PARAMS,
        cost_estimate=pl.CostEstimate(
            flops=4 * row_count * model_width * hidden_local,
            bytes_accessed=8 * 1024 * 1024,
            transcendentals=0,
        ),
        name="feed_grads",
    )(second_all, grad_pre, cot_all, activated)


def feed_finish_kernel(sum_ref, up_ref, down_ref):
    half = up_ref.shape[1]
    up_ref[...] = sum_ref[:, 0:half].astype(jnp.float32)
    down_ref[...] = sum_ref[:, half:].astype(jnp.float32).T


def feed_finish(total):
    shard, twice = total.shape
    shapes = ((shard, twice // 2), (twice // 2, shard))
    return pl.pallas_call(
        feed_finish_kernel,
        grid=(1,),
        out_shape=tuple(jax.ShapeDtypeStruct(shape, jnp.float32) for shape in shapes),
        in_specs=[whole_block(total)],
        out_specs=tuple(whole_shape(shape) for shape in shapes),
        compiler_params=KERNEL_PARAMS,
        name="feed_finish",
    )(total)


def mix_finish_kernel(mine_ref, came_ref, out_mine_ref, out_came_ref, mix_ref, out_ref):
    total = mine_ref[...].astype(jnp.float32) + came_ref[...].astype(jnp.float32)
    parts, _, part_width = mix_ref.shape
    for part in range(parts):
        mix_ref[part] = total[:, part * part_width : (part + 1) * part_width]
    out_ref[...] = (out_mine_ref[...].astype(jnp.float32) + out_came_ref[...].astype(jnp.float32)).T


def mix_finish(mine, came, out_mine, out_came):
    shard, dim_local = out_came.shape
    shapes = ((3, shard, dim_local), (dim_local, shard))
    arrays = (mine, came, out_mine, out_came)
    return pl.pallas_call(
        mix_finish_kernel,
        grid=(1,),
        out_shape=tuple(jax.ShapeDtypeStruct(shape, jnp.float32) for shape in shapes),
        in_specs=[whole_block(array) for array in arrays],
        out_specs=tuple(whole_shape(shape) for shape in shapes),
        compiler_params=KERNEL_PARAMS,
        name="mix_finish",
    )(*arrays)


def small_kernel(own_ref, first_ref, hidden_ref, early_ref, out_ref):
    devices, _, shard = out_ref.shape
    tp_count = 4
    own_tp = own_ref[0]
    share = 1.0 / tp_count
    rows = [
        first_ref[0:1, :],
        first_ref[1:2, :],
        hidden_ref[0:1, :] * share,
        hidden_ref[1:2, :] * share,
        hidden_ref[2:3, :] * share,
        early_ref[1:2, :] * share,
    ]
    out_ref[...] = jnp.zeros(out_ref.shape, jnp.float32)
    piece = shard // tp_count
    count = devices // tp_count
    for owner in range(count):
        for place in range(tp_count):
            index = owner * tp_count + place
            for number, row in enumerate(rows):
                out_ref[index, number : number + 1, :] = row[:, owner * shard : (owner + 1) * shard]
            own = jnp.where(own_tp == place, 1.0, 0.0)
            out_ref[index, len(rows) : len(rows) + 1, :] = (
                early_ref[0:1, owner * shard : (owner + 1) * shard] * own
            )
            for number, part in enumerate((0, 2)):
                low = part * count * piece + owner * piece
                out_ref[
                    index, len(rows) + 1 : len(rows) + 2, number * piece : (number + 1) * piece
                ] = first_ref[2:3, low : low + piece] * own


def small_pack(own, first_sums, hidden_sums, early_sums, count):
    shape = (4 * count, 8, first_sums.shape[1] // count)
    arrays = (first_sums, hidden_sums, early_sums)
    return pl.pallas_call(
        small_kernel,
        grid=(1,),
        out_shape=jax.ShapeDtypeStruct(shape, jnp.float32),
        in_specs=[SMEM_SPEC] + [whole_block(array) for array in arrays],
        out_specs=whole_shape(shape),
        compiler_params=KERNEL_PARAMS,
        name="small_pack",
    )(own, *arrays)


def halve(mine, came, bit):
    terms = mine.astype(jnp.float32) + came.astype(jnp.float32)
    terms = terms.reshape((-1, 2) + terms.shape[1:])
    at = jnp.where(lax.axis_index("ctx") & bit != 0, 1, 0)
    mine = lax.dynamic_index_in_dim(terms, at, 1, keepdims=False)
    other = lax.dynamic_index_in_dim(terms, 1 - at, 1, keepdims=False)
    return mine, swap(other.astype(jnp.bfloat16), "ctx", bit)


MLP_ROWS = 256


def branch_kernel(own_ref, attended_ref, weight_ref, mine_ref, other_ref, attended):
    core = own_ref[0] & 1
    count, seq_rows, width = attended_ref.shape
    seqs = mine_ref.shape[0] // seq_rows
    groups = count // (2 * seqs)
    for half, out_ref in ((1, other_ref), (0, mine_ref)):
        for seq in range(seqs):
            for group in range(groups):
                source = ((core ^ half) * seqs + seq) * groups + group
                attended[
                    seq * seq_rows : (seq + 1) * seq_rows, group * width : (group + 1) * width
                ] = attended_ref[source]
        out_ref[...] = mm(attended[...], weight_ref[...], NN).astype(jnp.bfloat16)


def branch_part(own, attended, out_full):
    count, seq_rows, width = attended.shape
    rows = count * seq_rows * width // out_full.shape[0]
    shape = (rows // 2, out_full.shape[1])
    return pl.pallas_call(
        branch_kernel,
        grid=(1,),
        out_shape=(jax.ShapeDtypeStruct(shape, jnp.bfloat16),) * 2,
        in_specs=[SMEM_SPEC, whole_block(attended), whole_block(out_full)],
        out_specs=(whole_shape(shape),) * 2,
        scratch_shapes=[pltpu.VMEM((rows // 2, out_full.shape[0]), jnp.bfloat16)],
        compiler_params=KERNEL_PARAMS,
        name="branch_part",
    )(own, attended, out_full)


def hidden_grad_kernel(
    own_ref,
    sum_ref,
    other_ref,
    cot_ref,
    hidden_ref,
    table_ref,
    weight_ref,
    send_ref,
    branch_ref,
    own_grad_ref,
    sums_ref,
    rows_ref,
):
    own_tp = own_ref[0]
    core = own_tp & 1
    count, seq_rows, width = send_ref.shape
    _, part_rows, model_width = own_grad_ref.shape
    seqs = sum_ref.shape[0] // seq_rows
    groups = count // (2 * seqs)
    block_rows = seq_rows // 2
    gain = table_ref[3:4, :]
    sums = [jnp.zeros((1, model_width), jnp.float32) for _ in range(3)]
    for half, grad_ref in enumerate((sum_ref, other_ref)):
        for chunk in range(seqs):
            seq = (core ^ half) * seqs + chunk
            rows = pl.ds(pl.multiple_of(seq * seq_rows, seq_rows), seq_rows)
            grad = grad_ref[chunk * seq_rows : (chunk + 1) * seq_rows, :].astype(jnp.float32)
            centered, scale = norm_parts(hidden_ref[rows, :])
            normal = centered * scale
            total = cot_ref[rows, :].astype(jnp.float32) + norm_backward(normal, scale, grad, gain)
            low = total.astype(jnp.bfloat16)
            branch_ref[rows, :] = low
            rows_ref[...] = total
            for block in range(2):
                first = pl.multiple_of(block * block_rows + own_tp * part_rows, part_rows)
                own_grad_ref[seq * 2 + block] = rows_ref[pl.ds(first, part_rows), :]
            sums[0] += jnp.sum(total, axis=0, keepdims=True)
            sums[1] += jnp.sum(grad * normal, axis=0, keepdims=True)
            sums[2] += jnp.sum(grad, axis=0, keepdims=True)
    attended = mm(branch_ref[...], weight_ref[...], NT).astype(jnp.bfloat16)
    for index in range(count):
        seq, group = index // groups, index % groups
        send_ref[index] = attended[
            seq * seq_rows : (seq + 1) * seq_rows, group * width : (group + 1) * width
        ]
    sums_ref[...] = jnp.zeros(sums_ref.shape, jnp.float32)
    for number, total in enumerate(sums):
        sums_ref[number : number + 1, :] = total


def hidden_grad_part(own, grad_sum, grad_other, cot_all, hidden, table, out_full, sizes):
    count, seq_rows, width, part_rows = sizes
    row_count, model_width = hidden.shape
    low = jnp.bfloat16
    shapes = (
        ((count, seq_rows, width), low),
        ((row_count, model_width), low),
        ((2 * row_count // seq_rows, part_rows, model_width), jnp.float32),
        ((8, model_width), jnp.float32),
    )
    arrays = (grad_sum, grad_other, cot_all, hidden, table, out_full)
    return pl.pallas_call(
        hidden_grad_kernel,
        grid=(1,),
        out_shape=tuple(jax.ShapeDtypeStruct(*shape) for shape in shapes),
        in_specs=[SMEM_SPEC] + [whole_block(array) for array in arrays],
        out_specs=tuple(whole_shape(shape) for shape, _ in shapes),
        scratch_shapes=[pltpu.VMEM((seq_rows, model_width), jnp.float32)],
        compiler_params=KERNEL_PARAMS,
        name="hidden_grad_part",
    )(own, *arrays)


def place_mixed(source_ref, target, width):
    count, seq_rows, total = source_ref.shape
    parts = total // width
    groups = target.shape[1] // total
    for index in range(count):
        seq, group = index // groups, index % groups
        for part in range(parts):
            low = (part * groups + group) * width
            target[seq * seq_rows : (seq + 1) * seq_rows, low : low + width] = source_ref[
                index, :, part * width : (part + 1) * width
            ]


def halved_grads_kernel(own_ref, left_ref, right_ref, mine_ref, other_ref, *placed):
    if placed:
        place_mixed(right_ref, placed[0], right_ref.shape[2])
        right_ref = placed[0]
    half, shard, _ = mine_ref.shape
    for flipped, out_ref in ((1, other_ref), (0, mine_ref)):
        for index in range(half):
            owner = 2 * index + ((own_ref[1] & 1) ^ flipped)
            columns = pl.ds(pl.multiple_of(owner * shard, shard), shard)
            out_ref[index] = mm(left_ref[:, columns], right_ref[...], TN).astype(jnp.bfloat16)


def halved_grads(own, left, right, count):
    row_count, model_width = left.shape
    width = right.size // row_count
    shape = (count // 2, model_width // count, width)
    placed = [pltpu.VMEM((row_count, width), jnp.bfloat16)] if len(right.shape) == 3 else []
    return pl.pallas_call(
        halved_grads_kernel,
        grid=(1,),
        out_shape=(jax.ShapeDtypeStruct(shape, jnp.bfloat16),) * 2,
        in_specs=[SMEM_SPEC, whole_block(left), whole_block(right)],
        out_specs=(whole_shape(shape),) * 2,
        scratch_shapes=placed,
        compiler_params=KERNEL_PARAMS,
        cost_estimate=pl.CostEstimate(
            flops=2 * model_width * row_count * width,
            bytes_accessed=2 * (left.size + right.size + model_width * width),
            transcendentals=0,
        ),
        name="halved_grads",
    )(own, left, right)


def mix_grads_kernel(keys, own_ref, grad_ref, *refs):
    pieces, (mine_ref, other_ref, normed) = refs[:-3], refs[-3:]
    own_core, own_ctx = own_ref[0] & 1, own_ref[1]
    half, shard, _ = mine_ref.shape
    for (piece_keys, core_key), piece in zip(keys, pieces):
        part_rows = piece.shape[1]
        for place, key in enumerate(piece_keys):
            start = (own_ctx ^ key) * 2 * part_rows + (own_core ^ core_key) * part_rows
            normed[pl.ds(pl.multiple_of(start, part_rows), part_rows), :] = piece[place]
    for flipped, out_ref in enumerate((mine_ref, other_ref)):
        for index in range(half):
            owner = 2 * index + ((own_ctx & 1) ^ flipped)
            columns = pl.ds(pl.multiple_of(owner * shard, shard), shard)
            out_ref[index] = mm(normed[:, columns], grad_ref[...], TN).astype(jnp.bfloat16)


def mix_grads(own, grad_qkv, count, held):
    keys = [(offsets, core_key) for offsets, core_key, _ in held]
    pieces = [piece for _, _, piece in held]
    length, width = grad_qkv.shape
    model_width = pieces[0].shape[2]
    shape = (count // 2, model_width // count, width)
    low = jnp.bfloat16
    arrays = (grad_qkv, *pieces)
    return pl.pallas_call(
        lambda *refs: mix_grads_kernel(keys, *refs),
        grid=(1,),
        out_shape=(jax.ShapeDtypeStruct(shape, low),) * 2,
        in_specs=[SMEM_SPEC] + [whole_block(array) for array in arrays],
        out_specs=(whole_shape(shape),) * 2,
        scratch_shapes=[pltpu.VMEM((length, model_width), low)],
        compiler_params=KERNEL_PARAMS,
        cost_estimate=pl.CostEstimate(
            flops=2 * model_width * length * width,
            bytes_accessed=8 * 1024 * 1024,
            transcendentals=0,
        ),
        name="mix_grads",
    )(own, *arrays)


def mix_join_kernel(own_ref, mine_ref, came_ref, keep_ref, send_ref):
    own_ctx = own_ref[1]
    is_first = (own_ctx & 1) == 0
    own_bit = (own_ctx >> 1) & 1
    width = mine_ref.shape[2] // 3
    for flipped, out_ref in enumerate((keep_ref, send_ref)):
        for index in range(out_ref.shape[0]):
            source = 2 * index + (own_bit ^ flipped)
            mine, came = mine_ref[source], came_ref[source]
            first = jnp.where(is_first, mine, came)
            second = jnp.where(is_first, came, mine)
            for part in range(3):
                lanes = slice(part * width, (part + 1) * width)
                low = 2 * part * width
                out_ref[index, :, low : low + width] = first[:, lanes]
                out_ref[index, :, low + width : low + 2 * width] = second[:, lanes]


def mix_join(own, mine, came):
    half, shard, total = mine.shape
    shape = (half // 2, shard, 2 * total)
    return pl.pallas_call(
        mix_join_kernel,
        grid=(1,),
        out_shape=(jax.ShapeDtypeStruct(shape, jnp.bfloat16),) * 2,
        in_specs=[SMEM_SPEC, whole_block(mine), whole_block(came)],
        out_specs=(whole_shape(shape),) * 2,
        compiler_params=KERNEL_PARAMS,
        name="mix_join",
    )(own, mine, came)


def first_grad_kernel(own_ref, mixed_ref, weight_ref, x_ref, mine_ref, other_ref, sums_ref, *refs):
    mixed, rows_ref = refs
    own_tp = own_ref[0]
    core = own_tp & 1
    count, seq_rows, total = mixed_ref.shape
    groups = mixed.shape[1] // total
    place_mixed(mixed_ref, mixed, total // 3)
    part_rows = mine_ref.shape[2]
    model_width = x_ref.shape[1]
    block_rows = seq_rows // 2
    sums = [jnp.zeros((1, model_width), jnp.float32) for _ in range(2)]
    partial_all = mm(mixed[...], weight_ref[...], NT)
    for seq in range(count // groups):
        rows = slice(seq * seq_rows, (seq + 1) * seq_rows)
        partial = partial_all[rows, :]
        rows_ref[...] = partial.astype(jnp.bfloat16)
        for block in range(2):
            for row in range(2):
                for flipped, out_ref in enumerate((mine_ref, other_ref)):
                    owner = 2 * row + (core ^ flipped)
                    first = pl.multiple_of(block * block_rows + owner * part_rows, part_rows)
                    out_ref[2 * seq + block, row] = rows_ref[pl.ds(first, part_rows), :]
        centered, scale = norm_parts(x_ref[rows, :].astype(jnp.float32))
        sums[0] += jnp.sum(partial * (centered * scale), axis=0, keepdims=True)
        sums[1] += jnp.sum(partial, axis=0, keepdims=True)
    sums_ref[...] = jnp.zeros(sums_ref.shape, jnp.float32)
    for number, value in enumerate(sums):
        sums_ref[number : number + 1, :] = value
    mixed_ref_sum = jnp.sum(mixed[...].astype(jnp.float32), axis=0, keepdims=True)
    sums_ref[2:3, 0 : mixed.shape[1]] = mixed_ref_sum


def first_grads(own, grad_mixed, mix_full, x_all, part_rows):
    count, seq_rows, total = grad_mixed.shape
    row_count, model_width = x_all.shape
    shape = (2 * row_count // seq_rows, 2, part_rows, model_width)
    low = jnp.bfloat16
    arrays = (grad_mixed, mix_full, x_all)
    return pl.pallas_call(
        first_grad_kernel,
        grid=(1,),
        out_shape=(
            jax.ShapeDtypeStruct(shape, low),
            jax.ShapeDtypeStruct(shape, low),
            jax.ShapeDtypeStruct((8, model_width), jnp.float32),
        ),
        in_specs=[SMEM_SPEC] + [whole_block(array) for array in arrays],
        out_specs=(whole_shape(shape), whole_shape(shape), whole_shape((8, model_width))),
        scratch_shapes=[
            pltpu.VMEM((row_count, mix_full.shape[1]), low),
            pltpu.VMEM((seq_rows, model_width), low),
        ],
        compiler_params=KERNEL_PARAMS,
        name="first_grads",
    )(own, *arrays)


def gelu_both(value):
    root = (2.0 / jnp.pi) ** 0.5
    square = value * value
    inner = jnp.tanh(root * value * (1.0 + 0.044715 * square))
    slope = 0.5 * (1.0 + inner) + 0.5 * value * (1.0 - inner * inner) * root * (
        1.0 + 3.0 * 0.044715 * square
    )
    return 0.5 * value * (1.0 + inner), slope


def feed_kernel(part_count, own_ref, sum_ref, other_ref, x_ref, table_ref, late_ref, *refs):
    cot_parts, refs = refs[:part_count], refs[part_count:]
    (
        hidden_ref,
        second_ref,
        activated_ref,
        grad_pre_ref,
        mine_ref,
        partner_ref,
        cot_ref,
        sums_ref,
    ) = refs
    own_tp = own_ref[0]
    core = own_tp & 1
    hidden_local = activated_ref.shape[1]
    blocks, part_rows, _ = cot_parts[0].shape
    for key, part in enumerate(cot_parts):
        for block in range(blocks):
            row = block * part_count * part_rows + (own_tp ^ key) * part_rows
            cot_ref[pl.ds(pl.multiple_of(row, part_rows), part_rows), :] = part[block]
    half_rows = sum_ref.shape[0]
    up_sum = jnp.zeros((1, hidden_local), jnp.float32)
    cot_sum = jnp.zeros((1, cot_ref.shape[1]), jnp.float32)
    for half, (branch_ref, out_ref) in enumerate(((sum_ref, mine_ref), (other_ref, partner_ref))):
        for chunk in range(half_rows // MLP_ROWS):
            inside = slice(chunk * MLP_ROWS, (chunk + 1) * MLP_ROWS)
            start = (core ^ half) * half_rows + chunk * MLP_ROWS
            rows = pl.ds(pl.multiple_of(start, MLP_ROWS), MLP_ROWS)
            hidden = (
                x_ref[rows, :].astype(jnp.float32)
                + branch_ref[inside, :].astype(jnp.float32)
                + table_ref[2:3, :]
            )
            hidden_ref[rows, :] = hidden
            centered, scale = norm_parts(hidden)
            second = (centered * scale * table_ref[3:4, :] + table_ref[4:5, :]).astype(jnp.bfloat16)
            second_ref[rows, :] = second
            activated, slope = gelu_both(mm(second, late_ref[:, 0:hidden_local], NN) + table_ref[6:7, :])
            activated_ref[rows, :] = activated.astype(jnp.bfloat16)
            cot = cot_ref[rows, :]
            grad_pre = (mm(cot, late_ref[:, hidden_local:], NN) * slope).astype(jnp.bfloat16)
            grad_pre_ref[rows, :] = grad_pre
            out_ref[inside, :] = mm(grad_pre, late_ref[:, 0:hidden_local], NT).astype(jnp.bfloat16)
            up_sum += jnp.sum(grad_pre.astype(jnp.float32), axis=0, keepdims=True)
            cot_sum += jnp.sum(cot.astype(jnp.float32), axis=0, keepdims=True)
    sums_ref[...] = jnp.zeros(sums_ref.shape, jnp.float32)
    sums_ref[0:1, 0:hidden_local] = up_sum
    sums_ref[1:2, 0 : cot_ref.shape[1]] = cot_sum


def feed_part(own, branch_sum, branch_other, x_all, table, late_all, cot_parts):
    row_count, model_width = x_all.shape
    hidden_local = late_all.shape[1] // 2
    low = jnp.bfloat16
    shapes = (
        ((row_count, model_width), jnp.float32),
        ((row_count, model_width), low),
        ((row_count, hidden_local), low),
        ((row_count, hidden_local), low),
        ((row_count // 2, model_width), low),
        ((row_count // 2, model_width), low),
        ((row_count, model_width), low),
        ((8, max(model_width, hidden_local)), jnp.float32),
    )
    arrays = (branch_sum, branch_other, x_all, table, late_all, *cot_parts)
    return pl.pallas_call(
        lambda *refs: feed_kernel(len(cot_parts), *refs),
        grid=(1,),
        out_shape=tuple(jax.ShapeDtypeStruct(*shape) for shape in shapes),
        in_specs=[SMEM_SPEC] + [whole_block(array) for array in arrays],
        out_specs=tuple(whole_shape(shape) for shape, _ in shapes),
        compiler_params=KERNEL_PARAMS,
        cost_estimate=pl.CostEstimate(
            flops=6 * row_count * model_width * hidden_local,
            bytes_accessed=16 * 1024 * 1024,
            transcendentals=row_count * hidden_local,
        ),
        name="feed_part",
    )(own, *arrays)


def spread_tp(part):
    return [part] + [swap(part, "tp", key) for key in (1, 2, 3)]


def add_halves(mine, other, beside=None):
    arrived = swap(other, "tp", 1)
    chip_sum = (mine.astype(jnp.float32) + arrived.astype(jnp.float32)).astype(jnp.bfloat16)
    arrived = swap(chip_sum, "tp", 2)
    if beside is not None:
        arrived, beside = together(arrived, beside)
    whole = (chip_sum.astype(jnp.float32) + arrived.astype(jnp.float32)).astype(jnp.bfloat16)
    return whole, swap(whole, "tp", 1), beside


def owner_first(partial, part_rows):
    core = lax.axis_index("tp") & 1
    parts = partial.astype(jnp.bfloat16).reshape(-1, 2, 2, part_rows, partial.shape[-1])
    mine = lax.dynamic_index_in_dim(parts, core, 2, keepdims=False)
    return mine, swap(lax.dynamic_index_in_dim(parts, 1 - core, 2, keepdims=False), "tp", 1)


def owner_second(mine, arrived):
    row = lax.axis_index("tp") >> 1
    chip_sum = mine.astype(jnp.float32) + arrived.astype(jnp.float32)
    mine = lax.dynamic_index_in_dim(chip_sum, row, 1, keepdims=False)
    other = lax.dynamic_index_in_dim(chip_sum, 1 - row, 1, keepdims=False)
    return mine, swap(other.astype(jnp.bfloat16), "tp", 2)


def add_rows_to_owner(partial, part_rows):
    mine, arrived = owner_second(*owner_first(partial, part_rows))
    return mine + arrived.astype(jnp.float32)


def exchange(pieces):
    return lax.all_to_all(pieces, "ctx", 0, 0, tiled=True)


def norm_parts(rows):
    row_mean = jnp.mean(rows, axis=-1, keepdims=True)
    centered = rows - row_mean
    variance = jnp.mean(centered * centered, axis=-1, keepdims=True)
    return centered, lax.rsqrt(variance + epsilon)


def norm_backward(normal, scale, gradient, gain):
    scaled = gradient * gain
    return scale * (
        scaled
        - jnp.mean(scaled, axis=-1, keepdims=True)
        - normal * jnp.mean(scaled * normal, axis=-1, keepdims=True)
    )


def fast_body(
    inputs,
    pairing,
    first_gain,
    first_shift,
    query_key_value_weight,
    mix_bias,
    output_projection_weight,
    out_bias,
    second_gain,
    second_shift,
    up_projection_weight,
    up_projection_bias,
    down_projection_weight,
    down_bias,
    cotangent,
):
    low = jnp.bfloat16
    wide = jnp.float32
    seq_count, _, _, part_rows, model_width = inputs.shape
    tp_count = lax.axis_size("tp")
    ctx_count = lax.axis_size("ctx")
    block_rows = part_rows * tp_count
    seq_rows = 2 * block_rows
    row_count = seq_count * seq_rows
    shard = model_width // ctx_count
    dim_local = query_key_value_weight.shape[2]
    hidden_local = up_projection_weight.shape[1]
    groups = ctx_count // seq_count
    width = dim_local // groups
    own_tp = lax.axis_index("tp")

    vectors = [
        first_gain[None],
        first_shift[None],
        out_bias[None],
        second_gain[None],
        second_shift[None],
        down_bias[None],
        up_projection_bias,
        jnp.concatenate([mix_bias[0], mix_bias[1]], axis=1),
    ]
    head, tail = pack(
        jnp.transpose(query_key_value_weight, (1, 0, 2)), output_projection_weight, vectors
    )
    bits = [1 << place for place in range(ctx_count.bit_length() - 1)]
    head_bits, tail_bits = bits[::-1], bits[:1] + bits[:0:-1]
    heads, tails = [((0,), head)], [((0,), tail)]
    row_parts = spread_tp(inputs.reshape(-1, part_rows, model_width))
    cot_part = cotangent.reshape(-1, part_rows, model_width)
    late_shard = pack_late(up_projection_weight, down_projection_weight)
    for step, (head_bit, tail_bit) in enumerate(zip(head_bits, tail_bits)):
        heads = list(spread_step(heads, "ctx", head_bit))
        tails = list(spread_step(tails, "ctx", tail_bit))
        arrivals = (heads[1][1], tails[1][1])
        if step == 0:
            arrivals, row_parts, cot_part = together(arrivals, row_parts, cot_part)
            cot_parts = spread_tp(cot_part)
        elif step == 1:
            arrivals, cot_parts = together(arrivals, cot_parts)
        else:
            arrivals, late_shard = together(arrivals, late_shard)
        heads[1], tails[1] = (heads[1][0], arrivals[0]), (tails[1][0], arrivals[1])
    late_all = lax.all_gather(late_shard, "ctx", axis=0, tiled=True)
    own = jnp.stack([own_tp, lax.axis_index("ctx")]).astype(jnp.int32)
    row_all, first_all, mix_full, out_full, table, projected = first_part(
        own, row_parts, heads, tails, seq_count, groups, 7, mix_bias.shape[2]
    )
    gain_one, bias_down = table[0], table[5]

    sequence = lax.axis_index("ctx") // groups
    pairs = lax.dynamic_index_in_dim(pairing, sequence, 0, keepdims=False)
    blocks = jnp.stack([pairs, 2 * ctx_count - 1 - pairs], axis=-1).reshape(-1)
    places = jnp.arange(2 * ctx_count, dtype=jnp.int32)
    slots = jnp.sum(
        jnp.where(blocks[None, :] == places[:, None], places[None, :], 0), axis=1
    ).astype(jnp.int32)
    qkv = exchange(projected).reshape(ctx_count * seq_rows, 3 * width)
    attended_heads, log_total = attend_forward(slots, qkv, block_rows)
    attended = exchange(attended_heads.reshape(ctx_count, seq_rows, width))
    attended, normed_seqs = together(attended, first_all.reshape(seq_count, 2, block_rows, -1))
    normed_seqs = lax.dynamic_index_in_dim(normed_seqs, own_tp & 1, 1, keepdims=False)
    held = []
    for key in range(0, ctx_count, groups):
        their_seq = (lax.axis_index("ctx") ^ key) // groups
        piece = lax.dynamic_index_in_dim(normed_seqs, their_seq, 0)
        held.append(((key,), swap(piece, "ctx", key) if key else piece))
    branch_sum, branch_other, _ = add_halves(*branch_part(own, attended, out_full))
    hidden, second_all, activated, grad_pre, mine, other, cot_all, early_sums = feed_part(
        own, branch_sum, branch_other, row_all, table, late_all, cot_parts
    )

    grad_pre, *pieces = together(grad_pre, *(piece for _, piece in held))
    held = [(keys, piece) for (keys, _), piece in zip(held, pieces)]
    feed_terms = feed_grads(second_all, grad_pre, cot_all, activated)
    feed_total = lax.psum_scatter(feed_terms, "ctx", scatter_dimension=0, tiled=True)
    held = list(spread_step(held, "ctx", 1))
    grad_sum, grad_other, last_piece = add_halves(mine, other, held[1][1])
    held[1] = (held[1][0], last_piece)
    offsets = held[0][0] + held[1][0]
    sent = jnp.concatenate([held[0][1], held[1][1]], axis=0)
    held = [(offsets, 0, sent), (offsets, 1, swap(sent, "tp", 1))]
    grad_attended, grad_branch, own_grad, hidden_sums = hidden_grad_part(
        own,
        grad_sum,
        grad_other,
        cot_all,
        hidden,
        table,
        out_full,
        (ctx_count, seq_rows, width, part_rows),
    )
    grad_attended, last_piece = together(grad_attended, held[1][2])
    held[1] = (offsets, 1, last_piece)
    out_mine, out_other = halved_grads(own, grad_branch, attended, ctx_count)
    out_came = swap(out_other, "ctx", 1)
    grad_heads = exchange(grad_attended).reshape(ctx_count * seq_rows, width)
    grad_qkv = attend_backward(slots, qkv, grad_heads, log_total, block_rows)
    grad_qkv, out_came = together(grad_qkv, out_came)
    mix_mine, mix_other = mix_grads(own, grad_qkv, ctx_count, held)
    mix_other, out_came = together(mix_other, out_came)
    out_mine, out_came = halve(out_mine, out_came, 2)
    down_sum = add_rows_to_owner(mm(activated, late_all[:, hidden_local:], NT), part_rows)
    own_hidden = lax.dynamic_index_in_dim(
        hidden.reshape(-1, tp_count, part_rows, model_width), own_tp, 1, keepdims=False
    )
    result = (own_hidden + down_sum + bias_down).astype(low)

    grad_mixed, mix_mine, mix_came, out_came, result = together(
        exchange(grad_qkv.reshape(ctx_count, seq_rows, 3 * width)),
        mix_mine,
        swap(mix_other, "ctx", 1),
        out_came,
        result,
    )
    mix_mine, mix_other = mix_join(own, mix_mine, mix_came)
    mix_came = swap(mix_other, "ctx", 2)
    grad_mixed, mix_mine = together(grad_mixed, mix_mine)
    for bit in bits[2:]:
        out_mine, out_came = halve(out_mine, out_came, bit)
    mine, other, first_sums = first_grads(own, grad_mixed, mix_full, row_all, part_rows)
    small_terms = small_pack(own, first_sums, hidden_sums, early_sums, ctx_count)
    other, small_terms = together(other, small_terms)
    small = lax.all_to_all(small_terms, ("ctx", "tp"), 0, 0, tiled=True)
    mine, came = owner_second(mine, swap(other, "tp", 1))
    mix_came, came, out_came = together(mix_came, came, out_came)
    for bit in bits[2:]:
        mix_mine, mix_came = halve(mix_mine, mix_came, bit)
    up_shard, down_shard = feed_finish(feed_total)
    grad_first = mine + came.astype(wide)
    own_rows = inputs.reshape(-1, part_rows, model_width).astype(wide)
    own_centered, own_scale = norm_parts(own_rows)
    grad_inputs = own_grad + norm_backward(
        own_centered * own_scale, own_scale, grad_first, gain_one
    )
    mix_came, grad_inputs, small, up_shard, down_shard = together(
        mix_came, grad_inputs, small, up_shard, down_shard
    )
    mix_shard_sum, out_shard_sum = mix_finish(mix_mine[0], mix_came[0], out_mine[0], out_came[0])
    sums = jnp.sum(small, axis=0)
    piece = dim_local // ctx_count
    return (
        result.reshape(inputs.shape),
        grad_inputs.reshape(inputs.shape),
        sums[0],
        sums[1],
        jnp.transpose(mix_shard_sum, (1, 0, 2)),
        jnp.stack([sums[7, :piece], sums[7, piece : 2 * piece]])[:, None, :],
        out_shard_sum,
        sums[2],
        sums[3],
        sums[4],
        up_shard,
        sums[6][None, :],
        down_shard,
        sums[5],
    )


def fits_exchange(inputs, query_key_value_weight, up_projection_weight):
    ctx_count, tp_count = lax.axis_size("ctx"), lax.axis_size("tp")
    seq_count = inputs.shape[0]
    if tp_count != 4 or ctx_count % seq_count or ctx_count & (ctx_count - 1):
        return False
    dim_local = query_key_value_weight.shape[2]
    groups = ctx_count // seq_count
    length = ctx_count * 2 * tp_count * inputs.shape[3]
    shard = inputs.shape[4] // ctx_count
    if groups != 2 or seq_count < 2 or dim_local * 4 != inputs.shape[4]:
        return False
    if up_projection_weight.shape[1] != inputs.shape[4]:
        return False
    return dim_local % (groups * LANES) == 0 and length <= 2048 and shard % LANES == 0


def body(inputs, pairing, first_gain, first_shift, query_key_value_weight, *others):
    fits = fits_exchange(inputs, query_key_value_weight, others[5])
    chosen = fast_body if fits else general_body
    return chosen(inputs, pairing, first_gain, first_shift, query_key_value_weight, *others)


def solution(mesh):
    return jax.shard_map(
        body,
        mesh=mesh,
        in_specs=(
            P(None, "ctx", None, "tp", None),
            P(),
            P("ctx"),
            P("ctx"),
            P("ctx", None, "tp"),
            P(None, "tp", "ctx"),
            P("tp", "ctx"),
            P("ctx"),
            P("ctx"),
            P("ctx"),
            P("ctx", "tp"),
            P("tp", "ctx"),
            P("tp", "ctx"),
            P("ctx"),
            P(None, "ctx", None, "tp", None),
        ),
        out_specs=(
            P(None, "ctx", None, "tp", None),
            P(None, "ctx", None, "tp", None),
            P("ctx"),
            P("ctx"),
            P("ctx", None, "tp"),
            P(None, "tp", "ctx"),
            P("tp", "ctx"),
            P("ctx"),
            P("ctx"),
            P("ctx"),
            P("ctx", "tp"),
            P("tp", "ctx"),
            P("tp", "ctx"),
            P("ctx"),
        ),
        check_vma=False,
    )
```
